32 devices in a mesh: tm: 8 (over z, y), space: 4 (over x, core).
Axes of the slice: x: 2, y: 2, z: 4, core: 2. Of those that a mesh axis runs over, the one named last changes fastest.
Arguments:
- iterate: float32 [2, 16, 32, 4096], P(None, 'tm', 'space'), may hold values from -6 to 6
- forcing: float32 [2, 16, 32, 4096], P(None, 'tm', 'space'), may hold values from -6 to 6
Outputs:
- smoothed: float32 [2, 16, 32, 4096], P(None, 'tm', 'space')
- coarse: float32 [2, 16, 32, 4096], P(None, 'tm', 'space')
The draws below stay inside these ranges and needn't reach their ends.
All inputs are finite; a program needn't handle non-finite values.
Results may differ from the reference program's by a relative error of at most 0.00002.
Values sent between devices are 32-bit elements; how exact they have to be, the bound alone decides.
No kernel may reach another device: no remote copies, remote signals or barrier semaphores. Data moves between devices by JAX's collectives and lax.ppermute only.
A program may use at most 320 MiB of HBM per device.

```python
import jax
import jax.numpy as jnp

NX = 64
NY = 64
NZ = 32
STEPS = 16
LEVELS = 5


def draw_forcing(key, part):
    key = jax.random.fold_in(key, 7)
    extent = (2, STEPS, NZ, NX * NY)
    return jnp.clip(jax.random.normal(key, extent, jnp.float32), -5.0, 5.0)


def steps_of(rng, dims, pieces, least, high):
    gain = 1.0
    for dim, parts in pieces:
        steps = jax.random.uniform(jax.random.fold_in(jax.random.fold_in(rng, 6), dim), (parts,), jnp.float32, least / len(pieces), high / len(pieces))
        gain = gain * jnp.repeat(jnp.exp(steps), dims[dim] // parts).reshape((-1,) + (1,) * (len(dims) - 1 - dim))
    return gain


def bell_draw(key, shape, spread, most, cuts=(), kind=jnp.bfloat16):
    level = steps_of(key, shape, cuts, -0.22, 0.18) if cuts else 1.0
    drawn = jax.random.normal(key, shape, jnp.float32) * spread * level
    return jnp.minimum(jnp.maximum(drawn, -most), most).astype(kind)


def setup_inputs(seed: int = 0) -> dict:
    splits = jax.random.split(jax.random.key(seed), 3)
    return {
        "iterate": bell_draw(splits[0], (2, STEPS, NZ, NX * NY), 1.0, 6.0, ((1, 8), (2, 4)), jnp.float32),
        "forcing": draw_forcing(jax.random.fold_in(splits[2], 71), 0),
    }


KAPPA_BASE = 0.25
COUPLING_BASE = 0.5
DAMPING = 0.6


def neighbour_plane(values, row_cells):
    length = values.shape[-1]
    columns = jnp.arange(length, dtype=jnp.int32) % row_cells
    single = jnp.zeros(values.shape[:-1] + (1,), jnp.float32)
    row_zero = jnp.zeros(values.shape[:-1] + (row_cells,), jnp.float32)
    left_side = jnp.where(columns != 0, jnp.concatenate([single, values[..., :-1]], -1), 0.0)
    right_side = jnp.where(columns != row_cells - 1, jnp.concatenate([values[..., 1:], single], -1), 0.0)
    upper_side = jnp.concatenate([row_zero, values[..., :-row_cells]], -1)
    lower_side = jnp.concatenate([values[..., row_cells:], row_zero], -1)
    return left_side + right_side + upper_side + lower_side


def operate(fields, extended, prev_state, next_adjoint, diffusion, coupling):
    neighbours = extended[:, :, 2:] + extended[:, :, :-2] + neighbour_plane(fields, NY)
    centre = 1.0 + 6.0 * diffusion
    state = fields[0]
    adjoint = fields[1]
    state_before = jnp.concatenate([prev_state, state[:-1]], 0)
    adjoint_after = jnp.concatenate([adjoint[1:], next_adjoint], 0)
    image_state = centre * state - diffusion * neighbours[0] - state_before + coupling * adjoint
    image_adjoint = centre * adjoint - diffusion * neighbours[1] - adjoint_after - coupling * state
    return jnp.stack([image_state, image_adjoint])


def relax(fields, defect, diffusion, coupling):
    centre = 1.0 + 6.0 * diffusion
    determinant = centre * centre + coupling * coupling
    along = DAMPING * centre / determinant
    across = DAMPING * coupling / determinant
    update = jnp.stack([along * defect[0] - across * defect[1], across * defect[0] + along * defect[1]])
    return fields + update


def full_operator(fields, diffusion, coupling):
    extended = jnp.pad(fields, ((0, 0), (0, 0), (1, 1), (0, 0)))
    blank_plane = jnp.zeros((1,) + fields.shape[2:], jnp.float32)
    return operate(fields, extended, blank_plane, blank_plane, diffusion, coupling)


def reference(iterate, forcing):
    fields = iterate
    source = forcing
    smoothed = iterate
    for level_index in range(LEVELS):
        diffusion = KAPPA_BASE * 2.0 ** level_index
        coupling = COUPLING_BASE * 2.0 ** level_index
        for sweep_index in range(2):
            if level_index > 0 and sweep_index == 0:
                defect = source
            else:
                defect = source - full_operator(fields, diffusion, coupling)
            fields = relax(fields, defect, diffusion, coupling)
        if level_index == 0:
            smoothed = fields
        if level_index < LEVELS - 1:
            defect = source - full_operator(fields, diffusion, coupling)
            count_now = defect.shape[1]
            paired = defect.reshape(2, count_now // 2, 2, defect.shape[2], defect.shape[3])
            source = paired[:, :, 0] + paired[:, :, 1]
            fields = jnp.zeros_like(source)
    coarse = jnp.broadcast_to(fields[:, :1], iterate.shape)
    return smoothed, coarse
```

```python
import numpy as np

import jax
import jax.numpy as jnp
from jax import lax
from jax.sharding import PartitionSpec as P

NY = 64

KAPPA_BASE = 0.25
COUPLING_BASE = 0.5
DAMPING = 0.6


def level_terms(level):
    diffusion = KAPPA_BASE * 2.0**level
    coupling = COUPLING_BASE * 2.0**level
    centre = 1.0 + 6.0 * diffusion
    determinant = centre * centre + coupling * coupling
    along = DAMPING * centre / determinant
    across = DAMPING * coupling / determinant
    return diffusion, coupling, centre, along, across


def coarse_polynomials(total_steps):
    levels = total_steps.bit_length()
    powers = 2 * levels + 1
    unit = np.eye(4 * total_steps).reshape(-1, 2, 2, total_steps)
    fields = np.zeros((4 * total_steps, 2, total_steps, powers))
    source = np.zeros_like(fields)
    fields[..., 0] = unit[:, 0]
    source[..., 0] = unit[:, 1]

    def image(values, diffusion, coupling, centre):
        out = centre * values
        out[..., 1:] -= diffusion * values[..., :-1]
        out[:, 0, 1:] -= values[:, 0, :-1]
        out[:, 1, :-1] -= values[:, 1, 1:]
        out[:, 0] += coupling * values[:, 1]
        out[:, 1] -= coupling * values[:, 0]
        return out

    for level in range(levels):
        diffusion, coupling, centre, along, across = level_terms(level)
        for _ in range(2):
            defect = source - image(fields, diffusion, coupling, centre)
            state, adjoint = defect[:, 0], defect[:, 1]
            fields = fields + np.stack([along * state - across * adjoint, across * state + along * adjoint], 1)
        if level < levels - 1:
            defect = source - image(fields, diffusion, coupling, centre)
            source = defect[:, :, 0::2] + defect[:, :, 1::2]
            fields = np.zeros_like(source)
    return fields[:, :, 0].reshape(2, 2, total_steps, 2, powers)


def plane_neighbours(values):
    length = values.shape[-1]
    columns = jnp.arange(length, dtype=jnp.int32) % NY
    single = jnp.zeros(values.shape[:-1] + (1,), jnp.float32)
    row = jnp.zeros(values.shape[:-1] + (NY,), jnp.float32)
    left = jnp.where(columns != 0, jnp.concatenate([single, values[..., :-1]], -1), 0.0)
    right = jnp.where(columns != NY - 1, jnp.concatenate([values[..., 1:], single], -1), 0.0)
    upper = jnp.concatenate([row, values[..., :-NY]], -1)
    lower = jnp.concatenate([values[..., NY:], row], -1)
    return left + right + upper + lower


def whole_neighbours(values):
    zero = jnp.zeros(values.shape[:-2] + (1, values.shape[-1]), jnp.float32)
    above = jnp.concatenate([zero, values[..., :-1, :]], -2)
    below = jnp.concatenate([values[..., 1:, :], zero], -2)
    return above + below + plane_neighbours(values)


def inner_neighbours(values):
    return values[..., :-2, :] + values[..., 2:, :] + plane_neighbours(values[..., 1:-1, :])


def shifted(value, axis, by):
    size = lax.axis_size(axis)
    return lax.ppermute(value, axis, [(i, i + by) for i in range(size) if 0 <= i + by < size])


def coarse_part(iterate, forcing):
    steps = iterate.shape[1]
    depth, cells = iterate.shape[2:]
    ranks, slabs = lax.axis_size("tm"), lax.axis_size("space")
    table = coarse_polynomials(steps * ranks)
    powers = table.shape[-1]
    table = table.reshape(2, 2, ranks, steps, 2, powers).transpose(2, 5, 4, 0, 1, 3).astype(np.float32)
    weights = jnp.asarray(table)[lax.axis_index("tm")]
    both = jnp.stack([iterate, forcing])
    offset = lax.axis_index("space") * depth
    total = jnp.zeros((2, depth * slabs, cells), jnp.float32)
    for power in reversed(range(powers)):
        share = jnp.sum(weights[power][..., None, None] * both[None], axis=(1, 2, 3))
        blank = jnp.zeros((2, depth * slabs, cells), jnp.float32)
        placed = lax.dynamic_update_slice(blank, share, (0, offset, 0))
        total = placed if power == powers - 1 else placed + whole_neighbours(total)
    return total


def smooth(iterate, forcing):
    depth = iterate.shape[2]
    rank, ranks = lax.axis_index("tm"), lax.axis_size("tm")
    slab, slabs = lax.axis_index("space"), lax.axis_size("space")
    diffusion, coupling, centre, along, across = level_terms(0)
    send_up = jnp.concatenate([iterate[:, :, -2:], forcing[:, :, -1:]], 2)
    send_down = jnp.concatenate([forcing[:, :, :1], iterate[:, :, :2]], 2)
    from_above = shifted(send_up, "space", 1)
    from_below = shifted(send_down, "space", -1)
    wide = jnp.concatenate([from_above[:, :, :2], iterate, from_below[:, :, 1:]], 2)
    source = jnp.concatenate([from_above[:, :, 2:], forcing, from_below[:, :, :1]], 2)

    def relaxed(fields, image_state, image_adjoint, source):
        defect_state = source[0] - image_state
        defect_adjoint = source[1] - image_adjoint
        return jnp.stack([
            fields[0] + along * defect_state - across * defect_adjoint,
            fields[1] + across * defect_state + along * defect_adjoint,
        ])

    def images(fields, around, before, after):
        state, adjoint = fields
        return (
            centre * state - diffusion * around[0] - before + coupling * adjoint,
            centre * adjoint - diffusion * around[1] - after - coupling * state,
        )

    middle = wide[:, :, 1:-1]
    none = jnp.zeros_like(middle[0, :1])
    before = jnp.concatenate([none, middle[0, :-1]], 0)
    after = jnp.concatenate([middle[1, 1:], none], 0)
    first = relaxed(middle, *images(middle, inner_neighbours(wide), before, after), source)
    plane = jnp.arange(depth + 2)
    inside = ((plane > 0) | (slab > 0)) & ((plane < depth + 1) | (slab < slabs - 1))
    first = jnp.where(inside[:, None], first, 0.0)
    forth = jnp.concatenate([middle[0, -1], first[0, -1, 1:-1]], 0)
    back = jnp.concatenate([middle[1, 0], first[1, 0, 1:-1]], 0)
    forth = shifted(forth, "tm", 1)
    back = shifted(back, "tm", -1)
    state_before, adjoint_after = forth[: depth + 2], back[: depth + 2]
    start = first[:, :1] + jnp.stack([along * state_before, across * state_before])[:, None]
    first = jnp.concatenate([start, first[:, 1:]], 1)
    end = first[:, -1:] + jnp.stack([-across * adjoint_after, along * adjoint_after])[:, None]
    first = jnp.concatenate([first[:, :-1], end], 1)
    before = jnp.where(rank > 0, forth[depth + 2 :] - across * iterate[1, 0], 0.0)
    after = jnp.where(rank < ranks - 1, back[depth + 2 :] + across * iterate[0, -1], 0.0)
    middle = first[:, :, 1:-1]
    before = jnp.concatenate([before[None], middle[0, :-1]], 0)
    after = jnp.concatenate([middle[1, 1:], after[None]], 0)
    return relaxed(middle, *images(middle, inner_neighbours(first), before, after), forcing)


def local(iterate, forcing):
    share = coarse_part(iterate, forcing)
    slab = lax.psum_scatter(share, "space", scatter_dimension=1, tiled=True)
    coarse = lax.psum(slab, "tm")
    smoothed = smooth(iterate, forcing)
    return smoothed, jnp.broadcast_to(coarse[:, None], iterate.shape)


def solution(mesh):
    specs = P(None, "tm", "space", None)
    return jax.shard_map(local, mesh=mesh, in_specs=(specs, specs), out_specs=(specs, specs), check_vma=False)
```

```python
import functools

import numpy as np

import jax
import jax.numpy as jnp
from jax import lax
from jax.experimental import pallas as pl
from jax.experimental.pallas import tpu as pltpu
from jax.sharding import PartitionSpec as P

NY = 64
LANES = 128

KAPPA_BASE = 0.25
COUPLING_BASE = 0.5
DAMPING = 0.6


def level_terms(level):
    diffusion = KAPPA_BASE * 2.0**level
    coupling = COUPLING_BASE * 2.0**level
    centre = 1.0 + 6.0 * diffusion
    determinant = centre * centre + coupling * coupling
    along = DAMPING * centre / determinant
    across = DAMPING * coupling / determinant
    return diffusion, coupling, centre, along, across


def coarse_polynomials(total_steps):
    levels = total_steps.bit_length()
    powers = 2 * levels + 1
    unit = np.eye(4 * total_steps).reshape(-1, 2, 2, total_steps)
    fields = np.zeros((4 * total_steps, 2, total_steps, powers))
    source = np.zeros_like(fields)
    fields[..., 0] = unit[:, 0]
    source[..., 0] = unit[:, 1]

    def image(values, diffusion, coupling, centre):
        out = centre * values
        out[..., 1:] -= diffusion * values[..., :-1]
        out[:, 0, 1:] -= values[:, 0, :-1]
        out[:, 1, :-1] -= values[:, 1, 1:]
        out[:, 0] += coupling * values[:, 1]
        out[:, 1] -= coupling * values[:, 0]
        return out

    for level in range(levels):
        diffusion, coupling, centre, along, across = level_terms(level)
        for _ in range(2):
            defect = source - image(fields, diffusion, coupling, centre)
            state, adjoint = defect[:, 0], defect[:, 1]
            fields = fields + np.stack([along * state - across * adjoint, across * state + along * adjoint], 1)
        if level < levels - 1:
            defect = source - image(fields, diffusion, coupling, centre)
            source = defect[:, :, 0::2] + defect[:, :, 1::2]
            fields = np.zeros_like(source)
    return fields[:, :, 0].reshape(2, 2, total_steps, 2, powers)


def plane_neighbours(values):
    length = values.shape[-1]
    columns = jnp.arange(length, dtype=jnp.int32) % NY
    single = jnp.zeros(values.shape[:-1] + (1,), jnp.float32)
    row = jnp.zeros(values.shape[:-1] + (NY,), jnp.float32)
    left = jnp.where(columns != 0, jnp.concatenate([single, values[..., :-1]], -1), 0.0)
    right = jnp.where(columns != NY - 1, jnp.concatenate([values[..., 1:], single], -1), 0.0)
    upper = jnp.concatenate([row, values[..., :-NY]], -1)
    lower = jnp.concatenate([values[..., NY:], row], -1)
    return left + right + upper + lower


def inner_neighbours(values):
    return values[..., :-2, :] + values[..., 2:, :] + plane_neighbours(values[..., 1:-1, :])


def swapped(value, axis, mask):
    return lax.ppermute(value, axis, [(i, i ^ mask) for i in range(lax.axis_size(axis))])


def shifted(value, axis, by):
    size = lax.axis_size(axis)
    return lax.ppermute(value, axis, [(i, i + by) for i in range(size) if 0 <= i + by < size])


def coarse_kernel(powers, inputs, rank_ref, weights_ref, iterate_ref, forcing_ref, keep_ref, send_ref, total):
    depth, cells = iterate_ref.shape[2:]
    slabs = total.shape[1] // depth
    columns = cells // LANES
    slab = rank_ref[1]
    base = rank_ref[0] * (powers * 2 * inputs)
    lane = lax.broadcasted_iota(jnp.int32, (depth, LANES), 1)
    sublane = lax.broadcasted_iota(jnp.int32, (depth, LANES), 0)
    low = lane < NY
    not_last = (lane % NY) != NY - 1
    not_first = (lane % NY) != 0
    top, bottom = sublane == 0, sublane == depth - 1
    zero = jnp.zeros((depth, LANES), jnp.float32)
    here = pl.ds(pl.multiple_of(slab * depth, depth), depth)

    def column(j):
        return pl.ds(j * LANES, LANES)

    def injected(power, out, values):
        first = base + (power * 2 + out) * inputs
        part = weights_ref[first] * values[0]
        for k in range(1, inputs):
            part = part + weights_ref[first + k] * values[k]
        return part

    def own(j):
        refs = (iterate_ref, forcing_ref)
        return [ref[f, n, :, column(j)] for ref in refs for f in range(2) for n in range(ref.shape[1])]

    def loaded(f, j):
        if j >= columns:
            return [zero] * slabs
        return [total[f, z * depth : (z + 1) * depth, column(j)] for z in range(slabs)]

    total[...] = jnp.zeros_like(total)
    for j in range(columns):
        values = own(j)
        for f in range(2):
            total[f, here, column(j)] = injected(powers - 1, f, values)

    def step(index, _):
        power = powers - 2 - index
        pairs = [[zero] * slabs for _ in range(2)]
        now = [loaded(f, 0) for f in range(2)]
        pairs = [now[f] for f in range(2)]
        for j in range(columns):
            values = own(j)
            for f in range(2):
                later = loaded(f, j + 1)
                current = now[f]
                pair = [a + b for a, b in zip(current, later)]
                forth = [pltpu.roll(v, 1, 0) for v in current]
                back = [pltpu.roll(v, depth - 1, 0) for v in current]
                for z in range(slabs):
                    rows = pltpu.roll(jnp.where(low, pair[z], pairs[f][z]), NY, 1)
                    left = pltpu.roll(jnp.where(not_last, current[z], 0.0), 1, 1)
                    right = pltpu.roll(jnp.where(not_first, current[z], 0.0), LANES - 1, 1)
                    above = jnp.where(top, forth[z - 1] if z else 0.0, forth[z])
                    below = jnp.where(bottom, back[z + 1] if z < slabs - 1 else 0.0, back[z])
                    total[f, z * depth : (z + 1) * depth, column(j)] = (rows + (left + right)) + (above + below)
                total[f, here, column(j)] += injected(power, f, values)
                pairs[f] = pair
                now[f] = later
        return 0

    lax.fori_loop(0, powers - 1, step, 0)
    bit = lax.rem(slab, 2)
    for half in range(slabs // 2):
        for ref, flag in ((keep_ref, bit), (send_ref, 1 - bit)):
            rows = pl.ds(pl.multiple_of((2 * half + flag) * depth, depth), depth)
            for f in range(2):
                for j in range(columns):
                    ref[half, f, j] = total[f, rows, column(j)]


def coarse_part(iterate, forcing):
    steps = iterate.shape[1]
    depth, cells = iterate.shape[2:]
    ranks, slabs = lax.axis_size("tm"), lax.axis_size("space")
    table = coarse_polynomials(steps * ranks)
    powers = table.shape[-1]
    table = table.reshape(2, 2, ranks, steps, 2, powers).transpose(2, 5, 4, 0, 1, 3).astype(np.float32)
    place = jnp.stack([lax.axis_index("tm"), lax.axis_index("space")]).astype(jnp.int32)
    half = jax.ShapeDtypeStruct((slabs // 2, 2, cells // LANES, depth, LANES), jnp.float32)
    smem = pl.BlockSpec(memory_space=pltpu.SMEM)
    vmem = pl.BlockSpec(memory_space=pltpu.VMEM)
    return pl.pallas_call(
        functools.partial(coarse_kernel, powers, 4 * steps),
        out_shape=(half, half),
        in_specs=[smem, smem, vmem, vmem],
        out_specs=(vmem, vmem),
        scratch_shapes=[pltpu.VMEM((2, depth * slabs, cells), jnp.float32)],
        compiler_params=pltpu.CompilerParams(vmem_limit_bytes=32 * 2**20),
        cost_estimate=pl.CostEstimate(flops=10**8, bytes_accessed=3 * 2**20, transcendentals=0),
    )(place, jnp.asarray(table.reshape(-1)), iterate, forcing)


def spread_sum(keep, send):
    slabs, ranks = lax.axis_size("space"), lax.axis_size("tm")
    slab = lax.axis_index("space")
    held = keep + swapped(send, "space", 1)
    mask = 2
    while mask < slabs:
        bit = (slab // mask) % 2
        held = held.reshape((-1, 2) + held.shape[1:])
        other = lax.dynamic_index_in_dim(held, 1 - bit, 1, keepdims=False)
        mine = lax.dynamic_index_in_dim(held, bit, 1, keepdims=False)
        held = mine + swapped(other, "space", mask)
        mask *= 2
    tiles = held.reshape((ranks, -1) + held.shape[-2:])
    parts = lax.all_to_all(tiles, "tm", 0, 0, tiled=True)
    part = jnp.sum(parts, axis=0)
    copies = jnp.broadcast_to(part[None], tiles.shape)
    return lax.all_to_all(copies, "tm", 0, 0, tiled=True).reshape((2, -1) + held.shape[-2:])


def smooth(iterate, forcing):
    depth = iterate.shape[2]
    rank, ranks = lax.axis_index("tm"), lax.axis_size("tm")
    slab, slabs = lax.axis_index("space"), lax.axis_size("space")
    diffusion, coupling, centre, along, across = level_terms(0)
    send_up = jnp.concatenate([iterate[:, :, -2:], forcing[:, :, -1:]], 2)
    send_down = jnp.concatenate([forcing[:, :, :1], iterate[:, :, :2]], 2)
    from_above = shifted(send_up, "space", 1)
    from_below = shifted(send_down, "space", -1)
    wide = jnp.concatenate([from_above[:, :, :2], iterate, from_below[:, :, 1:]], 2)
    source = jnp.concatenate([from_above[:, :, 2:], forcing, from_below[:, :, :1]], 2)

    def relaxed(fields, image_state, image_adjoint, source):
        defect_state = source[0] - image_state
        defect_adjoint = source[1] - image_adjoint
        return jnp.stack([
            fields[0] + along * defect_state - across * defect_adjoint,
            fields[1] + across * defect_state + along * defect_adjoint,
        ])

    def images(fields, around, before, after):
        state, adjoint = fields
        return (
            centre * state - diffusion * around[0] - before + coupling * adjoint,
            centre * adjoint - diffusion * around[1] - after - coupling * state,
        )

    middle = wide[:, :, 1:-1]
    none = jnp.zeros_like(middle[0, :1])
    before = jnp.concatenate([none, middle[0, :-1]], 0)
    after = jnp.concatenate([middle[1, 1:], none], 0)
    first = relaxed(middle, *images(middle, inner_neighbours(wide), before, after), source)
    plane = jnp.arange(depth + 2)
    inside = ((plane > 0) | (slab > 0)) & ((plane < depth + 1) | (slab < slabs - 1))
    first = jnp.where(inside[:, None], first, 0.0)
    forth = jnp.concatenate([middle[0, -1], first[0, -1, 1:-1]], 0)
    back = jnp.concatenate([middle[1, 0], first[1, 0, 1:-1]], 0)
    forth = shifted(forth, "tm", 1)
    back = shifted(back, "tm", -1)
    state_before, adjoint_after = forth[: depth + 2], back[: depth + 2]
    start = first[:, :1] + jnp.stack([along * state_before, across * state_before])[:, None]
    first = jnp.concatenate([start, first[:, 1:]], 1)
    end = first[:, -1:] + jnp.stack([-across * adjoint_after, along * adjoint_after])[:, None]
    first = jnp.concatenate([first[:, :-1], end], 1)
    before = jnp.where(rank > 0, forth[depth + 2 :] - across * iterate[1, 0], 0.0)
    after = jnp.where(rank < ranks - 1, back[depth + 2 :] + across * iterate[0, -1], 0.0)
    middle = first[:, :, 1:-1]
    before = jnp.concatenate([before[None], middle[0, :-1]], 0)
    after = jnp.concatenate([middle[1, 1:], after[None]], 0)
    return relaxed(middle, *images(middle, inner_neighbours(first), before, after), forcing)


def local(iterate, forcing):
    keep, send = coarse_part(iterate, forcing)
    smoothed = smooth(iterate, forcing)
    coarse = spread_sum(keep, send)
    coarse = coarse.transpose(0, 2, 1, 3).reshape(iterate.shape[:1] + iterate.shape[2:])
    return smoothed, jnp.broadcast_to(coarse[:, None], iterate.shape)


def solution(mesh):
    specs = P(None, "tm", "space", None)
    return jax.shard_map(local, mesh=mesh, in_specs=(specs, specs), out_specs=(specs, specs), check_vma=False)
```

```python
import functools

import numpy as np

import jax
import jax.numpy as jnp
from jax import lax
from jax.experimental import pallas as pl
from jax.experimental.pallas import tpu as pltpu
from jax.sharding import PartitionSpec as P

NY = 64
LANES = 128

KAPPA_BASE = 0.25
COUPLING_BASE = 0.5
DAMPING = 0.6


def level_terms(level):
    diffusion = KAPPA_BASE * 2.0**level
    coupling = COUPLING_BASE * 2.0**level
    centre = 1.0 + 6.0 * diffusion
    determinant = centre * centre + coupling * coupling
    along = DAMPING * centre / determinant
    across = DAMPING * coupling / determinant
    return diffusion, coupling, centre, along, across


def coarse_polynomials(total_steps):
    levels = total_steps.bit_length()
    powers = 2 * levels + 1
    unit = np.eye(4 * total_steps).reshape(-1, 2, 2, total_steps)
    fields = np.zeros((4 * total_steps, 2, total_steps, powers))
    source = np.zeros_like(fields)
    fields[..., 0] = unit[:, 0]
    source[..., 0] = unit[:, 1]

    def image(values, diffusion, coupling, centre):
        out = centre * values
        out[..., 1:] -= diffusion * values[..., :-1]
        out[:, 0, 1:] -= values[:, 0, :-1]
        out[:, 1, :-1] -= values[:, 1, 1:]
        out[:, 0] += coupling * values[:, 1]
        out[:, 1] -= coupling * values[:, 0]
        return out

    for level in range(levels):
        diffusion, coupling, centre, along, across = level_terms(level)
        for _ in range(2):
            defect = source - image(fields, diffusion, coupling, centre)
            state, adjoint = defect[:, 0], defect[:, 1]
            fields = fields + np.stack([along * state - across * adjoint, across * state + along * adjoint], 1)
        if level < levels - 1:
            defect = source - image(fields, diffusion, coupling, centre)
            source = defect[:, :, 0::2] + defect[:, :, 1::2]
            fields = np.zeros_like(source)
    return fields[:, :, 0].reshape(2, 2, total_steps, 2, powers)


def plane_neighbours(values):
    length = values.shape[-1]
    columns = jnp.arange(length, dtype=jnp.int32) % NY
    single = jnp.zeros(values.shape[:-1] + (1,), jnp.float32)
    row = jnp.zeros(values.shape[:-1] + (NY,), jnp.float32)
    left = jnp.where(columns != 0, jnp.concatenate([single, values[..., :-1]], -1), 0.0)
    right = jnp.where(columns != NY - 1, jnp.concatenate([values[..., 1:], single], -1), 0.0)
    upper = jnp.concatenate([row, values[..., :-NY]], -1)
    lower = jnp.concatenate([values[..., NY:], row], -1)
    return left + right + upper + lower


def inner_neighbours(values):
    return values[..., :-2, :] + values[..., 2:, :] + plane_neighbours(values[..., 1:-1, :])


def swapped(value, axis, mask):
    return lax.ppermute(value, axis, [(i, i ^ mask) for i in range(lax.axis_size(axis))])


def shifted(value, axis, by):
    size = lax.axis_size(axis)
    return lax.ppermute(value, axis, [(i, i + by) for i in range(size) if 0 <= i + by < size])


def coarse_kernel(powers, inputs, slabs, place_ref, weights_ref, iterate_ref, forcing_ref, keep_ref, send_ref, even, odd):
    depth, cells = iterate_ref.shape[2:]
    columns = cells // LANES
    middle = slabs - 1
    slab = place_ref[1]
    base = place_ref[0] * (powers * 2 * inputs)
    lane = lax.broadcasted_iota(jnp.int32, (depth, LANES), 1)
    sublane = lax.broadcasted_iota(jnp.int32, (depth, LANES), 0)
    low = lane < NY
    not_last = (lane % NY) != NY - 1
    not_first = (lane % NY) != 0
    top, bottom = sublane == 0, sublane == depth - 1
    zero = jnp.zeros((depth, LANES), jnp.float32)

    def inside(away):
        at = slab + away
        return jnp.where((at >= 0) & (at < slabs), 1.0, 0.0).astype(jnp.float32)

    def weights(power, out):
        first = base + (power * 2 + out) * inputs
        return [weights_ref[first + k] for k in range(inputs)]

    def injected(factors, j):
        refs = (iterate_ref, forcing_ref)
        columns = pl.ds(j * LANES, LANES)
        values = [ref[f, n, :, columns] for ref in refs for f in range(2) for n in range(ref.shape[1])]
        terms = [factor * value for factor, value in zip(factors, values)]
        while len(terms) > 1:
            terms = [sum(terms[k : k + 2]) for k in range(0, len(terms), 2)]
        return terms[0]

    def advance(source, target, power, reach):
        aways = list(range(-reach, reach + 1))
        masks = [inside(away) for away in aways]
        for f in range(2):
            factors = weights(power, f)

            def loaded(j):
                if j >= columns:
                    return [zero for _ in aways]
                return [source[f, middle + away, j] for away in aways]

            now = loaded(0)
            before = now
            for j in range(columns):
                later = loaded(j + 1)
                pair = [a + b for a, b in zip(now, later)]
                forth = [zero] + [pltpu.roll(v, 1, 0) for v in now]
                back = [pltpu.roll(v, depth - 1, 0) for v in now] + [zero]
                for k, away in enumerate(aways):
                    rows = pltpu.roll(jnp.where(low, pair[k], before[k]), NY, 1)
                    left = pltpu.roll(jnp.where(not_last, now[k], 0.0), 1, 1)
                    right = pltpu.roll(jnp.where(not_first, now[k], 0.0), LANES - 1, 1)
                    above = jnp.where(top, forth[k], forth[k + 1])
                    below = jnp.where(bottom, back[k + 1], back[k])
                    value = (rows + (left + right)) + (above + below)
                    if away:
                        value = value * masks[k]
                    else:
                        value = value + injected(factors, j)
                    target[f, middle + away, j] = value
                before, now = pair, later

    even[...] = jnp.zeros_like(even)
    odd[...] = jnp.zeros_like(odd)
    for f in range(2):
        factors = weights(powers - 1, f)
        for j in range(columns):
            even[f, middle, j] = injected(factors, j)
    buffers = (even, odd)
    done = 0
    while done < powers - 1:
        reach = min(done // depth + 1, middle)
        count = powers - 1 - done if reach == middle else min(depth, powers - 1 - done)

        def twice(index, _):
            power = powers - 2 - done - 2 * index
            advance(buffers[0], buffers[1], power, reach)
            advance(buffers[1], buffers[0], power - 1, reach)
            return 0

        lax.fori_loop(0, count // 2, twice, 0)
        done += count
        if count % 2:
            advance(buffers[0], buffers[1], powers - 1 - done, reach)
            buffers = buffers[::-1]

    bit = lax.rem(slab, 2)
    for half in range(slabs // 2):
        for ref, flag in ((keep_ref, bit), (send_ref, 1 - bit)):
            away = 2 * half + flag - slab
            for f in range(2):
                ref[half, f] = buffers[0][f, middle + away]


def coarse_part(iterate, forcing):
    steps = iterate.shape[1]
    depth, cells = iterate.shape[2:]
    ranks, slabs = lax.axis_size("tm"), lax.axis_size("space")
    table = coarse_polynomials(steps * ranks)
    powers = table.shape[-1]
    table = table.reshape(2, 2, ranks, steps, 2, powers).transpose(2, 5, 4, 0, 1, 3).astype(np.float32)
    place = jnp.stack([lax.axis_index("tm"), lax.axis_index("space")]).astype(jnp.int32)
    half = jax.ShapeDtypeStruct((slabs // 2, 2, cells // LANES, depth, LANES), jnp.float32)
    smem = pl.BlockSpec(memory_space=pltpu.SMEM)
    vmem = pl.BlockSpec(memory_space=pltpu.VMEM)
    return pl.pallas_call(
        functools.partial(coarse_kernel, powers, 4 * steps, slabs),
        out_shape=(half, half),
        in_specs=[smem, smem, vmem, vmem],
        out_specs=(vmem, vmem),
        scratch_shapes=[pltpu.VMEM((2, 2 * slabs - 1, cells // LANES, depth, LANES), jnp.float32)] * 2,
        compiler_params=pltpu.CompilerParams(vmem_limit_bytes=32 * 2**20),
        cost_estimate=pl.CostEstimate(flops=10**8, bytes_accessed=3 * 2**20, transcendentals=0),
    )(place, jnp.asarray(table.reshape(-1)), iterate, forcing)


def spread_sum(keep, send):
    slabs, ranks = lax.axis_size("space"), lax.axis_size("tm")
    slab = lax.axis_index("space")
    held = keep + swapped(send, "space", 1)
    mask = 2
    while mask < slabs:
        bit = (slab // mask) % 2
        held = held.reshape((-1, 2) + held.shape[1:])
        other = lax.dynamic_index_in_dim(held, 1 - bit, 1, keepdims=False)
        mine = lax.dynamic_index_in_dim(held, bit, 1, keepdims=False)
        held = mine + swapped(other, "space", mask)
        mask *= 2
    tiles = held.reshape((ranks, -1) + held.shape[-2:])
    parts = lax.all_to_all(tiles, "tm", 0, 0, tiled=True)
    part = jnp.sum(parts, axis=0)
    copies = jnp.broadcast_to(part[None], tiles.shape)
    return lax.all_to_all(copies, "tm", 0, 0, tiled=True).reshape((2, -1) + held.shape[-2:])


def smooth(iterate, forcing):
    depth = iterate.shape[2]
    rank, ranks = lax.axis_index("tm"), lax.axis_size("tm")
    slab, slabs = lax.axis_index("space"), lax.axis_size("space")
    diffusion, coupling, centre, along, across = level_terms(0)
    send_up = jnp.concatenate([iterate[:, :, -2:], forcing[:, :, -1:]], 2)
    send_down = jnp.concatenate([forcing[:, :, :1], iterate[:, :, :2]], 2)
    from_above = shifted(send_up, "space", 1)
    from_below = shifted(send_down, "space", -1)
    wide = jnp.concatenate([from_above[:, :, :2], iterate, from_below[:, :, 1:]], 2)
    source = jnp.concatenate([from_above[:, :, 2:], forcing, from_below[:, :, :1]], 2)

    def relaxed(fields, image_state, image_adjoint, source):
        defect_state = source[0] - image_state
        defect_adjoint = source[1] - image_adjoint
        return jnp.stack([
            fields[0] + along * defect_state - across * defect_adjoint,
            fields[1] + across * defect_state + along * defect_adjoint,
        ])

    def images(fields, around, before, after):
        state, adjoint = fields
        return (
            centre * state - diffusion * around[0] - before + coupling * adjoint,
            centre * adjoint - diffusion * around[1] - after - coupling * state,
        )

    middle = wide[:, :, 1:-1]
    none = jnp.zeros_like(middle[0, :1])
    before = jnp.concatenate([none, middle[0, :-1]], 0)
    after = jnp.concatenate([middle[1, 1:], none], 0)
    first = relaxed(middle, *images(middle, inner_neighbours(wide), before, after), source)
    plane = jnp.arange(depth + 2)
    inside = ((plane > 0) | (slab > 0)) & ((plane < depth + 1) | (slab < slabs - 1))
    first = jnp.where(inside[:, None], first, 0.0)
    forth = jnp.concatenate([middle[0, -1], first[0, -1, 1:-1]], 0)
    back = jnp.concatenate([middle[1, 0], first[1, 0, 1:-1]], 0)
    forth = shifted(forth, "tm", 1)
    back = shifted(back, "tm", -1)
    state_before, adjoint_after = forth[: depth + 2], back[: depth + 2]
    start = first[:, :1] + jnp.stack([along * state_before, across * state_before])[:, None]
    first = jnp.concatenate([start, first[:, 1:]], 1)
    end = first[:, -1:] + jnp.stack([-across * adjoint_after, along * adjoint_after])[:, None]
    first = jnp.concatenate([first[:, :-1], end], 1)
    before = jnp.where(rank > 0, forth[depth + 2 :] - across * iterate[1, 0], 0.0)
    after = jnp.where(rank < ranks - 1, back[depth + 2 :] + across * iterate[0, -1], 0.0)
    middle = first[:, :, 1:-1]
    before = jnp.concatenate([before[None], middle[0, :-1]], 0)
    after = jnp.concatenate([middle[1, 1:], after[None]], 0)
    return relaxed(middle, *images(middle, inner_neighbours(first), before, after), forcing)


def local(iterate, forcing):
    keep, send = coarse_part(iterate, forcing)
    smoothed = smooth(iterate, forcing)
    coarse = spread_sum(keep, send)
    coarse = coarse.transpose(0, 2, 1, 3).reshape(iterate.shape[:1] + iterate.shape[2:])
    return smoothed, jnp.broadcast_to(coarse[:, None], iterate.shape)


def solution(mesh):
    specs = P(None, "tm", "space", None)
    return jax.shard_map(local, mesh=mesh, in_specs=(specs, specs), out_specs=(specs, specs), check_vma=False)
```

```python
import functools

import numpy as np

import jax
import jax.numpy as jnp
from jax import lax
from jax.experimental import pallas as pl
from jax.experimental.pallas import tpu as pltpu
from jax.sharding import PartitionSpec as P

NY = 64
LANES = 128

KAPPA_BASE = 0.25
COUPLING_BASE = 0.5
DAMPING = 0.6


def level_terms(level):
    diffusion = KAPPA_BASE * 2.0**level
    coupling = COUPLING_BASE * 2.0**level
    centre = 1.0 + 6.0 * diffusion
    determinant = centre * centre + coupling * coupling
    along = DAMPING * centre / determinant
    across = DAMPING * coupling / determinant
    return diffusion, coupling, centre, along, across


def coarse_polynomials(total_steps):
    levels = total_steps.bit_length()
    powers = 2 * levels + 1
    unit = np.eye(4 * total_steps).reshape(-1, 2, 2, total_steps)
    fields = np.zeros((4 * total_steps, 2, total_steps, powers))
    source = np.zeros_like(fields)
    fields[..., 0] = unit[:, 0]
    source[..., 0] = unit[:, 1]

    def image(values, diffusion, coupling, centre):
        out = centre * values
        out[..., 1:] -= diffusion * values[..., :-1]
        out[:, 0, 1:] -= values[:, 0, :-1]
        out[:, 1, :-1] -= values[:, 1, 1:]
        out[:, 0] += coupling * values[:, 1]
        out[:, 1] -= coupling * values[:, 0]
        return out

    for level in range(levels):
        diffusion, coupling, centre, along, across = level_terms(level)
        for _ in range(2):
            defect = source - image(fields, diffusion, coupling, centre)
            state, adjoint = defect[:, 0], defect[:, 1]
            fields = fields + np.stack([along * state - across * adjoint, across * state + along * adjoint], 1)
        if level < levels - 1:
            defect = source - image(fields, diffusion, coupling, centre)
            source = defect[:, :, 0::2] + defect[:, :, 1::2]
            fields = np.zeros_like(source)
    return fields[:, :, 0].reshape(2, 2, total_steps, 2, powers)


def lane_index(depth):
    return lax.broadcasted_iota(jnp.int32, (depth, LANES), 1)


def sublane_index(depth):
    return lax.broadcasted_iota(jnp.int32, (depth, LANES), 0)


def column(j):
    return pl.ds(j * LANES, LANES)


def swapped_halves(value):
    return pltpu.roll(value, NY, 1)


def beside(value, lane):
    left = pltpu.roll(jnp.where((lane % NY) != NY - 1, value, 0.0), 1, 1)
    right = pltpu.roll(jnp.where((lane % NY) != 0, value, 0.0), LANES - 1, 1)
    return left + right


def tree_sum(terms):
    while len(terms) > 1:
        terms = [sum(terms[k : k + 2]) for k in range(0, len(terms), 2)]
    return terms[0]


def coarse_kernel(powers, steps, slabs, middle, place_ref, weights_ref, iterate_ref, forcing_ref, keep_ref, send_ref, even, odd, packed):
    depth, cells = iterate_ref.shape[2:]
    columns = cells // LANES
    rows = cells // NY
    inputs = 2 * steps
    slab, shift = place_ref[1], place_ref[2]
    base = place_ref[0] * (powers * 4 * inputs)
    lane = lane_index(depth)
    low = lane < NY
    zero = jnp.zeros((depth, LANES), jnp.float32)

    def inside(away):
        at = slab + away
        return jnp.where((at >= 0) & (at < slabs), 1.0, 0.0).astype(jnp.float32)

    for j in range(columns):
        for kind, ref in enumerate((iterate_ref, forcing_ref)):
            for n in range(steps):
                state, adjoint = ref[0, n, :, column(j)], ref[1, n, :, column(j)]
                state_turned, adjoint_turned = swapped_halves(state), swapped_halves(adjoint)
                k = 2 * (kind * steps + n)
                packed[k, 2 * j] = jnp.where(low, state, adjoint_turned)
                packed[k, 2 * j + 1] = jnp.where(low, state_turned, adjoint)
                packed[k + 1, 2 * j] = jnp.where(low, adjoint, state_turned)
                packed[k + 1, 2 * j + 1] = jnp.where(low, adjoint_turned, state)

    def weights(power):
        first = base + power * 4 * inputs
        return [
            jnp.where(low, weights_ref[first + 2 * k], weights_ref[first + 2 * k + 1]) for k in range(2 * inputs)
        ]

    def injected(factors, i):
        return tree_sum([factor * packed[k, i] for k, factor in enumerate(factors)])

    def advance(source, target, power, reach):
        aways = list(range(-reach, reach + 1))
        masks = [inside(away) for away in aways]
        factors = weights(power)

        def loaded(i):
            if i >= rows:
                return [zero for _ in aways]
            return [source[i, pl.ds((middle + away) * depth, depth), :] for away in aways]

        before = [zero for _ in aways]
        now = loaded(0)
        for i in range(rows):
            later = loaded(i + 1)
            for k, away in enumerate(aways):
                start = (middle + away) * depth
                above = source[i, pl.ds(shift + (start - 1), depth), :]
                below = source[i, pl.ds(shift + (start + 1), depth), :]
                value = (before[k] + later[k]) + beside(now[k], lane) + (above + below)
                if away:
                    value = value * masks[k]
                else:
                    value = value + injected(factors, i)
                target[i, pl.ds(start, depth), :] = value
            before, now = now, later

    even[...] = jnp.zeros_like(even)
    odd[...] = jnp.zeros_like(odd)
    factors = weights(powers - 1)
    for i in range(rows):
        even[i, pl.ds(middle * depth, depth), :] = injected(factors, i)
    buffers = (even, odd)
    done = 0
    while done < powers - 1:
        reach = min(done // depth + 1, slabs - 1)
        count = powers - 1 - done if reach == slabs - 1 else min(depth, powers - 1 - done)

        def twice(index, _):
            power = powers - 2 - done - 2 * index
            advance(buffers[0], buffers[1], power, reach)
            advance(buffers[1], buffers[0], power - 1, reach)
            return 0

        lax.fori_loop(0, count // 2, twice, 0)
        done += count
        if count % 2:
            advance(buffers[0], buffers[1], powers - 1 - done, reach)
            buffers = buffers[::-1]

    final = buffers[0]
    tiles = keep_ref.shape[2]
    bit = lax.rem(slab, 2)
    for half in range(slabs // 2):
        for ref, flag in ((keep_ref, bit), (send_ref, 1 - bit)):
            away = 2 * half + flag - slab
            planes = pl.ds(pl.multiple_of((middle + away) * depth, depth), depth)
            for j in range(columns):
                first, second = final[2 * j, planes, :], final[2 * j + 1, planes, :]
                for f, value in (
                    (0, jnp.where(low, first, swapped_halves(second))),
                    (1, jnp.where(low, swapped_halves(first), second)),
                ):
                    tile = f * columns + j
                    ref[tile // tiles, half, tile % tiles] = value


def vmem_call(kernel, out_shapes, smem_inputs, inputs, scratch=(), flops=10**6):
    smem = pl.BlockSpec(memory_space=pltpu.SMEM)
    vmem = pl.BlockSpec(memory_space=pltpu.VMEM)
    out_shape = tuple(jax.ShapeDtypeStruct(shape, jnp.float32) for shape in out_shapes)
    return pl.pallas_call(
        kernel,
        out_shape=out_shape,
        in_specs=[smem] * len(smem_inputs) + [vmem] * len(inputs),
        out_specs=(vmem,) * len(out_shape),
        scratch_shapes=list(scratch),
        compiler_params=pltpu.CompilerParams(vmem_limit_bytes=32 * 2**20),
        cost_estimate=pl.CostEstimate(flops=flops, bytes_accessed=2**20, transcendentals=0),
    )(*smem_inputs, *inputs)


def coarse_part(place, iterate, forcing):
    steps = iterate.shape[1]
    depth, cells = iterate.shape[2:]
    ranks, slabs = lax.axis_size("tm"), 2 * lax.axis_size("pair")
    table = coarse_polynomials(steps * ranks)
    powers = table.shape[-1]
    table = table.reshape(2, 2, ranks, steps, 2, powers)
    same = np.stack([table[:, 0, :, :, 0], table[:, 1, :, :, 1]], -1)
    other = np.stack([table[:, 1, :, :, 0], table[:, 0, :, :, 1]], -1)
    weights = np.stack([same, other], -2).transpose(1, 3, 0, 2, 4, 5).astype(np.float32)
    reach = min(-(-(powers - 1) // depth), slabs - 1)
    middle = max(reach + 1, slabs - 1)
    tiles = 2 * cells // LANES
    half = (ranks, slabs // 2, tiles // ranks, depth, LANES)
    buffer = pltpu.VMEM((cells // NY, (2 * middle + 1) * depth, LANES), jnp.float32)
    packed = pltpu.VMEM((4 * steps, cells // NY, depth, LANES), jnp.float32)
    return vmem_call(
        functools.partial(coarse_kernel, powers, steps, slabs, middle),
        (half, half),
        (place, jnp.asarray(weights.reshape(-1))),
        (iterate, forcing),
        (buffer, buffer, packed),
        flops=10**8,
    )


def relaxed(fields, around, before, after, source):
    diffusion, coupling, centre, along, across = level_terms(0)
    state, adjoint = fields
    defect_state = source[0] - (centre * state - diffusion * around[0] - before + coupling * adjoint)
    defect_adjoint = source[1] - (centre * adjoint - diffusion * around[1] - after - coupling * state)
    return (
        state + along * defect_state - across * defect_adjoint,
        adjoint + across * defect_state + along * defect_adjoint,
    )


def first_kernel(iterate_ref, forcing_ref, first_ref, up_ref, down_ref):
    steps, depth, cells = iterate_ref.shape[1:]
    columns = cells // LANES
    lane, sublane = lane_index(depth), sublane_index(depth)
    low = lane < NY
    zero = jnp.zeros((depth, LANES), jnp.float32)
    slots = [(f, n) for f in range(2) for n in range(steps)]

    def loaded(j):
        return {s: iterate_ref[s[0], s[1], :, column(j)] if j < columns else zero for s in slots}

    now = loaded(0)
    pairs_before = now
    for j in range(columns):
        later = loaded(j + 1)
        pairs = {s: now[s] + later[s] for s in slots}
        around = {}
        for s in slots:
            across_rows = swapped_halves(jnp.where(low, pairs[s], pairs_before[s]))
            above = jnp.where(sublane == 0, 0.0, pltpu.roll(now[s], 1, 0))
            below = jnp.where(sublane == depth - 1, 0.0, pltpu.roll(now[s], depth - 1, 0))
            around[s] = across_rows + beside(now[s], lane) + (above + below)
        for n in range(steps):
            values = relaxed(
                (now[0, n], now[1, n]),
                (around[0, n], around[1, n]),
                now[0, n - 1] if n else zero,
                now[1, n + 1] if n < steps - 1 else zero,
                (forcing_ref[0, n, :, column(j)], forcing_ref[1, n, :, column(j)]),
            )
            for f in range(2):
                first_ref[f, n, :, column(j)] = values[f]
                slot = f * steps + n
                for ref, plane in ((up_ref, depth - 1), (down_ref, 0)):
                    ref[slot : slot + 1, column(j)] = now[f, n][plane : plane + 1]
                    slot_after = 2 * steps + slot
                    ref[slot_after : slot_after + 1, column(j)] = values[f][plane : plane + 1]
        now, pairs_before = later, pairs


def second_kernel(
    steps, slabs, place_ref, iterate_ref, first_ref, up_ref, down_ref, above_ref, below_ref, swept_ref, edge_ref, forth_ref, back_ref
):
    diffusion, _, _, along, across = level_terms(0)
    depth, cells = iterate_ref.shape[2:]
    columns = cells // LANES
    slab = place_ref[1]
    sublane = sublane_index(depth)
    count = 2 * steps
    has_above = jnp.where(slab > 0, 1.0, 0.0).astype(jnp.float32)
    has_below = jnp.where(slab < slabs - 1, 1.0, 0.0).astype(jnp.float32)

    def mixed(rows):
        state, adjoint = rows[:steps], rows[steps:]
        return jnp.concatenate(
            [
                (along * diffusion) * state - (across * diffusion) * adjoint,
                (across * diffusion) * state + (along * diffusion) * adjoint,
            ],
            0,
        )

    def one(j):
        return slice(j * LANES, (j + 1) * LANES)

    for j in range(columns):
        from_above, from_below = above_ref[:, one(j)], below_ref[:, one(j)]
        edge_ref[:count, one(j)] = (from_above[count:] + mixed(down_ref[:count, one(j)])) * has_above
        edge_ref[count:, one(j)] = (from_below[count:] + mixed(up_ref[:count, one(j)])) * has_below
        add_above, add_below = mixed(from_above[:count]), mixed(from_below[:count])
        for f in range(2):
            for n in range(steps):
                k = f * steps + n
                value = first_ref[f, n, :, one(j)]
                value = value + jnp.where(sublane == 0, add_above[k : k + 1], 0.0)
                value = value + jnp.where(sublane == depth - 1, add_below[k : k + 1], 0.0)
                swept_ref[f, n, :, one(j)] = value
                for ref, field, step in ((forth_ref, 0, steps - 1), (back_ref, 1, 0)):
                    if (f, n) == (field, step):
                        ref[j] = iterate_ref[f, n, :, one(j)]
                        ref[columns + j] = value
                        block, row = 2 * columns + j // depth, j % depth
                        ref[block, row : row + 1] = from_above[k : k + 1]
                        block += columns // depth
                        ref[block, row : row + 1] = from_below[k : k + 1]


def third_kernel(steps, ranks, place_ref, iterate_ref, forcing_ref, swept_ref, edge_ref, forth_ref, back_ref, out_ref):
    _, _, _, along, across = level_terms(0)
    depth, cells = iterate_ref.shape[2:]
    columns = cells // LANES
    rank = place_ref[0]
    lane, sublane = lane_index(depth), sublane_index(depth)
    low = lane < NY
    zero = jnp.zeros((depth, LANES), jnp.float32)
    slots = [(f, n) for f in range(2) for n in range(steps)]
    has_before = jnp.where(rank > 0, 1.0, 0.0).astype(jnp.float32)
    has_after = jnp.where(rank < ranks - 1, 1.0, 0.0).astype(jnp.float32)
    gain = {(0, 0): ("forth", along), (1, 0): ("forth", across), (0, steps - 1): ("back", -across), (1, steps - 1): ("back", along)}

    def loaded(j):
        if j >= columns:
            return {s: zero for s in slots}
        near = {"forth": forth_ref[j], "back": back_ref[j]}
        values = {}
        for s in slots:
            values[s] = swept_ref[s[0], s[1], :, column(j)]
            if s in gain:
                values[s] = values[s] + gain[s][1] * near[gain[s][0]]
        return values

    def edges(j, side):
        block, row = 2 * columns + side * (columns // depth) + j // depth, j % depth
        near = {"forth": forth_ref[block, row : row + 1], "back": back_ref[block, row : row + 1]}
        values = {}
        for s in slots:
            k = side * 2 * steps + s[0] * steps + s[1]
            values[s] = edge_ref[k : k + 1, column(j)]
            if s in gain:
                values[s] = values[s] + gain[s][1] * near[gain[s][0]]
        return values

    now = loaded(0)
    pairs_before = now
    for j in range(columns):
        later = loaded(j + 1)
        over, under = edges(j, 0), edges(j, 1)
        pairs = {s: now[s] + later[s] for s in slots}
        around = {}
        for s in slots:
            across_rows = swapped_halves(jnp.where(low, pairs[s], pairs_before[s]))
            above = jnp.where(sublane == 0, over[s], pltpu.roll(now[s], 1, 0))
            below = jnp.where(sublane == depth - 1, under[s], pltpu.roll(now[s], depth - 1, 0))
            around[s] = across_rows + beside(now[s], lane) + (above + below)
        before = (forth_ref[columns + j] - across * iterate_ref[1, 0, :, column(j)]) * has_before
        after = (back_ref[columns + j] + across * iterate_ref[0, steps - 1, :, column(j)]) * has_after
        for n in range(steps):
            values = relaxed(
                (now[0, n], now[1, n]),
                (around[0, n], around[1, n]),
                now[0, n - 1] if n else before,
                now[1, n + 1] if n < steps - 1 else after,
                (forcing_ref[0, n, :, column(j)], forcing_ref[1, n, :, column(j)]),
            )
            for f in range(2):
                out_ref[f, n, :, column(j)] = values[f]
        now, pairs_before = later, pairs


def shifted(value, axis, by):
    size = lax.axis_size(axis)
    return lax.ppermute(value, axis, [(i, i + by) for i in range(size) if 0 <= i + by < size])


def sum_kernel(parts_ref, copies_ref):
    tiles = copies_ref.shape[1]
    for tile in range(tiles):
        total = tree_sum([parts_ref[k, tile] for k in range(parts_ref.shape[0])])
        for k in range(copies_ref.shape[0]):
            copies_ref[k, tile] = total


def local(iterate, forcing):
    steps, depth, cells = iterate.shape[1:]
    columns = cells // LANES
    ranks, slabs = lax.axis_size("tm"), 2 * lax.axis_size("pair")
    place = jnp.stack([lax.axis_index("tm"), lax.axis_index(("pair", "core")), jnp.zeros((), jnp.int32)]).astype(jnp.int32)
    first, up, down = vmem_call(
        first_kernel, (iterate.shape, (4 * steps, cells), (4 * steps, cells)), (), (iterate, forcing)
    )
    above = shifted(up, ("pair", "core"), 1)
    below = shifted(down, ("pair", "core"), -1)
    payload = (2 * columns + 2 * columns // depth, depth, LANES)
    swept, edge, forth, back = vmem_call(
        functools.partial(second_kernel, steps, slabs),
        (iterate.shape, (4 * steps, cells), payload, payload),
        (place,),
        (iterate, first, up, down, above, below),
    )
    forth = shifted(forth, "tm", 1)
    back = shifted(back, "tm", -1)

    keep, send = coarse_part(place, iterate, forcing)
    held = keep + lax.ppermute(send, "core", [(0, 1), (1, 0)])
    shape = held.shape
    parts = lax.all_to_all(held.reshape((-1,) + shape[2:]), ("tm", "pair"), 0, 0, tiled=True)
    (copies,) = vmem_call(sum_kernel, ((ranks,) + shape[2:],), (), (parts,))
    coarse = lax.all_to_all(copies, "tm", 0, 0, tiled=True).reshape(2, columns, depth, LANES)
    coarse = coarse.transpose(0, 2, 1, 3).reshape(2, depth, cells)

    (smoothed,) = vmem_call(
        functools.partial(third_kernel, steps, ranks),
        (iterate.shape,),
        (place,),
        (iterate, forcing, swept, edge, forth, back),
    )
    return smoothed, jnp.broadcast_to(coarse[:, None], iterate.shape)


def solution(mesh):
    ranks, slabs = mesh.shape["tm"], mesh.shape["space"]
    fine = jax.sharding.Mesh(mesh.devices.reshape(ranks, slabs // 2, 2), ("tm", "pair", "core"))
    specs = P(None, "tm", ("pair", "core"), None)
    return jax.shard_map(local, mesh=fine, in_specs=(specs, specs), out_specs=(specs, specs), check_vma=False)
```

```python
import functools

import numpy as np

import jax
import jax.numpy as jnp
from jax import lax
from jax.experimental import pallas as pl
from jax.experimental.pallas import tpu as pltpu
from jax.sharding import PartitionSpec as P

NY = 64
LANES = 128

KAPPA_BASE = 0.25
COUPLING_BASE = 0.5
DAMPING = 0.6


def level_terms(level):
    diffusion = KAPPA_BASE * 2.0**level
    coupling = COUPLING_BASE * 2.0**level
    centre = 1.0 + 6.0 * diffusion
    determinant = centre * centre + coupling * coupling
    along = DAMPING * centre / determinant
    across = DAMPING * coupling / determinant
    return diffusion, coupling, centre, along, across


def coarse_polynomials(total_steps):
    levels = total_steps.bit_length()
    powers = 2 * levels + 1
    unit = np.eye(4 * total_steps).reshape(-1, 2, 2, total_steps)
    fields = np.zeros((4 * total_steps, 2, total_steps, powers))
    source = np.zeros_like(fields)
    fields[..., 0] = unit[:, 0]
    source[..., 0] = unit[:, 1]

    def image(values, diffusion, coupling, centre):
        out = centre * values
        out[..., 1:] -= diffusion * values[..., :-1]
        out[:, 0, 1:] -= values[:, 0, :-1]
        out[:, 1, :-1] -= values[:, 1, 1:]
        out[:, 0] += coupling * values[:, 1]
        out[:, 1] -= coupling * values[:, 0]
        return out

    for level in range(levels):
        diffusion, coupling, centre, along, across = level_terms(level)
        for _ in range(2):
            defect = source - image(fields, diffusion, coupling, centre)
            state, adjoint = defect[:, 0], defect[:, 1]
            fields = fields + np.stack([along * state - across * adjoint, across * state + along * adjoint], 1)
        if level < levels - 1:
            defect = source - image(fields, diffusion, coupling, centre)
            source = defect[:, :, 0::2] + defect[:, :, 1::2]
            fields = np.zeros_like(source)
    return fields[:, :, 0].reshape(2, 2, total_steps, 2, powers)


def lane_index(depth):
    return lax.broadcasted_iota(jnp.int32, (depth, LANES), 1)


def sublane_index(depth):
    return lax.broadcasted_iota(jnp.int32, (depth, LANES), 0)


def column(j):
    return pl.ds(j * LANES, LANES)


def swapped_halves(value):
    return pltpu.roll(value, NY, 1)


def beside(value, lane):
    left = pltpu.roll(jnp.where((lane % NY) != NY - 1, value, 0.0), 1, 1)
    right = pltpu.roll(jnp.where((lane % NY) != 0, value, 0.0), LANES - 1, 1)
    return left + right


def tree_sum(terms):
    while len(terms) > 1:
        terms = [sum(terms[k : k + 2]) for k in range(0, len(terms), 2)]
    return terms[0]


def coarse_kernel(powers, steps, slabs, middle, place_ref, weights_ref, iterate_ref, forcing_ref, keep_ref, send_ref, even, odd, packed):
    depth, cells = iterate_ref.shape[2:]
    columns = cells // LANES
    rows = cells // NY
    inputs = 2 * steps
    slab, shift = place_ref[1], place_ref[2]
    base = place_ref[0] * (powers * 4 * inputs)
    lane = lane_index(depth)
    low = lane < NY
    zero = jnp.zeros((depth, LANES), jnp.float32)

    def inside(away):
        at = slab + away
        return jnp.where((at >= 0) & (at < slabs), 1.0, 0.0).astype(jnp.float32)

    for j in range(columns):
        for kind, ref in enumerate((iterate_ref, forcing_ref)):
            for n in range(steps):
                state, adjoint = ref[0, n, :, column(j)], ref[1, n, :, column(j)]
                state_turned, adjoint_turned = swapped_halves(state), swapped_halves(adjoint)
                k = 2 * (kind * steps + n)
                packed[k, 2 * j] = jnp.where(low, state, adjoint_turned)
                packed[k, 2 * j + 1] = jnp.where(low, state_turned, adjoint)
                packed[k + 1, 2 * j] = jnp.where(low, adjoint, state_turned)
                packed[k + 1, 2 * j + 1] = jnp.where(low, adjoint_turned, state)

    def weights(power):
        first = base + power * 4 * inputs
        return [
            jnp.where(low, weights_ref[first + 2 * k], weights_ref[first + 2 * k + 1]) for k in range(2 * inputs)
        ]

    def injected(factors, i):
        return tree_sum([factor * packed[k, i] for k, factor in enumerate(factors)])

    def advance(source, target, power, reach):
        aways = list(range(-reach, reach + 1))
        masks = [inside(away) for away in aways]
        factors = weights(power)

        def loaded(i):
            if i >= rows:
                return [zero for _ in aways]
            return [source[i, pl.ds((middle + away) * depth, depth), :] for away in aways]

        before = [zero for _ in aways]
        now = loaded(0)
        for i in range(rows):
            later = loaded(i + 1)
            for k, away in enumerate(aways):
                start = (middle + away) * depth
                above = source[i, pl.ds(shift + (start - 1), depth), :]
                below = source[i, pl.ds(shift + (start + 1), depth), :]
                value = (before[k] + later[k]) + beside(now[k], lane) + (above + below)
                if away:
                    value = value * masks[k]
                else:
                    value = value + injected(factors, i)
                target[i, pl.ds(start, depth), :] = value
            before, now = now, later

    even[...] = jnp.zeros_like(even)
    odd[...] = jnp.zeros_like(odd)
    factors = weights(powers - 1)
    for i in range(rows):
        even[i, pl.ds(middle * depth, depth), :] = injected(factors, i)
    buffers = (even, odd)
    done = 0
    while done < powers - 1:
        reach = min(done // depth + 1, slabs - 1)
        count = powers - 1 - done if reach == slabs - 1 else min(depth, powers - 1 - done)

        def twice(index, _):
            power = powers - 2 - done - 2 * index
            advance(buffers[0], buffers[1], power, reach)
            advance(buffers[1], buffers[0], power - 1, reach)
            return 0

        lax.fori_loop(0, count // 2, twice, 0)
        done += count
        if count % 2:
            advance(buffers[0], buffers[1], powers - 1 - done, reach)
            buffers = buffers[::-1]

    final = buffers[0]
    tiles = keep_ref.shape[2]
    bit = lax.rem(slab, 2)
    for half in range(slabs // 2):
        for ref, flag in ((keep_ref, bit), (send_ref, 1 - bit)):
            away = 2 * half + flag - slab
            planes = pl.ds(pl.multiple_of((middle + away) * depth, depth), depth)
            for j in range(columns):
                first, second = final[2 * j, planes, :], final[2 * j + 1, planes, :]
                for f, value in (
                    (0, jnp.where(low, first, swapped_halves(second))),
                    (1, jnp.where(low, swapped_halves(first), second)),
                ):
                    tile = f * columns + j
                    ref[half, tile // tiles, tile % tiles] = value


def vmem_call(kernel, out_shapes, smem_inputs, inputs, scratch=(), flops=10**6, space=pltpu.VMEM):
    smem = pl.BlockSpec(memory_space=pltpu.SMEM)
    vmem = pl.BlockSpec(memory_space=pltpu.VMEM)
    out_shape = tuple(jax.ShapeDtypeStruct(shape, jnp.float32) for shape in out_shapes)
    return pl.pallas_call(
        kernel,
        out_shape=out_shape,
        in_specs=[smem] * len(smem_inputs) + [pl.BlockSpec(memory_space=space)] * len(inputs),
        out_specs=(vmem,) * len(out_shape),
        scratch_shapes=list(scratch),
        compiler_params=pltpu.CompilerParams(vmem_limit_bytes=32 * 2**20),
        cost_estimate=pl.CostEstimate(flops=flops, bytes_accessed=2**20, transcendentals=0),
    )(*smem_inputs, *inputs)


def coarse_part(place, iterate, forcing):
    steps = iterate.shape[1]
    depth, cells = iterate.shape[2:]
    ranks, slabs = lax.axis_size("tm"), 2 * lax.axis_size("pair")
    table = coarse_polynomials(steps * ranks)
    powers = table.shape[-1]
    table = table.reshape(2, 2, ranks, steps, 2, powers)
    same = np.stack([table[:, 0, :, :, 0], table[:, 1, :, :, 1]], -1)
    other = np.stack([table[:, 1, :, :, 0], table[:, 0, :, :, 1]], -1)
    weights = np.stack([same, other], -2).transpose(1, 3, 0, 2, 4, 5).astype(np.float32)
    reach = min(-(-(powers - 1) // depth), slabs - 1)
    middle = max(reach + 1, slabs - 1)
    tiles = 2 * cells // LANES
    half = (slabs // 2, ranks, tiles // ranks, depth, LANES)
    buffer = pltpu.VMEM((cells // NY, (2 * middle + 1) * depth, LANES), jnp.float32)
    packed = pltpu.VMEM((4 * steps, cells // NY, depth, LANES), jnp.float32)
    return vmem_call(
        functools.partial(coarse_kernel, powers, steps, slabs, middle),
        (half, half),
        (place, jnp.asarray(weights.reshape(-1))),
        (iterate, forcing),
        (buffer, buffer, packed),
        flops=10**8,
    )


def relaxed(fields, around, before, after, source):
    diffusion, coupling, centre, along, across = level_terms(0)
    state, adjoint = fields
    defect_state = source[0] - (centre * state - diffusion * around[0] - before + coupling * adjoint)
    defect_adjoint = source[1] - (centre * adjoint - diffusion * around[1] - after - coupling * state)
    return (
        state + along * defect_state - across * defect_adjoint,
        adjoint + across * defect_state + along * defect_adjoint,
    )


def first_kernel(iterate_hbm, forcing_hbm, first_ref, up_ref, down_ref, iterate_ref, forcing_ref, arrived):
    steps, depth, cells = iterate_ref.shape[1:]
    copies = [
        pltpu.make_async_copy(source.at[f, n], target.at[f, n], arrived.at[kind, f, n])
        for kind, (source, target) in enumerate(((iterate_hbm, iterate_ref), (forcing_hbm, forcing_ref)))
        for f in range(2)
        for n in range(steps)
    ]
    for copy in copies:
        copy.start()
    for copy in copies:
        copy.wait()
    columns = cells // LANES
    lane, sublane = lane_index(depth), sublane_index(depth)
    low = lane < NY
    zero = jnp.zeros((depth, LANES), jnp.float32)
    slots = [(f, n) for f in range(2) for n in range(steps)]

    def loaded(j):
        return {s: iterate_ref[s[0], s[1], :, column(j)] if j < columns else zero for s in slots}

    now = loaded(0)
    pairs_before = now
    for j in range(columns):
        later = loaded(j + 1)
        pairs = {s: now[s] + later[s] for s in slots}
        around = {}
        for s in slots:
            across_rows = swapped_halves(jnp.where(low, pairs[s], pairs_before[s]))
            above = jnp.where(sublane == 0, 0.0, pltpu.roll(now[s], 1, 0))
            below = jnp.where(sublane == depth - 1, 0.0, pltpu.roll(now[s], depth - 1, 0))
            around[s] = across_rows + beside(now[s], lane) + (above + below)
        for n in range(steps):
            values = relaxed(
                (now[0, n], now[1, n]),
                (around[0, n], around[1, n]),
                now[0, n - 1] if n else zero,
                now[1, n + 1] if n < steps - 1 else zero,
                (forcing_ref[0, n, :, column(j)], forcing_ref[1, n, :, column(j)]),
            )
            for f in range(2):
                first_ref[f, n, :, column(j)] = values[f]
                slot = f * steps + n
                for ref, plane in ((up_ref, depth - 1), (down_ref, 0)):
                    ref[slot : slot + 1, column(j)] = now[f, n][plane : plane + 1]
                    slot_after = 2 * steps + slot
                    ref[slot_after : slot_after + 1, column(j)] = values[f][plane : plane + 1]
        now, pairs_before = later, pairs


def second_kernel(
    steps, slabs, place_ref, iterate_ref, first_ref, up_ref, down_ref, above_ref, below_ref, swept_ref, edge_ref, forth_ref, back_ref
):
    diffusion, _, _, along, across = level_terms(0)
    depth, cells = iterate_ref.shape[2:]
    columns = cells // LANES
    slab = place_ref[1]
    sublane = sublane_index(depth)
    count = 2 * steps
    has_above = jnp.where(slab > 0, 1.0, 0.0).astype(jnp.float32)
    has_below = jnp.where(slab < slabs - 1, 1.0, 0.0).astype(jnp.float32)

    def mixed(rows):
        state, adjoint = rows[:steps], rows[steps:]
        return jnp.concatenate(
            [
                (along * diffusion) * state - (across * diffusion) * adjoint,
                (across * diffusion) * state + (along * diffusion) * adjoint,
            ],
            0,
        )

    def one(j):
        return slice(j * LANES, (j + 1) * LANES)

    for j in range(columns):
        from_above, from_below = above_ref[:, one(j)], below_ref[:, one(j)]
        edge_ref[:count, one(j)] = (from_above[count:] + mixed(down_ref[:count, one(j)])) * has_above
        edge_ref[count:, one(j)] = (from_below[count:] + mixed(up_ref[:count, one(j)])) * has_below
        add_above, add_below = mixed(from_above[:count]), mixed(from_below[:count])
        for f in range(2):
            for n in range(steps):
                k = f * steps + n
                value = first_ref[f, n, :, one(j)]
                value = value + jnp.where(sublane == 0, add_above[k : k + 1], 0.0)
                value = value + jnp.where(sublane == depth - 1, add_below[k : k + 1], 0.0)
                swept_ref[f, n, :, one(j)] = value
                for ref, field, step in ((forth_ref, 0, steps - 1), (back_ref, 1, 0)):
                    if (f, n) == (field, step):
                        ref[j] = iterate_ref[f, n, :, one(j)]
                        ref[columns + j] = value
                        block, row = 2 * columns + j // depth, j % depth
                        ref[block, row : row + 1] = from_above[k : k + 1]
                        block += columns // depth
                        ref[block, row : row + 1] = from_below[k : k + 1]


def third_kernel(steps, ranks, place_ref, iterate_ref, forcing_ref, swept_ref, edge_ref, forth_ref, back_ref, out_ref):
    _, _, _, along, across = level_terms(0)
    depth, cells = iterate_ref.shape[2:]
    columns = cells // LANES
    rank = place_ref[0]
    lane, sublane = lane_index(depth), sublane_index(depth)
    low = lane < NY
    zero = jnp.zeros((depth, LANES), jnp.float32)
    slots = [(f, n) for f in range(2) for n in range(steps)]
    has_before = jnp.where(rank > 0, 1.0, 0.0).astype(jnp.float32)
    has_after = jnp.where(rank < ranks - 1, 1.0, 0.0).astype(jnp.float32)
    gain = {(0, 0): ("forth", along), (1, 0): ("forth", across), (0, steps - 1): ("back", -across), (1, steps - 1): ("back", along)}

    def loaded(j):
        if j >= columns:
            return {s: zero for s in slots}
        near = {"forth": forth_ref[j], "back": back_ref[j]}
        values = {}
        for s in slots:
            values[s] = swept_ref[s[0], s[1], :, column(j)]
            if s in gain:
                values[s] = values[s] + gain[s][1] * near[gain[s][0]]
        return values

    def edges(j, side):
        block, row = 2 * columns + side * (columns // depth) + j // depth, j % depth
        near = {"forth": forth_ref[block, row : row + 1], "back": back_ref[block, row : row + 1]}
        values = {}
        for s in slots:
            k = side * 2 * steps + s[0] * steps + s[1]
            values[s] = edge_ref[k : k + 1, column(j)]
            if s in gain:
                values[s] = values[s] + gain[s][1] * near[gain[s][0]]
        return values

    now = loaded(0)
    pairs_before = now
    for j in range(columns):
        later = loaded(j + 1)
        over, under = edges(j, 0), edges(j, 1)
        pairs = {s: now[s] + later[s] for s in slots}
        around = {}
        for s in slots:
            across_rows = swapped_halves(jnp.where(low, pairs[s], pairs_before[s]))
            above = jnp.where(sublane == 0, over[s], pltpu.roll(now[s], 1, 0))
            below = jnp.where(sublane == depth - 1, under[s], pltpu.roll(now[s], depth - 1, 0))
            around[s] = across_rows + beside(now[s], lane) + (above + below)
        before = (forth_ref[columns + j] - across * iterate_ref[1, 0, :, column(j)]) * has_before
        after = (back_ref[columns + j] + across * iterate_ref[0, steps - 1, :, column(j)]) * has_after
        for n in range(steps):
            values = relaxed(
                (now[0, n], now[1, n]),
                (around[0, n], around[1, n]),
                now[0, n - 1] if n else before,
                now[1, n + 1] if n < steps - 1 else after,
                (forcing_ref[0, n, :, column(j)], forcing_ref[1, n, :, column(j)]),
            )
            for f in range(2):
                out_ref[f, n, :, column(j)] = values[f]
        now, pairs_before = later, pairs


def shifted(value, axis, by):
    size = lax.axis_size(axis)
    return lax.ppermute(value, axis, [(i, i + by) for i in range(size) if 0 <= i + by < size])


def sum_kernel(parts_ref, copies_ref):
    tiles = copies_ref.shape[1]
    for tile in range(tiles):
        total = tree_sum([parts_ref[k, tile] for k in range(parts_ref.shape[0])])
        for k in range(copies_ref.shape[0]):
            copies_ref[k, tile] = total


def local(iterate, forcing):
    steps, depth, cells = iterate.shape[1:]
    columns = cells // LANES
    ranks, slabs = lax.axis_size("tm"), 2 * lax.axis_size("pair")
    place = jnp.stack([lax.axis_index("tm"), lax.axis_index(("pair", "core")), jnp.zeros((), jnp.int32)]).astype(jnp.int32)
    first, up, down = vmem_call(
        first_kernel,
        (iterate.shape, (4 * steps, cells), (4 * steps, cells)),
        (),
        [pltpu.with_memory_space_constraint(array, pltpu.HBM) for array in (iterate, forcing)],
        (
            pltpu.VMEM(iterate.shape, jnp.float32),
            pltpu.VMEM(forcing.shape, jnp.float32),
            pltpu.SemaphoreType.DMA((2, 2, steps)),
        ),
        space=pltpu.HBM,
    )
    up, down, later_place = lax.optimization_barrier((up, down, place))
    above = shifted(up, ("pair", "core"), 1)
    below = shifted(down, ("pair", "core"), -1)
    keep, send = coarse_part(later_place, iterate, forcing)
    send, above, below = lax.optimization_barrier((send, above, below))
    received = lax.ppermute(send, "core", [(0, 1), (1, 0)])

    payload = (2 * columns + 2 * columns // depth, depth, LANES)
    swept, edge, forth, back = vmem_call(
        functools.partial(second_kernel, steps, slabs),
        (iterate.shape, (4 * steps, cells), payload, payload),
        (place,),
        (iterate, first, up, down, above, below),
    )
    pairs, pair = lax.axis_size("pair"), lax.axis_index("pair")

    def half(array, index):
        return lax.dynamic_index_in_dim(array, index, 0, keepdims=False)

    total = None
    for mask in range(1, pairs):
        away = pair ^ mask
        other = half(keep, away) + half(received, away)
        if total is None:
            other, forth, back = lax.optimization_barrier((other, forth, back))
        term = lax.ppermute(other, "pair", [(i, i ^ mask) for i in range(pairs)])
        total = term if total is None else total + term
    own = half(keep, pair) + half(received, pair)
    forth = shifted(forth, "tm", 1)
    back = shifted(back, "tm", -1)
    total = own + total
    shape = total.shape
    parts = lax.all_to_all(total, "tm", 0, 0, tiled=True)
    (copies,) = vmem_call(sum_kernel, (shape,), (), (parts,))
    copies, forth, back = lax.optimization_barrier((copies, forth, back))
    coarse = lax.all_to_all(copies, "tm", 0, 0, tiled=True).reshape(2, columns, depth, LANES)
    coarse = coarse.transpose(0, 2, 1, 3).reshape(2, depth, cells)
    (smoothed,) = vmem_call(
        functools.partial(third_kernel, steps, ranks),
        (iterate.shape,),
        (place,),
        (iterate, forcing, swept, edge, forth, back),
    )
    return smoothed, jnp.broadcast_to(coarse[:, None], iterate.shape)


def solution(mesh):
    ranks, slabs = mesh.shape["tm"], mesh.shape["space"]
    fine = jax.sharding.Mesh(mesh.devices.reshape(ranks, slabs // 2, 2), ("tm", "pair", "core"))
    specs = P(None, "tm", ("pair", "core"), None)
    return jax.shard_map(local, mesh=fine, in_specs=(specs, specs), out_specs=(specs, specs), check_vma=False)
```

```python
import functools

import numpy as np

import jax
import jax.numpy as jnp
from jax import lax
from jax.experimental import pallas as pl
from jax.experimental.pallas import tpu as pltpu
from jax.sharding import PartitionSpec as P

NY = 64
LANES = 128

KAPPA_BASE = 0.25
COUPLING_BASE = 0.5
DAMPING = 0.6


def level_terms(level):
    diffusion = KAPPA_BASE * 2.0**level
    coupling = COUPLING_BASE * 2.0**level
    centre = 1.0 + 6.0 * diffusion
    determinant = centre * centre + coupling * coupling
    along = DAMPING * centre / determinant
    across = DAMPING * coupling / determinant
    return diffusion, coupling, centre, along, across


def coarse_polynomials(total_steps):
    levels = total_steps.bit_length()
    powers = 2 * levels + 1
    unit = np.eye(4 * total_steps).reshape(-1, 2, 2, total_steps)
    fields = np.zeros((4 * total_steps, 2, total_steps, powers))
    source = np.zeros_like(fields)
    fields[..., 0] = unit[:, 0]
    source[..., 0] = unit[:, 1]

    def image(values, diffusion, coupling, centre):
        out = centre * values
        out[..., 1:] -= diffusion * values[..., :-1]
        out[:, 0, 1:] -= values[:, 0, :-1]
        out[:, 1, :-1] -= values[:, 1, 1:]
        out[:, 0] += coupling * values[:, 1]
        out[:, 1] -= coupling * values[:, 0]
        return out

    for level in range(levels):
        diffusion, coupling, centre, along, across = level_terms(level)
        for _ in range(2):
            defect = source - image(fields, diffusion, coupling, centre)
            state, adjoint = defect[:, 0], defect[:, 1]
            fields = fields + np.stack([along * state - across * adjoint, across * state + along * adjoint], 1)
        if level < levels - 1:
            defect = source - image(fields, diffusion, coupling, centre)
            source = defect[:, :, 0::2] + defect[:, :, 1::2]
            fields = np.zeros_like(source)
    return fields[:, :, 0].reshape(2, 2, total_steps, 2, powers)


def lane_index(depth):
    return lax.broadcasted_iota(jnp.int32, (depth, LANES), 1)


def sublane_index(depth):
    return lax.broadcasted_iota(jnp.int32, (depth, LANES), 0)


def column(j):
    return pl.ds(j * LANES, LANES)


def swapped_halves(value):
    return pltpu.roll(value, NY, 1)


def beside(value, lane):
    left = pltpu.roll(jnp.where((lane % NY) != NY - 1, value, 0.0), 1, 1)
    right = pltpu.roll(jnp.where((lane % NY) != 0, value, 0.0), LANES - 1, 1)
    return left + right


def tree_sum(terms):
    while len(terms) > 1:
        terms = [sum(terms[k : k + 2]) for k in range(0, len(terms), 2)]
    return terms[0]


def coarse_kernel(
    powers, steps, slabs, middle, place_ref, weights_ref, iterate_hbm, forcing_hbm, keep_ref, send_ref, even, odd, packed, iterate_ref, forcing_ref, arrived
):
    copies = {
        (kind, f, n): pltpu.make_async_copy(source.at[f, n], target.at[f, n], arrived.at[kind, f, n])
        for kind, (source, target) in enumerate(((iterate_hbm, iterate_ref), (forcing_hbm, forcing_ref)))
        for n in range(steps)
        for f in range(2)
    }
    for copy in copies.values():
        copy.start()
    even[...] = jnp.zeros_like(even)
    odd[...] = jnp.zeros_like(odd)
    depth, cells = iterate_ref.shape[2:]
    columns = cells // LANES
    rows = cells // NY
    inputs = 2 * steps
    slab, shift = place_ref[1], place_ref[2]
    base = place_ref[0] * (powers * 4 * inputs)
    lane = lane_index(depth)
    low = lane < NY
    zero = jnp.zeros((depth, LANES), jnp.float32)

    def inside(away):
        at = slab + away
        return jnp.where((at >= 0) & (at < slabs), 1.0, 0.0).astype(jnp.float32)

    for kind, ref in enumerate((iterate_ref, forcing_ref)):
        for n in range(steps):
            copies[kind, 0, n].wait()
            copies[kind, 1, n].wait()
            for j in range(columns):
                state, adjoint = ref[0, n, :, column(j)], ref[1, n, :, column(j)]
                state_turned, adjoint_turned = swapped_halves(state), swapped_halves(adjoint)
                k = 2 * (kind * steps + n)
                packed[k, 2 * j] = jnp.where(low, state, adjoint_turned)
                packed[k, 2 * j + 1] = jnp.where(low, state_turned, adjoint)
                packed[k + 1, 2 * j] = jnp.where(low, adjoint, state_turned)
                packed[k + 1, 2 * j + 1] = jnp.where(low, adjoint_turned, state)

    def weights(power):
        first = base + power * 4 * inputs
        return [
            jnp.where(low, weights_ref[first + 2 * k], weights_ref[first + 2 * k + 1]) for k in range(2 * inputs)
        ]

    def injected(factors, i):
        return tree_sum([factor * packed[k, i] for k, factor in enumerate(factors)])

    def advance(source, target, power, reach):
        aways = list(range(-reach, reach + 1))
        masks = [inside(away) for away in aways]
        factors = weights(power)

        def loaded(i):
            if i >= rows:
                return [zero for _ in aways]
            return [source[i, pl.ds((middle + away) * depth, depth), :] for away in aways]

        before = [zero for _ in aways]
        now = loaded(0)
        for i in range(rows):
            later = loaded(i + 1)
            for k, away in enumerate(aways):
                start = (middle + away) * depth
                above = source[i, pl.ds(shift + (start - 1), depth), :]
                below = source[i, pl.ds(shift + (start + 1), depth), :]
                value = (before[k] + later[k]) + beside(now[k], lane) + (above + below)
                if away:
                    value = value * masks[k]
                else:
                    value = value + injected(factors, i)
                target[i, pl.ds(start, depth), :] = value
            before, now = now, later

    factors = weights(powers - 1)
    for i in range(rows):
        even[i, pl.ds(middle * depth, depth), :] = injected(factors, i)
    buffers = (even, odd)
    done = 0
    while done < powers - 1:
        reach = min(done // depth + 1, slabs - 1)
        count = powers - 1 - done if reach == slabs - 1 else min(depth, powers - 1 - done)

        def twice(index, _):
            power = powers - 2 - done - 2 * index
            advance(buffers[0], buffers[1], power, reach)
            advance(buffers[1], buffers[0], power - 1, reach)
            return 0

        lax.fori_loop(0, count // 2, twice, 0)
        done += count
        if count % 2:
            advance(buffers[0], buffers[1], powers - 1 - done, reach)
            buffers = buffers[::-1]

    final = buffers[0]
    tiles = keep_ref.shape[2]
    bit = lax.rem(slab, 2)
    for half in range(slabs // 2):
        for ref, flag in ((keep_ref, bit), (send_ref, 1 - bit)):
            away = 2 * half + flag - slab
            planes = pl.ds(pl.multiple_of((middle + away) * depth, depth), depth)
            for j in range(columns):
                first, second = final[2 * j, planes, :], final[2 * j + 1, planes, :]
                for f, value in (
                    (0, jnp.where(low, first, swapped_halves(second))),
                    (1, jnp.where(low, swapped_halves(first), second)),
                ):
                    tile = f * columns + j
                    ref[half, tile // tiles, tile % tiles] = value


def vmem_call(kernel, out_shapes, smem_inputs, inputs, scratch=(), flops=10**6, space=pltpu.VMEM, limit=6):
    smem = pl.BlockSpec(memory_space=pltpu.SMEM)
    vmem = pl.BlockSpec(memory_space=pltpu.VMEM)
    out_shape = tuple(jax.ShapeDtypeStruct(shape, jnp.float32) for shape in out_shapes)
    return pl.pallas_call(
        kernel,
        out_shape=out_shape,
        in_specs=[smem] * len(smem_inputs) + [pl.BlockSpec(memory_space=space)] * len(inputs),
        out_specs=(vmem,) * len(out_shape),
        scratch_shapes=list(scratch),
        compiler_params=pltpu.CompilerParams(vmem_limit_bytes=limit * 2**20),
        cost_estimate=pl.CostEstimate(flops=flops, bytes_accessed=2**20, transcendentals=0),
    )(*smem_inputs, *inputs)


def coarse_part(place, iterate, forcing):
    steps = iterate.shape[1]
    depth, cells = iterate.shape[2:]
    ranks, slabs = lax.axis_size("tm"), 2 * lax.axis_size("pair")
    table = coarse_polynomials(steps * ranks)
    powers = table.shape[-1]
    table = table.reshape(2, 2, ranks, steps, 2, powers)
    same = np.stack([table[:, 0, :, :, 0], table[:, 1, :, :, 1]], -1)
    other = np.stack([table[:, 1, :, :, 0], table[:, 0, :, :, 1]], -1)
    weights = np.stack([same, other], -2).transpose(1, 3, 0, 2, 4, 5).astype(np.float32)
    reach = min(-(-(powers - 1) // depth), slabs - 1)
    middle = max(reach + 1, slabs - 1)
    tiles = 2 * cells // LANES
    half = (slabs // 2, ranks, tiles // ranks, depth, LANES)
    buffer = pltpu.VMEM((cells // NY, (2 * middle + 1) * depth, LANES), jnp.float32)
    packed = pltpu.VMEM((4 * steps, cells // NY, depth, LANES), jnp.float32)
    return vmem_call(
        functools.partial(coarse_kernel, powers, steps, slabs, middle),
        (half, half),
        (place, jnp.asarray(weights.reshape(-1))),
        [pltpu.with_memory_space_constraint(array, pltpu.HBM) for array in (iterate, forcing)],
        (
            buffer,
            buffer,
            packed,
            pltpu.VMEM(iterate.shape, jnp.float32),
            pltpu.VMEM(forcing.shape, jnp.float32),
            pltpu.SemaphoreType.DMA((2, 2, steps)),
        ),
        flops=10**8,
        space=pltpu.HBM,
        limit=12,
    )


def relaxed(fields, around, before, after, source):
    diffusion, coupling, centre, along, across = level_terms(0)
    state, adjoint = fields
    defect_state = source[0] - (centre * state - diffusion * around[0] - before + coupling * adjoint)
    defect_adjoint = source[1] - (centre * adjoint - diffusion * around[1] - after - coupling * state)
    return (
        state + along * defect_state - across * defect_adjoint,
        adjoint + across * defect_state + along * defect_adjoint,
    )


def first_kernel(iterate_ref, forcing_ref, first_ref, up_ref, down_ref):
    steps, depth, cells = iterate_ref.shape[1:]
    columns = cells // LANES
    lane, sublane = lane_index(depth), sublane_index(depth)
    low = lane < NY
    zero = jnp.zeros((depth, LANES), jnp.float32)
    slots = [(f, n) for f in range(2) for n in range(steps)]

    def loaded(j):
        return {s: iterate_ref[s[0], s[1], :, column(j)] if j < columns else zero for s in slots}

    now = loaded(0)
    pairs_before = now
    for j in range(columns):
        later = loaded(j + 1)
        pairs = {s: now[s] + later[s] for s in slots}
        around = {}
        for s in slots:
            across_rows = swapped_halves(jnp.where(low, pairs[s], pairs_before[s]))
            above = jnp.where(sublane == 0, 0.0, pltpu.roll(now[s], 1, 0))
            below = jnp.where(sublane == depth - 1, 0.0, pltpu.roll(now[s], depth - 1, 0))
            around[s] = across_rows + beside(now[s], lane) + (above + below)
        for n in range(steps):
            values = relaxed(
                (now[0, n], now[1, n]),
                (around[0, n], around[1, n]),
                now[0, n - 1] if n else zero,
                now[1, n + 1] if n < steps - 1 else zero,
                (forcing_ref[0, n, :, column(j)], forcing_ref[1, n, :, column(j)]),
            )
            for f in range(2):
                first_ref[f, n, :, column(j)] = values[f]
                slot = f * steps + n
                for ref, plane in ((up_ref, depth - 1), (down_ref, 0)):
                    ref[slot : slot + 1, column(j)] = now[f, n][plane : plane + 1]
                    slot_after = 2 * steps + slot
                    ref[slot_after : slot_after + 1, column(j)] = values[f][plane : plane + 1]
        now, pairs_before = later, pairs


def second_kernel(
    steps, slabs, place_ref, iterate_ref, first_ref, up_ref, down_ref, above_ref, below_ref, swept_ref, edge_ref, forth_ref, back_ref
):
    diffusion, _, _, along, across = level_terms(0)
    depth, cells = iterate_ref.shape[2:]
    columns = cells // LANES
    slab = place_ref[1]
    sublane = sublane_index(depth)
    count = 2 * steps
    has_above = jnp.where(slab > 0, 1.0, 0.0).astype(jnp.float32)
    has_below = jnp.where(slab < slabs - 1, 1.0, 0.0).astype(jnp.float32)

    def mixed(rows):
        state, adjoint = rows[:steps], rows[steps:]
        return jnp.concatenate(
            [
                (along * diffusion) * state - (across * diffusion) * adjoint,
                (across * diffusion) * state + (along * diffusion) * adjoint,
            ],
            0,
        )

    def one(j):
        return slice(j * LANES, (j + 1) * LANES)

    for j in range(columns):
        from_above, from_below = above_ref[:, one(j)], below_ref[:, one(j)]
        edge_ref[:count, one(j)] = (from_above[count:] + mixed(down_ref[:count, one(j)])) * has_above
        edge_ref[count:, one(j)] = (from_below[count:] + mixed(up_ref[:count, one(j)])) * has_below
        add_above, add_below = mixed(from_above[:count]), mixed(from_below[:count])
        for f in range(2):
            for n in range(steps):
                k = f * steps + n
                value = first_ref[f, n, :, one(j)]
                value = value + jnp.where(sublane == 0, add_above[k : k + 1], 0.0)
                value = value + jnp.where(sublane == depth - 1, add_below[k : k + 1], 0.0)
                swept_ref[f, n, :, one(j)] = value
                for ref, field, step in ((forth_ref, 0, steps - 1), (back_ref, 1, 0)):
                    if (f, n) == (field, step):
                        ref[j] = iterate_ref[f, n, :, one(j)]
                        ref[columns + j] = value
                        block, row = 2 * columns + j // depth, j % depth
                        ref[block, row : row + 1] = from_above[k : k + 1]
                        block += columns // depth
                        ref[block, row : row + 1] = from_below[k : k + 1]


def third_kernel(steps, ranks, place_ref, iterate_ref, forcing_ref, swept_ref, edge_ref, forth_ref, back_ref, out_ref):
    _, _, _, along, across = level_terms(0)
    depth, cells = iterate_ref.shape[2:]
    columns = cells // LANES
    rank = place_ref[0]
    lane, sublane = lane_index(depth), sublane_index(depth)
    low = lane < NY
    zero = jnp.zeros((depth, LANES), jnp.float32)
    slots = [(f, n) for f in range(2) for n in range(steps)]
    has_before = jnp.where(rank > 0, 1.0, 0.0).astype(jnp.float32)
    has_after = jnp.where(rank < ranks - 1, 1.0, 0.0).astype(jnp.float32)
    gain = {(0, 0): ("forth", along), (1, 0): ("forth", across), (0, steps - 1): ("back", -across), (1, steps - 1): ("back", along)}

    def loaded(j):
        if j >= columns:
            return {s: zero for s in slots}
        near = {"forth": forth_ref[j], "back": back_ref[j]}
        values = {}
        for s in slots:
            values[s] = swept_ref[s[0], s[1], :, column(j)]
            if s in gain:
                values[s] = values[s] + gain[s][1] * near[gain[s][0]]
        return values

    def edges(j, side):
        block, row = 2 * columns + side * (columns // depth) + j // depth, j % depth
        near = {"forth": forth_ref[block, row : row + 1], "back": back_ref[block, row : row + 1]}
        values = {}
        for s in slots:
            k = side * 2 * steps + s[0] * steps + s[1]
            values[s] = edge_ref[k : k + 1, column(j)]
            if s in gain:
                values[s] = values[s] + gain[s][1] * near[gain[s][0]]
        return values

    now = loaded(0)
    pairs_before = now
    for j in range(columns):
        later = loaded(j + 1)
        over, under = edges(j, 0), edges(j, 1)
        pairs = {s: now[s] + later[s] for s in slots}
        around = {}
        for s in slots:
            across_rows = swapped_halves(jnp.where(low, pairs[s], pairs_before[s]))
            above = jnp.where(sublane == 0, over[s], pltpu.roll(now[s], 1, 0))
            below = jnp.where(sublane == depth - 1, under[s], pltpu.roll(now[s], depth - 1, 0))
            around[s] = across_rows + beside(now[s], lane) + (above + below)
        before = (forth_ref[columns + j] - across * iterate_ref[1, 0, :, column(j)]) * has_before
        after = (back_ref[columns + j] + across * iterate_ref[0, steps - 1, :, column(j)]) * has_after
        for n in range(steps):
            values = relaxed(
                (now[0, n], now[1, n]),
                (around[0, n], around[1, n]),
                now[0, n - 1] if n else before,
                now[1, n + 1] if n < steps - 1 else after,
                (forcing_ref[0, n, :, column(j)], forcing_ref[1, n, :, column(j)]),
            )
            for f in range(2):
                out_ref[f, n, :, column(j)] = values[f]
        now, pairs_before = later, pairs


def shifted(value, axis, by):
    size = lax.axis_size(axis)
    return lax.ppermute(value, axis, [(i, i + by) for i in range(size) if 0 <= i + by < size])


def sum_kernel(parts_ref, copies_ref):
    tiles = copies_ref.shape[1]
    for tile in range(tiles):
        total = tree_sum([parts_ref[k, tile] for k in range(parts_ref.shape[0])])
        for k in range(copies_ref.shape[0]):
            copies_ref[k, tile] = total


def local(iterate, forcing):
    steps, depth, cells = iterate.shape[1:]
    columns = cells // LANES
    ranks, slabs = lax.axis_size("tm"), 2 * lax.axis_size("pair")
    place = jnp.stack([lax.axis_index("tm"), lax.axis_index(("pair", "core")), jnp.zeros((), jnp.int32)]).astype(jnp.int32)
    keep, send = coarse_part(place, iterate, forcing)
    received = lax.ppermute(send, "core", [(0, 1), (1, 0)])

    keep, iterate_after, forcing_after = lax.optimization_barrier((keep, iterate, forcing))
    first, up, down = vmem_call(
        first_kernel, (iterate.shape, (4 * steps, cells), (4 * steps, cells)), (), (iterate_after, forcing_after)
    )
    pairs, pair = lax.axis_size("pair"), lax.axis_index("pair")

    def half(array, index):
        return lax.dynamic_index_in_dim(array, index, 0, keepdims=False)

    total = None
    for mask in range(1, pairs):
        away = pair ^ mask
        other = half(keep, away) + half(received, away)
        if total is None:
            other, up, down = lax.optimization_barrier((other, up, down))
            above = shifted(up, ("pair", "core"), 1)
            below = shifted(down, ("pair", "core"), -1)
        term = lax.ppermute(other, "pair", [(i, i ^ mask) for i in range(pairs)])
        total = term if total is None else total + term
    own = half(keep, pair) + half(received, pair)
    total = own + total
    total, above, below = lax.optimization_barrier((total, above, below))
    payload = (2 * columns + 2 * columns // depth, depth, LANES)
    swept, edge, forth, back = vmem_call(
        functools.partial(second_kernel, steps, slabs),
        (iterate.shape, (4 * steps, cells), payload, payload),
        (place,),
        (iterate, first, up, down, above, below),
    )
    shape = total.shape
    parts = lax.all_to_all(total, "tm", 0, 0, tiled=True)
    (copies,) = vmem_call(sum_kernel, (shape,), (), (parts,))
    copies, _, _ = lax.optimization_barrier((copies, forth, back))
    forth = shifted(forth, "tm", 1)
    back = shifted(back, "tm", -1)
    coarse = lax.all_to_all(copies, "tm", 0, 0, tiled=True).reshape(2, columns, depth, LANES)
    coarse = coarse.transpose(0, 2, 1, 3).reshape(2, depth, cells)
    (smoothed,) = vmem_call(
        functools.partial(third_kernel, steps, ranks),
        (iterate.shape,),
        (place,),
        (iterate, forcing, swept, edge, forth, back),
    )
    return smoothed, jnp.broadcast_to(coarse[:, None], iterate.shape)


def solution(mesh):
    ranks, slabs = mesh.shape["tm"], mesh.shape["space"]
    fine = jax.sharding.Mesh(mesh.devices.reshape(ranks, slabs // 2, 2), ("tm", "pair", "core"))
    specs = P(None, "tm", ("pair", "core"), None)
    return jax.shard_map(local, mesh=fine, in_specs=(specs, specs), out_specs=(specs, specs), check_vma=False)
```

```python
import functools

import numpy as np

import jax
import jax.numpy as jnp
from jax import lax
from jax.experimental import pallas as pl
from jax.experimental.pallas import tpu as pltpu
from jax.sharding import PartitionSpec as P

NY = 64
LANES = 128

KAPPA_BASE = 0.25
COUPLING_BASE = 0.5
DAMPING = 0.6


def level_terms(level):
    diffusion = KAPPA_BASE * 2.0**level
    coupling = COUPLING_BASE * 2.0**level
    centre = 1.0 + 6.0 * diffusion
    determinant = centre * centre + coupling * coupling
    along = DAMPING * centre / determinant
    across = DAMPING * coupling / determinant
    return diffusion, coupling, centre, along, across


def coarse_polynomials(total_steps):
    levels = total_steps.bit_length()
    powers = 2 * levels + 1
    unit = np.eye(4 * total_steps).reshape(-1, 2, 2, total_steps)
    fields = np.zeros((4 * total_steps, 2, total_steps, powers))
    source = np.zeros_like(fields)
    fields[..., 0] = unit[:, 0]
    source[..., 0] = unit[:, 1]

    def image(values, diffusion, coupling, centre):
        out = centre * values
        out[..., 1:] -= diffusion * values[..., :-1]
        out[:, 0, 1:] -= values[:, 0, :-1]
        out[:, 1, :-1] -= values[:, 1, 1:]
        out[:, 0] += coupling * values[:, 1]
        out[:, 1] -= coupling * values[:, 0]
        return out

    for level in range(levels):
        diffusion, coupling, centre, along, across = level_terms(level)
        for _ in range(2):
            defect = source - image(fields, diffusion, coupling, centre)
            state, adjoint = defect[:, 0], defect[:, 1]
            fields = fields + np.stack([along * state - across * adjoint, across * state + along * adjoint], 1)
        if level < levels - 1:
            defect = source - image(fields, diffusion, coupling, centre)
            source = defect[:, :, 0::2] + defect[:, :, 1::2]
            fields = np.zeros_like(source)
    return fields[:, :, 0].reshape(2, 2, total_steps, 2, powers)


def lane_index(depth):
    return lax.broadcasted_iota(jnp.int32, (depth, LANES), 1)


def sublane_index(depth):
    return lax.broadcasted_iota(jnp.int32, (depth, LANES), 0)


def column(j):
    return pl.ds(j * LANES, LANES)


def swapped_halves(value):
    return pltpu.roll(value, NY, 1)


def beside(value, lane):
    left = pltpu.roll(jnp.where((lane % NY) != NY - 1, value, 0.0), 1, 1)
    right = pltpu.roll(jnp.where((lane % NY) != 0, value, 0.0), LANES - 1, 1)
    return left + right


def tree_sum(terms):
    while len(terms) > 1:
        terms = [sum(terms[k : k + 2]) for k in range(0, len(terms), 2)]
    return terms[0]


def coarse_kernel(
    powers, steps, slabs, middle, place_ref, weights_hbm, iterate_hbm, forcing_hbm, keep_ref, send_ref, even, odd, packed, iterate_ref, forcing_ref, weights_ref, arrived, weighed
):
    copies = {
        (kind, f, n): pltpu.make_async_copy(source.at[f, n], target.at[f, n], arrived.at[kind, f, n])
        for kind, (source, target) in enumerate(((iterate_hbm, iterate_ref), (forcing_hbm, forcing_ref)))
        for n in range(steps)
        for f in range(2)
    }
    weighing = pltpu.make_async_copy(weights_hbm.at[place_ref[0]], weights_ref, weighed)
    for copy in copies.values():
        copy.start()
    weighing.start()
    even[...] = jnp.zeros_like(even)
    odd[...] = jnp.zeros_like(odd)
    depth, cells = iterate_ref.shape[2:]
    columns = cells // LANES
    rows = cells // NY
    inputs = 2 * steps
    slab, shift = place_ref[1], place_ref[2]
    lane = lane_index(depth)
    low = lane < NY
    zero = jnp.zeros((depth, LANES), jnp.float32)

    def inside(away):
        at = slab + away
        return jnp.where((at >= 0) & (at < slabs), 1.0, 0.0).astype(jnp.float32)

    for kind, ref in enumerate((iterate_ref, forcing_ref)):
        for n in range(steps):
            copies[kind, 0, n].wait()
            copies[kind, 1, n].wait()
            for j in range(columns):
                state, adjoint = ref[0, n, :, column(j)], ref[1, n, :, column(j)]
                state_turned, adjoint_turned = swapped_halves(state), swapped_halves(adjoint)
                k = 2 * (kind * steps + n)
                packed[k, 2 * j] = jnp.where(low, state, adjoint_turned)
                packed[k, 2 * j + 1] = jnp.where(low, state_turned, adjoint)
                packed[k + 1, 2 * j] = jnp.where(low, adjoint, state_turned)
                packed[k + 1, 2 * j + 1] = jnp.where(low, adjoint_turned, state)

    def weights(power):
        return [
            jnp.broadcast_to(weights_ref[pl.ds(power * 2 * inputs + k, 1), :], (depth, LANES)) for k in range(2 * inputs)
        ]

    def injected(factors, i):
        return tree_sum([factor * packed[k, i] for k, factor in enumerate(factors)])

    def advance(source, target, power, reach):
        aways = list(range(-reach, reach + 1))
        masks = [inside(away) for away in aways]
        factors = weights(power)

        def loaded(i):
            if i >= rows:
                return [zero for _ in aways]
            return [source[i, pl.ds((middle + away) * depth, depth), :] for away in aways]

        before = [zero for _ in aways]
        now = loaded(0)
        for i in range(rows):
            later = loaded(i + 1)
            for k, away in enumerate(aways):
                start = (middle + away) * depth
                above = source[i, pl.ds(shift + (start - 1), depth), :]
                below = source[i, pl.ds(shift + (start + 1), depth), :]
                value = (before[k] + later[k]) + beside(now[k], lane) + (above + below)
                if away:
                    value = value * masks[k]
                else:
                    value = value + injected(factors, i)
                target[i, pl.ds(start, depth), :] = value
            before, now = now, later

    weighing.wait()
    factors = weights(powers - 1)
    for i in range(rows):
        even[i, pl.ds(middle * depth, depth), :] = injected(factors, i)
    buffers = (even, odd)
    done = 0
    while done < powers - 1:
        reach = min(done // depth + 1, slabs - 1)
        count = powers - 1 - done if reach == slabs - 1 else min(depth, powers - 1 - done)

        def twice(index, _):
            power = powers - 2 - done - 2 * index
            advance(buffers[0], buffers[1], power, reach)
            advance(buffers[1], buffers[0], power - 1, reach)
            return 0

        lax.fori_loop(0, count // 2, twice, 0)
        done += count
        if count % 2:
            advance(buffers[0], buffers[1], powers - 1 - done, reach)
            buffers = buffers[::-1]

    final = buffers[0]
    bit = lax.rem(slab, 2)
    for half in range(slabs // 2):
        for ref, flag in ((keep_ref, bit), (send_ref, 1 - bit)):
            away = 2 * half + flag - slab
            planes = pl.ds(pl.multiple_of((middle + away) * depth, depth), depth)
            for j in range(columns):
                first, second = final[2 * j, planes, :], final[2 * j + 1, planes, :]
                for f, value in (
                    (0, jnp.where(low, first, swapped_halves(second))),
                    (1, jnp.where(low, swapped_halves(first), second)),
                ):
                    ref[half, f, j] = value


def vmem_call(kernel, out_shapes, smem_inputs, inputs, scratch=(), spaces=None, limit=6, cost=2**20):
    smem = pl.BlockSpec(memory_space=pltpu.SMEM)
    vmem = pl.BlockSpec(memory_space=pltpu.VMEM)
    out_shape = tuple(jax.ShapeDtypeStruct(shape, jnp.float32) for shape in out_shapes)
    return pl.pallas_call(
        kernel,
        out_shape=out_shape,
        in_specs=[smem] * len(smem_inputs) + [pl.BlockSpec(memory_space=space) for space in spaces or [pltpu.VMEM] * len(inputs)],
        out_specs=(vmem,) * len(out_shape),
        scratch_shapes=list(scratch),
        compiler_params=pltpu.CompilerParams(vmem_limit_bytes=limit * 2**20),
        cost_estimate=pl.CostEstimate(flops=10**6, bytes_accessed=cost, transcendentals=0),
    )(*smem_inputs, *inputs)


def coarse_part(place, iterate, forcing):
    steps = iterate.shape[1]
    depth, cells = iterate.shape[2:]
    ranks, slabs = lax.axis_size("tm"), 2 * lax.axis_size("pair")
    table = coarse_polynomials(steps * ranks)
    powers = table.shape[-1]
    table = table.reshape(2, 2, ranks, steps, 2, powers)
    same = np.stack([table[:, 0, :, :, 0], table[:, 1, :, :, 1]], -1)
    other = np.stack([table[:, 1, :, :, 0], table[:, 0, :, :, 1]], -1)
    weights = np.stack([same, other], -2).transpose(1, 3, 0, 2, 4, 5).astype(np.float32)
    reach = min(-(-(powers - 1) // depth), slabs - 1)
    middle = max(reach + 1, slabs - 1)
    weights = np.repeat(weights.reshape(ranks, -1, 2), NY, -1)
    half = (slabs // 2, 2, cells // LANES, depth, LANES)
    buffer = pltpu.VMEM((cells // NY, (2 * middle + 1) * depth, LANES), jnp.float32)
    packed = pltpu.VMEM((4 * steps, cells // NY, depth, LANES), jnp.float32)
    return vmem_call(
        functools.partial(coarse_kernel, powers, steps, slabs, middle),
        (half, half),
        (place,),
        [pltpu.with_memory_space_constraint(array, pltpu.HBM) for array in (jnp.asarray(weights), iterate, forcing)],
        (
            buffer,
            buffer,
            packed,
            pltpu.VMEM(iterate.shape, jnp.float32),
            pltpu.VMEM(forcing.shape, jnp.float32),
            pltpu.VMEM(weights.shape[1:], jnp.float32),
            pltpu.SemaphoreType.DMA((2, 2, steps)),
            pltpu.SemaphoreType.DMA,
        ),
        spaces=(pltpu.HBM,) * 3,
        limit=12,
        cost=24 * 2**20,
    )


def relaxed(fields, around, before, after, source):
    diffusion, coupling, centre, along, across = level_terms(0)
    state, adjoint = fields
    defect_state = source[0] - (centre * state - diffusion * around[0] - before + coupling * adjoint)
    defect_adjoint = source[1] - (centre * adjoint - diffusion * around[1] - after - coupling * state)
    return (
        state + along * defect_state - across * defect_adjoint,
        adjoint + across * defect_state + along * defect_adjoint,
    )


def first_kernel(iterate_ref, forcing_ref, first_ref, up_ref, down_ref):
    steps, depth, cells = iterate_ref.shape[1:]
    columns = cells // LANES
    lane, sublane = lane_index(depth), sublane_index(depth)
    low = lane < NY
    zero = jnp.zeros((depth, LANES), jnp.float32)
    slots = [(f, n) for f in range(2) for n in range(steps)]

    def loaded(j):
        return {s: iterate_ref[s[0], s[1], :, column(j)] if j < columns else zero for s in slots}

    now = loaded(0)
    pairs_before = now
    for j in range(columns):
        later = loaded(j + 1)
        pairs = {s: now[s] + later[s] for s in slots}
        around = {}
        for s in slots:
            across_rows = swapped_halves(jnp.where(low, pairs[s], pairs_before[s]))
            above = jnp.where(sublane == 0, 0.0, pltpu.roll(now[s], 1, 0))
            below = jnp.where(sublane == depth - 1, 0.0, pltpu.roll(now[s], depth - 1, 0))
            around[s] = across_rows + beside(now[s], lane) + (above + below)
        for n in range(steps):
            values = relaxed(
                (now[0, n], now[1, n]),
                (around[0, n], around[1, n]),
                now[0, n - 1] if n else zero,
                now[1, n + 1] if n < steps - 1 else zero,
                (forcing_ref[0, n, :, column(j)], forcing_ref[1, n, :, column(j)]),
            )
            for f in range(2):
                first_ref[f, n, :, column(j)] = values[f]
                slot = f * steps + n
                for ref, plane in ((up_ref, depth - 1), (down_ref, 0)):
                    ref[slot : slot + 1, column(j)] = now[f, n][plane : plane + 1]
                    slot_after = 2 * steps + slot
                    ref[slot_after : slot_after + 1, column(j)] = values[f][plane : plane + 1]
        now, pairs_before = later, pairs


def second_kernel(
    steps, slabs, place_ref, iterate_ref, first_ref, up_ref, down_ref, above_ref, below_ref, swept_ref, edge_ref, forth_ref, back_ref
):
    diffusion, _, _, along, across = level_terms(0)
    depth, cells = iterate_ref.shape[2:]
    columns = cells // LANES
    slab = place_ref[1]
    sublane = sublane_index(depth)
    count = 2 * steps
    has_above = jnp.where(slab > 0, 1.0, 0.0).astype(jnp.float32)
    has_below = jnp.where(slab < slabs - 1, 1.0, 0.0).astype(jnp.float32)

    def mixed(rows):
        state, adjoint = rows[:steps], rows[steps:]
        return jnp.concatenate(
            [
                (along * diffusion) * state - (across * diffusion) * adjoint,
                (across * diffusion) * state + (along * diffusion) * adjoint,
            ],
            0,
        )

    def one(j):
        return slice(j * LANES, (j + 1) * LANES)

    for j in range(columns):
        from_above, from_below = above_ref[:, one(j)], below_ref[:, one(j)]
        edge_ref[:count, one(j)] = (from_above[count:] + mixed(down_ref[:count, one(j)])) * has_above
        edge_ref[count:, one(j)] = (from_below[count:] + mixed(up_ref[:count, one(j)])) * has_below
        add_above, add_below = mixed(from_above[:count]), mixed(from_below[:count])
        for f in range(2):
            for n in range(steps):
                k = f * steps + n
                value = first_ref[f, n, :, one(j)]
                value = value + jnp.where(sublane == 0, add_above[k : k + 1], 0.0)
                value = value + jnp.where(sublane == depth - 1, add_below[k : k + 1], 0.0)
                swept_ref[f, n, :, one(j)] = value
                for ref, field, step in ((forth_ref, 0, steps - 1), (back_ref, 1, 0)):
                    if (f, n) == (field, step):
                        ref[j] = iterate_ref[f, n, :, one(j)]
                        ref[columns + j] = value
                        block, row = 2 * columns + j // depth, j % depth
                        ref[block, row : row + 1] = from_above[k : k + 1]
                        block += columns // depth
                        ref[block, row : row + 1] = from_below[k : k + 1]


def third_kernel(steps, ranks, place_ref, iterate_ref, forcing_ref, swept_ref, edge_ref, forth_ref, back_ref, out_ref):
    _, _, _, along, across = level_terms(0)
    depth, cells = iterate_ref.shape[2:]
    columns = cells // LANES
    rank = place_ref[0]
    lane, sublane = lane_index(depth), sublane_index(depth)
    low = lane < NY
    zero = jnp.zeros((depth, LANES), jnp.float32)
    slots = [(f, n) for f in range(2) for n in range(steps)]
    has_before = jnp.where(rank > 0, 1.0, 0.0).astype(jnp.float32)
    has_after = jnp.where(rank < ranks - 1, 1.0, 0.0).astype(jnp.float32)
    gain = {(0, 0): ("forth", along), (1, 0): ("forth", across), (0, steps - 1): ("back", -across), (1, steps - 1): ("back", along)}

    def loaded(j):
        if j >= columns:
            return {s: zero for s in slots}
        near = {"forth": forth_ref[j], "back": back_ref[j]}
        values = {}
        for s in slots:
            values[s] = swept_ref[s[0], s[1], :, column(j)]
            if s in gain:
                values[s] = values[s] + gain[s][1] * near[gain[s][0]]
        return values

    def edges(j, side):
        block, row = 2 * columns + side * (columns // depth) + j // depth, j % depth
        near = {"forth": forth_ref[block, row : row + 1], "back": back_ref[block, row : row + 1]}
        values = {}
        for s in slots:
            k = side * 2 * steps + s[0] * steps + s[1]
            values[s] = edge_ref[k : k + 1, column(j)]
            if s in gain:
                values[s] = values[s] + gain[s][1] * near[gain[s][0]]
        return values

    now = loaded(0)
    pairs_before = now
    for j in range(columns):
        later = loaded(j + 1)
        over, under = edges(j, 0), edges(j, 1)
        pairs = {s: now[s] + later[s] for s in slots}
        around = {}
        for s in slots:
            across_rows = swapped_halves(jnp.where(low, pairs[s], pairs_before[s]))
            above = jnp.where(sublane == 0, over[s], pltpu.roll(now[s], 1, 0))
            below = jnp.where(sublane == depth - 1, under[s], pltpu.roll(now[s], depth - 1, 0))
            around[s] = across_rows + beside(now[s], lane) + (above + below)
        before = (forth_ref[columns + j] - across * iterate_ref[1, 0, :, column(j)]) * has_before
        after = (back_ref[columns + j] + across * iterate_ref[0, steps - 1, :, column(j)]) * has_after
        for n in range(steps):
            values = relaxed(
                (now[0, n], now[1, n]),
                (around[0, n], around[1, n]),
                now[0, n - 1] if n else before,
                now[1, n + 1] if n < steps - 1 else after,
                (forcing_ref[0, n, :, column(j)], forcing_ref[1, n, :, column(j)]),
            )
            for f in range(2):
                out_ref[f, n, :, column(j)] = values[f]
        now, pairs_before = later, pairs


def swapped(value, axis, mask):
    return lax.ppermute(value, axis, [(i, i ^ mask) for i in range(lax.axis_size(axis))])


def shifted(value, axis, by):
    size = lax.axis_size(axis)
    return lax.ppermute(value, axis, [(i, i + by) for i in range(size) if 0 <= i + by < size])


def add_kernel(place_ref, keep_ref, received_any, other_ref, own_ref, received_ref, arrived):
    pair = lax.div(place_ref[1], 2)
    parts = [(index, f) for index in (1 - pair, pair) for f in range(2)]
    copies = [
        pltpu.make_async_copy(received_any.at[index, f], received_ref.at[k], arrived.at[k])
        for k, (index, f) in enumerate(parts)
    ]
    for copy in copies:
        copy.start()
    for k, (index, f) in enumerate(parts):
        copies[k].wait()
        (other_ref, own_ref)[k // 2][f] = keep_ref[index, f] + received_ref[k]


def last_kernel(place_ref, mine_ref, given_ref, out_ref):
    steps = out_ref.shape[1]
    field = lax.rem(place_ref[0], 2)
    for j in range(mine_ref.shape[0]):
        for n in range(steps):
            out_ref[field, n, :, column(j)] = mine_ref[j]
            out_ref[1 - field, n, :, column(j)] = given_ref[j]


def local(iterate, forcing):
    steps, depth, cells = iterate.shape[1:]
    columns = cells // LANES
    ranks, slabs = lax.axis_size("tm"), 2 * lax.axis_size("pair")
    place = jnp.stack([lax.axis_index("tm"), lax.axis_index(("pair", "core")), jnp.zeros((), jnp.int32)]).astype(jnp.int32)
    keep, send = coarse_part(place, iterate, forcing)
    received = lax.ppermute(send, "core", [(0, 1), (1, 0)])

    keep, iterate_after, forcing_after = lax.optimization_barrier((keep, iterate, forcing))
    first, up, down = vmem_call(
        first_kernel, (iterate.shape, (4 * steps, cells), (4 * steps, cells)), (), (iterate_after, forcing_after)
    )
    other, own = vmem_call(
        add_kernel,
        (keep.shape[1:], keep.shape[1:]),
        (place,),
        (keep, received),
        (pltpu.VMEM((4,) + keep.shape[2:], jnp.float32), pltpu.SemaphoreType.DMA((4,))),
        spaces=(pltpu.VMEM, pl.ANY),
    )
    other, up, down = lax.optimization_barrier((other, up, down))
    above = shifted(up, ("pair", "core"), 1)
    below = shifted(down, ("pair", "core"), -1)
    term = swapped(other, "pair", 1)
    field = lax.rem(lax.axis_index("tm"), 2)

    def chosen(array, index):
        return lax.dynamic_index_in_dim(array, index, 0, keepdims=False)

    half = chosen(own, 1 - field) + chosen(term, 1 - field)
    half, above, below = lax.optimization_barrier((half, above, below))
    mine = chosen(own, field) + chosen(term, field) + swapped(half, "tm", 1)
    payload = (2 * columns + 2 * columns // depth, depth, LANES)
    swept, edge, forth, back = vmem_call(
        functools.partial(second_kernel, steps, slabs),
        (iterate.shape, (4 * steps, cells), payload, payload),
        (place,),
        (iterate, first, up, down, above, below),
    )
    mine, _, _ = lax.optimization_barrier((mine, forth, back))
    mask = 2
    while mask < ranks:
        mine = mine + swapped(mine, "tm", mask)
        mask *= 2
    given = swapped(mine, "tm", 1)
    (coarse,) = vmem_call(last_kernel, (iterate.shape,), (place,), (mine, given))
    forth = shifted(forth, "tm", 1)
    back = shifted(back, "tm", -1)
    (smoothed,) = vmem_call(
        functools.partial(third_kernel, steps, ranks),
        (iterate.shape,),
        (place,),
        (iterate, forcing, swept, edge, forth, back),
        cost=64 * 2**20,
    )
    return smoothed, coarse


def solution(mesh):
    ranks, slabs = mesh.shape["tm"], mesh.shape["space"]
    fine = jax.sharding.Mesh(mesh.devices.reshape(ranks, slabs // 2, 2), ("tm", "pair", "core"))
    specs = P(None, "tm", ("pair", "core"), None)
    return jax.shard_map(local, mesh=fine, in_specs=(specs, specs), out_specs=(specs, specs), check_vma=False)
```

```python
import functools

import numpy as np

import jax
import jax.numpy as jnp
from jax import lax
from jax.experimental import pallas as pl
from jax.experimental.pallas import tpu as pltpu
from jax.sharding import PartitionSpec as P

NY = 64
LANES = 128

KAPPA_BASE = 0.25
COUPLING_BASE = 0.5
DAMPING = 0.6


def level_terms(level):
    diffusion = KAPPA_BASE * 2.0**level
    coupling = COUPLING_BASE * 2.0**level
    centre = 1.0 + 6.0 * diffusion
    determinant = centre * centre + coupling * coupling
    along = DAMPING * centre / determinant
    across = DAMPING * coupling / determinant
    return diffusion, coupling, centre, along, across


def coarse_polynomials(total_steps):
    levels = total_steps.bit_length()
    powers = 2 * levels + 1
    unit = np.eye(4 * total_steps).reshape(-1, 2, 2, total_steps)
    fields = np.zeros((4 * total_steps, 2, total_steps, powers))
    source = np.zeros_like(fields)
    fields[..., 0] = unit[:, 0]
    source[..., 0] = unit[:, 1]

    def image(values, diffusion, coupling, centre):
        out = centre * values
        out[..., 1:] -= diffusion * values[..., :-1]
        out[:, 0, 1:] -= values[:, 0, :-1]
        out[:, 1, :-1] -= values[:, 1, 1:]
        out[:, 0] += coupling * values[:, 1]
        out[:, 1] -= coupling * values[:, 0]
        return out

    for level in range(levels):
        diffusion, coupling, centre, along, across = level_terms(level)
        for _ in range(2):
            defect = source - image(fields, diffusion, coupling, centre)
            state, adjoint = defect[:, 0], defect[:, 1]
            fields = fields + np.stack([along * state - across * adjoint, across * state + along * adjoint], 1)
        if level < levels - 1:
            defect = source - image(fields, diffusion, coupling, centre)
            source = defect[:, :, 0::2] + defect[:, :, 1::2]
            fields = np.zeros_like(source)
    return fields[:, :, 0].reshape(2, 2, total_steps, 2, powers)


def lane_index(depth):
    return lax.broadcasted_iota(jnp.int32, (depth, LANES), 1)


def sublane_index(depth):
    return lax.broadcasted_iota(jnp.int32, (depth, LANES), 0)


def column(j):
    return pl.ds(j * LANES, LANES)


def swapped_halves(value):
    return pltpu.roll(value, NY, 1)


def beside(value, lane):
    left = pltpu.roll(jnp.where((lane % NY) != NY - 1, value, 0.0), 1, 1)
    right = pltpu.roll(jnp.where((lane % NY) != 0, value, 0.0), LANES - 1, 1)
    return left + right


def tree_sum(terms):
    while len(terms) > 1:
        terms = [sum(terms[k : k + 2]) for k in range(0, len(terms), 2)]
    return terms[0]


def coarse_kernel(
    powers, steps, slabs, middle, place_ref, weights_hbm, iterate_hbm, forcing_hbm, keep_ref, send_ref, even, odd, packed, iterate_ref, forcing_ref, weights_ref, arrived, weighed
):
    copies = {
        (kind, f, n): pltpu.make_async_copy(source.at[f, n], target.at[f, n], arrived.at[kind, f, n])
        for kind, (source, target) in enumerate(((iterate_hbm, iterate_ref), (forcing_hbm, forcing_ref)))
        for n in range(steps)
        for f in range(2)
    }
    weighing = pltpu.make_async_copy(weights_hbm.at[place_ref[0]], weights_ref, weighed)
    for copy in copies.values():
        copy.start()
    weighing.start()
    even[...] = jnp.zeros_like(even)
    odd[...] = jnp.zeros_like(odd)
    depth, cells = iterate_ref.shape[2:]
    columns = cells // LANES
    rows = cells // NY
    inputs = 2 * steps
    slab, shift = place_ref[1], place_ref[2]
    lane = lane_index(depth)
    low = lane < NY
    zero = jnp.zeros((depth, LANES), jnp.float32)

    def inside(away):
        at = slab + away
        return jnp.where((at >= 0) & (at < slabs), 1.0, 0.0).astype(jnp.float32)

    for kind, ref in enumerate((iterate_ref, forcing_ref)):
        for n in range(steps):
            copies[kind, 0, n].wait()
            copies[kind, 1, n].wait()
            for j in range(columns):
                state, adjoint = ref[0, n, :, column(j)], ref[1, n, :, column(j)]
                state_turned, adjoint_turned = swapped_halves(state), swapped_halves(adjoint)
                k = 2 * (kind * steps + n)
                packed[k, 2 * j] = jnp.where(low, state, adjoint_turned)
                packed[k, 2 * j + 1] = jnp.where(low, state_turned, adjoint)
                packed[k + 1, 2 * j] = jnp.where(low, adjoint, state_turned)
                packed[k + 1, 2 * j + 1] = jnp.where(low, adjoint_turned, state)

    def weights(power):
        return [
            jnp.broadcast_to(weights_ref[pl.ds(power * 2 * inputs + k, 1), :], (depth, LANES)) for k in range(2 * inputs)
        ]

    def injected(factors, i):
        return tree_sum([factor * packed[k, i] for k, factor in enumerate(factors)])

    def advance(source, target, power, reach):
        aways = list(range(-reach, reach + 1))
        masks = [inside(away) for away in aways]
        factors = weights(power)

        def loaded(i):
            if i >= rows:
                return [zero for _ in aways]
            return [source[i, pl.ds((middle + away) * depth, depth), :] for away in aways]

        before = [zero for _ in aways]
        now = loaded(0)
        for i in range(rows):
            later = loaded(i + 1)
            for k, away in enumerate(aways):
                start = (middle + away) * depth
                above = source[i, pl.ds(shift + (start - 1), depth), :]
                below = source[i, pl.ds(shift + (start + 1), depth), :]
                value = (before[k] + later[k]) + beside(now[k], lane) + (above + below)
                if away:
                    value = value * masks[k]
                else:
                    value = value + injected(factors, i)
                target[i, pl.ds(start, depth), :] = value
            before, now = now, later

    weighing.wait()
    factors = weights(powers - 1)
    for i in range(rows):
        even[i, pl.ds(middle * depth, depth), :] = injected(factors, i)
    buffers = (even, odd)
    done = 0
    while done < powers - 1:
        reach = min(done // depth + 1, slabs - 1)
        count = powers - 1 - done if reach == slabs - 1 else min(depth, powers - 1 - done)

        def twice(index, _):
            power = powers - 2 - done - 2 * index
            advance(buffers[0], buffers[1], power, reach)
            advance(buffers[1], buffers[0], power - 1, reach)
            return 0

        lax.fori_loop(0, count // 2, twice, 0)
        done += count
        if count % 2:
            advance(buffers[0], buffers[1], powers - 1 - done, reach)
            buffers = buffers[::-1]

    final = buffers[0]
    bit = lax.rem(slab, 2)
    for half in range(slabs // 2):
        for ref, flag in ((keep_ref, bit), (send_ref, 1 - bit)):
            away = 2 * half + flag - slab
            planes = pl.ds(pl.multiple_of((middle + away) * depth, depth), depth)
            for j in range(columns):
                first, second = final[2 * j, planes, :], final[2 * j + 1, planes, :]
                for f, value in (
                    (0, jnp.where(low, first, swapped_halves(second))),
                    (1, jnp.where(low, swapped_halves(first), second)),
                ):
                    ref[half, f, j] = value


def vmem_call(kernel, out_shapes, smem_inputs, inputs, scratch=(), spaces=None, limit=6, cost=2**20):
    smem = pl.BlockSpec(memory_space=pltpu.SMEM)
    vmem = pl.BlockSpec(memory_space=pltpu.VMEM)
    out_shape = tuple(jax.ShapeDtypeStruct(shape, jnp.float32) for shape in out_shapes)
    return pl.pallas_call(
        kernel,
        out_shape=out_shape,
        in_specs=[smem] * len(smem_inputs) + [pl.BlockSpec(memory_space=space) for space in spaces or [pltpu.VMEM] * len(inputs)],
        out_specs=(vmem,) * len(out_shape),
        scratch_shapes=list(scratch),
        compiler_params=pltpu.CompilerParams(vmem_limit_bytes=limit * 2**20),
        cost_estimate=pl.CostEstimate(flops=10**6, bytes_accessed=cost, transcendentals=0),
    )(*smem_inputs, *inputs)


def coarse_part(place, iterate, forcing):
    steps = iterate.shape[1]
    depth, cells = iterate.shape[2:]
    ranks, slabs = lax.axis_size("tm"), 2 * lax.axis_size("pair")
    table = coarse_polynomials(steps * ranks)
    powers = table.shape[-1]
    table = table.reshape(2, 2, ranks, steps, 2, powers)
    same = np.stack([table[:, 0, :, :, 0], table[:, 1, :, :, 1]], -1)
    other = np.stack([table[:, 1, :, :, 0], table[:, 0, :, :, 1]], -1)
    weights = np.stack([same, other], -2).transpose(1, 3, 0, 2, 4, 5).astype(np.float32)
    reach = min(-(-(powers - 1) // depth), slabs - 1)
    middle = max(reach + 1, slabs - 1)
    weights = np.repeat(weights.reshape(ranks, -1, 2), NY, -1)
    half = (slabs // 2, 2, cells // LANES, depth, LANES)
    buffer = pltpu.VMEM((cells // NY, (2 * middle + 1) * depth, LANES), jnp.float32)
    packed = pltpu.VMEM((4 * steps, cells // NY, depth, LANES), jnp.float32)
    return vmem_call(
        functools.partial(coarse_kernel, powers, steps, slabs, middle),
        (half, half),
        (place,),
        [pltpu.with_memory_space_constraint(array, pltpu.HBM) for array in (jnp.asarray(weights), iterate, forcing)],
        (
            buffer,
            buffer,
            packed,
            pltpu.VMEM(iterate.shape, jnp.float32),
            pltpu.VMEM(forcing.shape, jnp.float32),
            pltpu.VMEM(weights.shape[1:], jnp.float32),
            pltpu.SemaphoreType.DMA((2, 2, steps)),
            pltpu.SemaphoreType.DMA,
        ),
        spaces=(pltpu.HBM,) * 3,
        limit=12,
        cost=24 * 2**20,
    )


def relaxed(fields, around, before, after, source):
    diffusion, coupling, centre, along, across = level_terms(0)
    state, adjoint = fields
    defect_state = source[0] - (centre * state - diffusion * around[0] - before + coupling * adjoint)
    defect_adjoint = source[1] - (centre * adjoint - diffusion * around[1] - after - coupling * state)
    return (
        state + along * defect_state - across * defect_adjoint,
        adjoint + across * defect_state + along * defect_adjoint,
    )


def first_kernel(iterate_ref, forcing_ref, first_ref, up_ref, down_ref, forth_ref, back_ref):
    steps, depth, cells = iterate_ref.shape[1:]
    columns = cells // LANES
    lane, sublane = lane_index(depth), sublane_index(depth)
    low = lane < NY
    zero = jnp.zeros((depth, LANES), jnp.float32)
    slots = [(f, n) for f in range(2) for n in range(steps)]

    def loaded(j):
        return {s: iterate_ref[s[0], s[1], :, column(j)] if j < columns else zero for s in slots}

    now = loaded(0)
    pairs_before = now
    for j in range(columns):
        later = loaded(j + 1)
        pairs = {s: now[s] + later[s] for s in slots}
        around = {}
        for s in slots:
            across_rows = swapped_halves(jnp.where(low, pairs[s], pairs_before[s]))
            above = jnp.where(sublane == 0, 0.0, pltpu.roll(now[s], 1, 0))
            below = jnp.where(sublane == depth - 1, 0.0, pltpu.roll(now[s], depth - 1, 0))
            around[s] = across_rows + beside(now[s], lane) + (above + below)
        for n in range(steps):
            values = relaxed(
                (now[0, n], now[1, n]),
                (around[0, n], around[1, n]),
                now[0, n - 1] if n else zero,
                now[1, n + 1] if n < steps - 1 else zero,
                (forcing_ref[0, n, :, column(j)], forcing_ref[1, n, :, column(j)]),
            )
            for f in range(2):
                first_ref[f, n, :, column(j)] = values[f]
                for ref, field, step in ((forth_ref, 0, steps - 1), (back_ref, 1, 0)):
                    if (f, n) == (field, step):
                        ref[j] = now[f, n]
                        ref[columns + j] = values[f]
                slot = f * steps + n
                for ref, plane in ((up_ref, depth - 1), (down_ref, 0)):
                    ref[slot : slot + 1, column(j)] = now[f, n][plane : plane + 1]
                    slot_after = 2 * steps + slot
                    ref[slot_after : slot_after + 1, column(j)] = values[f][plane : plane + 1]
        now, pairs_before = later, pairs


def second_kernel(
    steps, slabs, place_ref, first_ref, up_ref, down_ref, above_ref, below_ref, swept_ref, edge_ref, forth_ref, back_ref
):
    diffusion, _, _, along, across = level_terms(0)
    depth, cells = first_ref.shape[2:]
    columns = cells // LANES
    slab = place_ref[1]
    sublane = sublane_index(depth)
    count = 2 * steps
    has_above = jnp.where(slab > 0, 1.0, 0.0).astype(jnp.float32)
    has_below = jnp.where(slab < slabs - 1, 1.0, 0.0).astype(jnp.float32)

    def mixed(rows):
        state, adjoint = rows[:steps], rows[steps:]
        return jnp.concatenate(
            [
                (along * diffusion) * state - (across * diffusion) * adjoint,
                (across * diffusion) * state + (along * diffusion) * adjoint,
            ],
            0,
        )

    def one(j):
        return slice(j * LANES, (j + 1) * LANES)

    for j in range(columns):
        from_above, from_below = above_ref[:, one(j)], below_ref[:, one(j)]
        edge_ref[:count, one(j)] = (from_above[count:] + mixed(down_ref[:count, one(j)])) * has_above
        edge_ref[count:, one(j)] = (from_below[count:] + mixed(up_ref[:count, one(j)])) * has_below
        add_above, add_below = mixed(from_above[:count]), mixed(from_below[:count])
        for f in range(2):
            for n in range(steps):
                k = f * steps + n
                value = first_ref[f, n, :, one(j)]
                value = value + jnp.where(sublane == 0, add_above[k : k + 1], 0.0)
                value = value + jnp.where(sublane == depth - 1, add_below[k : k + 1], 0.0)
                swept_ref[f, n, :, one(j)] = value
                for ref, step in ((forth_ref, steps - 1), (back_ref, 0)):
                    if n == step:
                        for side, rows in enumerate((from_above, from_below)):
                            block, row = (2 * side + f) * (columns // depth) + j // depth, j % depth
                            ref[block, row : row + 1] = rows[k : k + 1]


def third_kernel(
    steps, ranks, place_ref, iterate_ref, forcing_ref, swept_ref, edge_ref, forth_ref, back_ref, forth_edge_ref, back_edge_ref, out_ref
):
    diffusion, _, _, along, across = level_terms(0)
    depth, cells = iterate_ref.shape[2:]
    columns = cells // LANES
    rank = place_ref[0]
    lane, sublane = lane_index(depth), sublane_index(depth)
    low = lane < NY
    zero = jnp.zeros((depth, LANES), jnp.float32)
    slots = [(f, n) for f in range(2) for n in range(steps)]
    has_before = jnp.where(rank > 0, 1.0, 0.0).astype(jnp.float32)
    has_after = jnp.where(rank < ranks - 1, 1.0, 0.0).astype(jnp.float32)
    gain = {(0, 0): ("forth", along), (1, 0): ("forth", across), (0, steps - 1): ("back", -across), (1, steps - 1): ("back", along)}

    def loaded(j):
        if j >= columns:
            return {s: zero for s in slots}
        near = {"forth": forth_ref[j], "back": back_ref[j]}
        values = {}
        for s in slots:
            values[s] = swept_ref[s[0], s[1], :, column(j)]
            if s in gain:
                values[s] = values[s] + gain[s][1] * near[gain[s][0]]
        return values

    def edge_row(ref, j, side, f):
        block, row = (2 * side + f) * (columns // depth) + j // depth, j % depth
        return ref[block, row : row + 1]

    def edges(j, side):
        near = {"forth": edge_row(forth_edge_ref, j, side, 0), "back": edge_row(back_edge_ref, j, side, 1)}
        values = {}
        for s in slots:
            k = side * 2 * steps + s[0] * steps + s[1]
            values[s] = edge_ref[k : k + 1, column(j)]
            if s in gain:
                values[s] = values[s] + gain[s][1] * near[gain[s][0]]
        return values

    now = loaded(0)
    pairs_before = now
    for j in range(columns):
        later = loaded(j + 1)
        over, under = edges(j, 0), edges(j, 1)
        pairs = {s: now[s] + later[s] for s in slots}
        around = {}
        for s in slots:
            across_rows = swapped_halves(jnp.where(low, pairs[s], pairs_before[s]))
            above = jnp.where(sublane == 0, over[s], pltpu.roll(now[s], 1, 0))
            below = jnp.where(sublane == depth - 1, under[s], pltpu.roll(now[s], depth - 1, 0))
            around[s] = across_rows + beside(now[s], lane) + (above + below)
        before = forth_ref[columns + j] - across * iterate_ref[1, 0, :, column(j)]
        after = back_ref[columns + j] + across * iterate_ref[0, steps - 1, :, column(j)]
        for side, at in ((0, sublane == 0), (1, sublane == depth - 1)):
            state, adjoint = (edge_row(forth_edge_ref, j, side, f) for f in range(2))
            before = before + jnp.where(at, (along * diffusion) * state - (across * diffusion) * adjoint, 0.0)
            state, adjoint = (edge_row(back_edge_ref, j, side, f) for f in range(2))
            after = after + jnp.where(at, (across * diffusion) * state + (along * diffusion) * adjoint, 0.0)
        before, after = before * has_before, after * has_after
        for n in range(steps):
            values = relaxed(
                (now[0, n], now[1, n]),
                (around[0, n], around[1, n]),
                now[0, n - 1] if n else before,
                now[1, n + 1] if n < steps - 1 else after,
                (forcing_ref[0, n, :, column(j)], forcing_ref[1, n, :, column(j)]),
            )
            for f in range(2):
                out_ref[f, n, :, column(j)] = values[f]
        now, pairs_before = later, pairs


def swapped(value, axis, mask):
    return lax.ppermute(value, axis, [(i, i ^ mask) for i in range(lax.axis_size(axis))])


def shifted(value, axis, by):
    size = lax.axis_size(axis)
    return lax.ppermute(value, axis, [(i, i + by) for i in range(size) if 0 <= i + by < size])


def add_kernel(place_ref, keep_ref, received_any, other_ref, own_ref, received_ref, arrived):
    pair = lax.div(place_ref[1], 2)
    parts = [(index, f) for index in (1 - pair, pair) for f in range(2)]
    copies = [
        pltpu.make_async_copy(received_any.at[index, f], received_ref.at[k], arrived.at[k])
        for k, (index, f) in enumerate(parts)
    ]
    for copy in copies:
        copy.start()
    for k, (index, f) in enumerate(parts):
        copies[k].wait()
        (other_ref, own_ref)[k // 2][f] = keep_ref[index, f] + received_ref[k]


def last_kernel(place_ref, mine_ref, given_ref, out_ref):
    steps = out_ref.shape[1]
    field = lax.rem(place_ref[0], 2)
    for j in range(mine_ref.shape[0]):
        for n in range(steps):
            out_ref[field, n, :, column(j)] = mine_ref[j]
            out_ref[1 - field, n, :, column(j)] = given_ref[j]


def local(iterate, forcing):
    steps, depth, cells = iterate.shape[1:]
    columns = cells // LANES
    ranks, slabs = lax.axis_size("tm"), 2 * lax.axis_size("pair")
    place = jnp.stack([lax.axis_index("tm"), lax.axis_index(("pair", "core")), jnp.zeros((), jnp.int32)]).astype(jnp.int32)
    keep, send = coarse_part(place, iterate, forcing)
    received = lax.ppermute(send, "core", [(0, 1), (1, 0)])

    keep, iterate_after, forcing_after = lax.optimization_barrier((keep, iterate, forcing))
    last = (2 * columns, depth, LANES)
    first, up, down, forth, back = vmem_call(
        first_kernel,
        (iterate.shape, (4 * steps, cells), (4 * steps, cells), last, last),
        (),
        (iterate_after, forcing_after),
    )
    other, own = vmem_call(
        add_kernel,
        (keep.shape[1:], keep.shape[1:]),
        (place,),
        (keep, received),
        (pltpu.VMEM((4,) + keep.shape[2:], jnp.float32), pltpu.SemaphoreType.DMA((4,))),
        spaces=(pltpu.VMEM, pl.ANY),
    )
    other, up, down, forth, back = lax.optimization_barrier((other, up, down, forth, back))
    forth = shifted(forth, "tm", 1)
    back = shifted(back, "tm", -1)
    above = shifted(up, ("pair", "core"), 1)
    below = shifted(down, ("pair", "core"), -1)
    term = swapped(other, "pair", 1)
    field = lax.rem(lax.axis_index("tm"), 2)

    def chosen(array, index):
        return lax.dynamic_index_in_dim(array, index, 0, keepdims=False)

    half = chosen(own, 1 - field) + chosen(term, 1 - field)
    half, above, below = lax.optimization_barrier((half, above, below))
    mine = chosen(own, field) + chosen(term, field) + swapped(half, "tm", 1)
    rows = (4 * columns // depth, depth, LANES)
    swept, edge, forth_edge, back_edge = vmem_call(
        functools.partial(second_kernel, steps, slabs),
        (iterate.shape, (4 * steps, cells), rows, rows),
        (place,),
        (first, up, down, above, below),
    )
    mine, forth_edge, back_edge = lax.optimization_barrier((mine, forth_edge, back_edge))
    forth_edge = shifted(forth_edge, "tm", 1)
    back_edge = shifted(back_edge, "tm", -1)
    mine, forth, back = lax.optimization_barrier((mine, forth, back))
    mask = 2
    while mask < ranks:
        mine = mine + swapped(mine, "tm", mask)
        mask *= 2
    mine, forth_edge, back_edge = lax.optimization_barrier((mine, forth_edge, back_edge))
    given = swapped(mine, "tm", 1)
    (coarse,) = vmem_call(last_kernel, (iterate.shape,), (place,), (mine, given))
    (smoothed,) = vmem_call(
        functools.partial(third_kernel, steps, ranks),
        (iterate.shape,),
        (place,),
        (iterate, forcing, swept, edge, forth, back, forth_edge, back_edge),
        cost=8 * 2**20,
    )
    return smoothed, coarse


def solution(mesh):
    ranks, slabs = mesh.shape["tm"], mesh.shape["space"]
    fine = jax.sharding.Mesh(mesh.devices.reshape(ranks, slabs // 2, 2), ("tm", "pair", "core"))
    specs = P(None, "tm", ("pair", "core"), None)
    return jax.shard_map(local, mesh=fine, in_specs=(specs, specs), out_specs=(specs, specs), check_vma=False)
```

```python
import functools

import numpy as np

import jax
import jax.numpy as jnp
from jax import lax
from jax.experimental import pallas as pl
from jax.experimental.pallas import tpu as pltpu
from jax.sharding import PartitionSpec as P

NY = 64
LANES = 128

KAPPA_BASE = 0.25
COUPLING_BASE = 0.5
DAMPING = 0.6


def level_terms(level):
    diffusion = KAPPA_BASE * 2.0**level
    coupling = COUPLING_BASE * 2.0**level
    centre = 1.0 + 6.0 * diffusion
    determinant = centre * centre + coupling * coupling
    along = DAMPING * centre / determinant
    across = DAMPING * coupling / determinant
    return diffusion, coupling, centre, along, across


def coarse_polynomials(total_steps):
    levels = total_steps.bit_length()
    powers = 2 * levels + 1
    unit = np.eye(4 * total_steps).reshape(-1, 2, 2, total_steps)
    fields = np.zeros((4 * total_steps, 2, total_steps, powers))
    source = np.zeros_like(fields)
    fields[..., 0] = unit[:, 0]
    source[..., 0] = unit[:, 1]

    def image(values, diffusion, coupling, centre):
        out = centre * values
        out[..., 1:] -= diffusion * values[..., :-1]
        out[:, 0, 1:] -= values[:, 0, :-1]
        out[:, 1, :-1] -= values[:, 1, 1:]
        out[:, 0] += coupling * values[:, 1]
        out[:, 1] -= coupling * values[:, 0]
        return out

    for level in range(levels):
        diffusion, coupling, centre, along, across = level_terms(level)
        for _ in range(2):
            defect = source - image(fields, diffusion, coupling, centre)
            state, adjoint = defect[:, 0], defect[:, 1]
            fields = fields + np.stack([along * state - across * adjoint, across * state + along * adjoint], 1)
        if level < levels - 1:
            defect = source - image(fields, diffusion, coupling, centre)
            source = defect[:, :, 0::2] + defect[:, :, 1::2]
            fields = np.zeros_like(source)
    return fields[:, :, 0].reshape(2, 2, total_steps, 2, powers)


def lane_index(depth):
    return lax.broadcasted_iota(jnp.int32, (depth, LANES), 1)


def sublane_index(depth):
    return lax.broadcasted_iota(jnp.int32, (depth, LANES), 0)


def column(j):
    return pl.ds(j * LANES, LANES)


def swapped_halves(value):
    return pltpu.roll(value, NY, 1)


def beside(value, lane):
    left = pltpu.roll(jnp.where((lane % NY) != NY - 1, value, 0.0), 1, 1)
    right = pltpu.roll(jnp.where((lane % NY) != 0, value, 0.0), LANES - 1, 1)
    return left + right


def tree_sum(terms):
    while len(terms) > 1:
        terms = [sum(terms[k : k + 2]) for k in range(0, len(terms), 2)]
    return terms[0]


def coarse_kernel(
    powers, steps, slabs, middle, place_ref, weights_hbm, iterate_hbm, forcing_hbm, keep_ref, send_ref, even, odd, packed, iterate_ref, forcing_ref, weights_ref, arrived, weighed
):
    copies = {
        (kind, f, n): pltpu.make_async_copy(source.at[f, n], target.at[f, n], arrived.at[kind, f, n])
        for kind, (source, target) in enumerate(((iterate_hbm, iterate_ref), (forcing_hbm, forcing_ref)))
        for n in range(steps)
        for f in range(2)
    }
    weighing = pltpu.make_async_copy(weights_hbm.at[place_ref[0]], weights_ref, weighed)
    for copy in copies.values():
        copy.start()
    weighing.start()
    even[...] = jnp.zeros_like(even)
    odd[...] = jnp.zeros_like(odd)
    depth, cells = iterate_ref.shape[2:]
    columns = cells // LANES
    rows = cells // NY
    inputs = 2 * steps
    slab, shift = place_ref[1], place_ref[2]
    lane = lane_index(depth)
    low = lane < NY
    zero = jnp.zeros((depth, LANES), jnp.float32)

    def inside(away):
        at = slab + away
        return jnp.where((at >= 0) & (at < slabs), 1.0, 0.0).astype(jnp.float32)

    for kind, ref in enumerate((iterate_ref, forcing_ref)):
        for n in range(steps):
            copies[kind, 0, n].wait()
            copies[kind, 1, n].wait()
            for j in range(columns):
                state, adjoint = ref[0, n, :, column(j)], ref[1, n, :, column(j)]
                state_turned, adjoint_turned = swapped_halves(state), swapped_halves(adjoint)
                k = 2 * (kind * steps + n)
                packed[k, 2 * j] = jnp.where(low, state, adjoint_turned)
                packed[k, 2 * j + 1] = jnp.where(low, state_turned, adjoint)
                packed[k + 1, 2 * j] = jnp.where(low, adjoint, state_turned)
                packed[k + 1, 2 * j + 1] = jnp.where(low, adjoint_turned, state)

    def weights(power):
        return [
            jnp.broadcast_to(weights_ref[pl.ds(power * 2 * inputs + k, 1), :], (depth, LANES)) for k in range(2 * inputs)
        ]

    def injected(factors, i):
        return tree_sum([factor * packed[k, i] for k, factor in enumerate(factors)])

    def advance(source, target, power, reach):
        aways = list(range(-reach, reach + 1))
        masks = [inside(away) for away in aways]
        factors = weights(power)

        def loaded(i):
            if i >= rows:
                return [zero for _ in aways]
            return [source[i, pl.ds((middle + away) * depth, depth), :] for away in aways]

        before = [zero for _ in aways]
        now = loaded(0)
        for i in range(rows):
            later = loaded(i + 1)
            for k, away in enumerate(aways):
                start = (middle + away) * depth
                above = source[i, pl.ds(shift + (start - 1), depth), :]
                below = source[i, pl.ds(shift + (start + 1), depth), :]
                value = (before[k] + later[k]) + beside(now[k], lane) + (above + below)
                if away:
                    value = value * masks[k]
                else:
                    value = value + injected(factors, i)
                target[i, pl.ds(start, depth), :] = value
            before, now = now, later

    weighing.wait()
    factors = weights(powers - 1)
    for i in range(rows):
        even[i, pl.ds(middle * depth, depth), :] = injected(factors, i)
    buffers = (even, odd)
    done = 0
    while done < powers - 1:
        reach = min(done // depth + 1, slabs - 1)
        count = powers - 1 - done if reach == slabs - 1 else min(depth, powers - 1 - done)

        def twice(index, _):
            power = powers - 2 - done - 2 * index
            advance(buffers[0], buffers[1], power, reach)
            advance(buffers[1], buffers[0], power - 1, reach)
            return 0

        lax.fori_loop(0, count // 2, twice, 0)
        done += count
        if count % 2:
            advance(buffers[0], buffers[1], powers - 1 - done, reach)
            buffers = buffers[::-1]

    final = buffers[0]
    bit = lax.rem(slab, 2)
    for half in range(slabs // 2):
        for ref, flag in ((keep_ref, bit), (send_ref, 1 - bit)):
            away = 2 * half + flag - slab
            planes = pl.ds(pl.multiple_of((middle + away) * depth, depth), depth)
            for j in range(columns):
                first, second = final[2 * j, planes, :], final[2 * j + 1, planes, :]
                for f, value in (
                    (0, jnp.where(low, first, swapped_halves(second))),
                    (1, jnp.where(low, swapped_halves(first), second)),
                ):
                    ref[half, f, j] = value


def vmem_call(kernel, out_shapes, smem_inputs, inputs, scratch=(), spaces=None, target=pltpu.VMEM, limit=6, cost=2**20):
    smem = pl.BlockSpec(memory_space=pltpu.SMEM)
    out_shape = tuple(jax.ShapeDtypeStruct(shape, jnp.float32) for shape in out_shapes)
    return pl.pallas_call(
        kernel,
        out_shape=out_shape,
        in_specs=[smem] * len(smem_inputs) + [pl.BlockSpec(memory_space=space) for space in spaces or [pltpu.VMEM] * len(inputs)],
        out_specs=(pl.BlockSpec(memory_space=target),) * len(out_shape),
        scratch_shapes=list(scratch),
        compiler_params=pltpu.CompilerParams(vmem_limit_bytes=limit * 2**20),
        cost_estimate=pl.CostEstimate(flops=10**6, bytes_accessed=cost, transcendentals=0),
    )(*smem_inputs, *inputs)


def coarse_part(place, iterate, forcing):
    steps = iterate.shape[1]
    depth, cells = iterate.shape[2:]
    ranks, slabs = lax.axis_size("tm"), 2 * lax.axis_size("pair")
    table = coarse_polynomials(steps * ranks)
    powers = table.shape[-1]
    table = table.reshape(2, 2, ranks, steps, 2, powers)
    same = np.stack([table[:, 0, :, :, 0], table[:, 1, :, :, 1]], -1)
    other = np.stack([table[:, 1, :, :, 0], table[:, 0, :, :, 1]], -1)
    weights = np.stack([same, other], -2).transpose(1, 3, 0, 2, 4, 5).astype(np.float32)
    reach = min(-(-(powers - 1) // depth), slabs - 1)
    middle = max(reach + 1, slabs - 1)
    weights = np.repeat(weights.reshape(ranks, -1, 2), NY, -1)
    half = (slabs // 2, 2, cells // LANES, depth, LANES)
    buffer = pltpu.VMEM((cells // NY, (2 * middle + 1) * depth, LANES), jnp.float32)
    packed = pltpu.VMEM((4 * steps, cells // NY, depth, LANES), jnp.float32)
    return vmem_call(
        functools.partial(coarse_kernel, powers, steps, slabs, middle),
        (half, half),
        (place,),
        [pltpu.with_memory_space_constraint(array, pltpu.HBM) for array in (jnp.asarray(weights), iterate, forcing)],
        (
            buffer,
            buffer,
            packed,
            pltpu.VMEM(iterate.shape, jnp.float32),
            pltpu.VMEM(forcing.shape, jnp.float32),
            pltpu.VMEM(weights.shape[1:], jnp.float32),
            pltpu.SemaphoreType.DMA((2, 2, steps)),
            pltpu.SemaphoreType.DMA,
        ),
        spaces=(pltpu.HBM,) * 3,
        limit=12,
        cost=24 * 2**20,
    )


def relaxed(fields, around, before, after, source):
    diffusion, coupling, centre, along, across = level_terms(0)
    state, adjoint = fields
    defect_state = source[0] - (centre * state - diffusion * around[0] - before + coupling * adjoint)
    defect_adjoint = source[1] - (centre * adjoint - diffusion * around[1] - after - coupling * state)
    return (
        state + along * defect_state - across * defect_adjoint,
        adjoint + across * defect_state + along * defect_adjoint,
    )


def first_kernel(iterate_ref, forcing_ref, first_ref, up_ref, down_ref, forth_ref, back_ref):
    steps, depth, cells = iterate_ref.shape[1:]
    columns = cells // LANES
    lane, sublane = lane_index(depth), sublane_index(depth)
    low = lane < NY
    zero = jnp.zeros((depth, LANES), jnp.float32)
    slots = [(f, n) for f in range(2) for n in range(steps)]

    def loaded(j):
        return {s: iterate_ref[s[0], s[1], :, column(j)] if j < columns else zero for s in slots}

    now = loaded(0)
    pairs_before = now
    for j in range(columns):
        later = loaded(j + 1)
        pairs = {s: now[s] + later[s] for s in slots}
        around = {}
        for s in slots:
            across_rows = swapped_halves(jnp.where(low, pairs[s], pairs_before[s]))
            above = jnp.where(sublane == 0, 0.0, pltpu.roll(now[s], 1, 0))
            below = jnp.where(sublane == depth - 1, 0.0, pltpu.roll(now[s], depth - 1, 0))
            around[s] = across_rows + beside(now[s], lane) + (above + below)
        for n in range(steps):
            values = relaxed(
                (now[0, n], now[1, n]),
                (around[0, n], around[1, n]),
                now[0, n - 1] if n else zero,
                now[1, n + 1] if n < steps - 1 else zero,
                (forcing_ref[0, n, :, column(j)], forcing_ref[1, n, :, column(j)]),
            )
            for f in range(2):
                first_ref[f, n, :, column(j)] = values[f]
                for ref, field, step in ((forth_ref, 0, steps - 1), (back_ref, 1, 0)):
                    if (f, n) == (field, step):
                        ref[j] = now[f, n]
                        ref[columns + j] = values[f]
                slot = f * steps + n
                for ref, plane in ((up_ref, depth - 1), (down_ref, 0)):
                    ref[slot : slot + 1, column(j)] = now[f, n][plane : plane + 1]
                    slot_after = 2 * steps + slot
                    ref[slot_after : slot_after + 1, column(j)] = values[f][plane : plane + 1]
        now, pairs_before = later, pairs


def second_kernel(
    steps, slabs, place_ref, first_ref, up_ref, down_ref, above_ref, below_ref, swept_ref, edge_ref, forth_ref, back_ref
):
    diffusion, _, _, along, across = level_terms(0)
    depth, cells = first_ref.shape[2:]
    columns = cells // LANES
    slab = place_ref[1]
    sublane = sublane_index(depth)
    count = 2 * steps
    has_above = jnp.where(slab > 0, 1.0, 0.0).astype(jnp.float32)
    has_below = jnp.where(slab < slabs - 1, 1.0, 0.0).astype(jnp.float32)

    def mixed(rows):
        state, adjoint = rows[:steps], rows[steps:]
        return jnp.concatenate(
            [
                (along * diffusion) * state - (across * diffusion) * adjoint,
                (across * diffusion) * state + (along * diffusion) * adjoint,
            ],
            0,
        )

    def one(j):
        return slice(j * LANES, (j + 1) * LANES)

    for j in range(columns):
        from_above, from_below = above_ref[:, one(j)], below_ref[:, one(j)]
        edge_ref[:count, one(j)] = (from_above[count:] + mixed(down_ref[:count, one(j)])) * has_above
        edge_ref[count:, one(j)] = (from_below[count:] + mixed(up_ref[:count, one(j)])) * has_below
        add_above, add_below = mixed(from_above[:count]), mixed(from_below[:count])
        for f in range(2):
            for n in range(steps):
                k = f * steps + n
                value = first_ref[f, n, :, one(j)]
                value = value + jnp.where(sublane == 0, add_above[k : k + 1], 0.0)
                value = value + jnp.where(sublane == depth - 1, add_below[k : k + 1], 0.0)
                swept_ref[f, n, :, one(j)] = value
                for ref, step in ((forth_ref, steps - 1), (back_ref, 0)):
                    if n == step:
                        for side, rows in enumerate((from_above, from_below)):
                            block, row = (2 * side + f) * (columns // depth) + j // depth, j % depth
                            ref[block, row : row + 1] = rows[k : k + 1]


def third_kernel(
    steps, ranks, place_ref, iterate_ref, forcing_ref, swept_ref, edge_ref, forth_ref, back_ref, forth_edge_ref, back_edge_ref, out_ref
):
    diffusion, _, _, along, across = level_terms(0)
    depth, cells = iterate_ref.shape[2:]
    columns = cells // LANES
    rank = place_ref[0]
    lane, sublane = lane_index(depth), sublane_index(depth)
    low = lane < NY
    zero = jnp.zeros((depth, LANES), jnp.float32)
    slots = [(f, n) for f in range(2) for n in range(steps)]
    has_before = jnp.where(rank > 0, 1.0, 0.0).astype(jnp.float32)
    has_after = jnp.where(rank < ranks - 1, 1.0, 0.0).astype(jnp.float32)
    gain = {(0, 0): ("forth", along), (1, 0): ("forth", across), (0, steps - 1): ("back", -across), (1, steps - 1): ("back", along)}

    def loaded(j):
        if j >= columns:
            return {s: zero for s in slots}
        near = {"forth": forth_ref[j], "back": back_ref[j]}
        values = {}
        for s in slots:
            values[s] = swept_ref[s[0], s[1], :, column(j)]
            if s in gain:
                values[s] = values[s] + gain[s][1] * near[gain[s][0]]
        return values

    def edge_row(ref, j, side, f):
        block, row = (2 * side + f) * (columns // depth) + j // depth, j % depth
        return ref[block, row : row + 1]

    def edges(j, side):
        near = {"forth": edge_row(forth_edge_ref, j, side, 0), "back": edge_row(back_edge_ref, j, side, 1)}
        values = {}
        for s in slots:
            k = side * 2 * steps + s[0] * steps + s[1]
            values[s] = edge_ref[k : k + 1, column(j)]
            if s in gain:
                values[s] = values[s] + gain[s][1] * near[gain[s][0]]
        return values

    now = loaded(0)
    pairs_before = now
    for j in range(columns):
        later = loaded(j + 1)
        over, under = edges(j, 0), edges(j, 1)
        pairs = {s: now[s] + later[s] for s in slots}
        around = {}
        for s in slots:
            across_rows = swapped_halves(jnp.where(low, pairs[s], pairs_before[s]))
            above = jnp.where(sublane == 0, over[s], pltpu.roll(now[s], 1, 0))
            below = jnp.where(sublane == depth - 1, under[s], pltpu.roll(now[s], depth - 1, 0))
            around[s] = across_rows + beside(now[s], lane) + (above + below)
        before = forth_ref[columns + j] - across * iterate_ref[1, 0, :, column(j)]
        after = back_ref[columns + j] + across * iterate_ref[0, steps - 1, :, column(j)]
        for side, at in ((0, sublane == 0), (1, sublane == depth - 1)):
            state, adjoint = (edge_row(forth_edge_ref, j, side, f) for f in range(2))
            before = before + jnp.where(at, (along * diffusion) * state - (across * diffusion) * adjoint, 0.0)
            state, adjoint = (edge_row(back_edge_ref, j, side, f) for f in range(2))
            after = after + jnp.where(at, (across * diffusion) * state + (along * diffusion) * adjoint, 0.0)
        before, after = before * has_before, after * has_after
        for n in range(steps):
            values = relaxed(
                (now[0, n], now[1, n]),
                (around[0, n], around[1, n]),
                now[0, n - 1] if n else before,
                now[1, n + 1] if n < steps - 1 else after,
                (forcing_ref[0, n, :, column(j)], forcing_ref[1, n, :, column(j)]),
            )
            for f in range(2):
                out_ref[f, n, :, column(j)] = values[f]
        now, pairs_before = later, pairs


def swapped(value, axis, mask):
    return lax.ppermute(value, axis, [(i, i ^ mask) for i in range(lax.axis_size(axis))])


def shifted(value, axis, by):
    size = lax.axis_size(axis)
    return lax.ppermute(value, axis, [(i, i + by) for i in range(size) if 0 <= i + by < size])


def add_kernel(place_ref, keep_ref, received_any, other_ref, own_ref, received_ref, arrived):
    pair = lax.div(place_ref[1], 2)
    parts = [(index, f) for index in (1 - pair, pair) for f in range(2)]
    copies = [
        pltpu.make_async_copy(received_any.at[index, f], received_ref.at[k], arrived.at[k])
        for k, (index, f) in enumerate(parts)
    ]
    for copy in copies:
        copy.start()
    for k, (index, f) in enumerate(parts):
        copies[k].wait()
        (other_ref, own_ref)[k // 2][f] = keep_ref[index, f] + received_ref[k]


def last_kernel(place_ref, mine_ref, given_ref, out_hbm, whole_ref, left):
    steps = out_hbm.shape[1]
    field = lax.rem(place_ref[0], 2)
    copies = []
    for k, (ref, f) in enumerate(((mine_ref, field), (given_ref, 1 - field))):
        for j in range(ref.shape[0]):
            whole_ref[k, :, column(j)] = ref[j]
        for n in range(steps):
            copies.append(pltpu.make_async_copy(whole_ref.at[k], out_hbm.at[f, n], left.at[k, n]))
            copies[-1].start()
    for copy in copies:
        copy.wait()


def local(iterate, forcing):
    steps, depth, cells = iterate.shape[1:]
    columns = cells // LANES
    ranks, slabs = lax.axis_size("tm"), 2 * lax.axis_size("pair")
    place = jnp.stack([lax.axis_index("tm"), lax.axis_index(("pair", "core")), jnp.zeros((), jnp.int32)]).astype(jnp.int32)
    keep, send = coarse_part(place, iterate, forcing)
    received = lax.ppermute(send, "core", [(0, 1), (1, 0)])

    keep, iterate_after, forcing_after = lax.optimization_barrier((keep, iterate, forcing))
    last = (2 * columns, depth, LANES)
    first, up, down, forth, back = vmem_call(
        first_kernel,
        (iterate.shape, (4 * steps, cells), (4 * steps, cells), last, last),
        (),
        (iterate_after, forcing_after),
    )
    other, own = vmem_call(
        add_kernel,
        (keep.shape[1:], keep.shape[1:]),
        (place,),
        (keep, received),
        (pltpu.VMEM((4,) + keep.shape[2:], jnp.float32), pltpu.SemaphoreType.DMA((4,))),
        spaces=(pltpu.VMEM, pl.ANY),
    )
    other, up, down, forth, back = lax.optimization_barrier((other, up, down, forth, back))
    forth = shifted(forth, "tm", 1)
    term = swapped(other, "pair", 1)
    field = lax.rem(lax.axis_index("tm"), 2)

    def chosen(array, index):
        return lax.dynamic_index_in_dim(array, index, 0, keepdims=False)

    half = chosen(own, 1 - field) + chosen(term, 1 - field)
    half, forth = lax.optimization_barrier((half, forth))
    half, up, down = lax.optimization_barrier((half, up, down))
    mine = chosen(own, field) + chosen(term, field) + swapped(half, "tm", 1)
    above = shifted(up, ("pair", "core"), 1)
    below = shifted(down, ("pair", "core"), -1)
    mine, above, below, back = lax.optimization_barrier((mine, above, below, back))
    rows = (4 * columns // depth, depth, LANES)
    swept, edge, forth_edge, back_edge = vmem_call(
        functools.partial(second_kernel, steps, slabs),
        (iterate.shape, (4 * steps, cells), rows, rows),
        (place,),
        (first, up, down, above, below),
    )
    back = shifted(back, "tm", -1)
    mask = 2
    while mask < ranks:
        if 2 * mask == ranks:
            mine, back, forth_edge, back_edge = lax.optimization_barrier((mine, back, forth_edge, back_edge))
        mine = mine + swapped(mine, "tm", mask)
        mask *= 2
    forth_edge = shifted(forth_edge, "tm", 1)
    back_edge = shifted(back_edge, "tm", -1)
    mine, forth_edge, back_edge = lax.optimization_barrier((mine, forth_edge, back_edge))
    given = swapped(mine, "tm", 1)
    (coarse,) = vmem_call(
        last_kernel,
        (iterate.shape,),
        (place,),
        (mine, given),
        (pltpu.VMEM((2, depth, cells), jnp.float32), pltpu.SemaphoreType.DMA((2, steps))),
        target=pltpu.HBM,
    )
    (smoothed,) = vmem_call(
        functools.partial(third_kernel, steps, ranks),
        (iterate.shape,),
        (place,),
        (iterate, forcing, swept, edge, forth, back, forth_edge, back_edge),
        cost=8 * 2**20,
    )
    return smoothed, coarse


def solution(mesh):
    ranks, slabs = mesh.shape["tm"], mesh.shape["space"]
    fine = jax.sharding.Mesh(mesh.devices.reshape(ranks, slabs // 2, 2), ("tm", "pair", "core"))
    specs = P(None, "tm", ("pair", "core"), None)
    return jax.shard_map(local, mesh=fine, in_specs=(specs, specs), out_specs=(specs, specs), check_vma=False)
```

```python
import functools

import numpy as np

import jax
import jax.numpy as jnp
from jax import lax
from jax.experimental import pallas as pl
from jax.experimental.pallas import tpu as pltpu
from jax.sharding import PartitionSpec as P

NY = 64
LANES = 128

KAPPA_BASE = 0.25
COUPLING_BASE = 0.5
DAMPING = 0.6


def level_terms(level):
    diffusion = KAPPA_BASE * 2.0**level
    coupling = COUPLING_BASE * 2.0**level
    centre = 1.0 + 6.0 * diffusion
    determinant = centre * centre + coupling * coupling
    along = DAMPING * centre / determinant
    across = DAMPING * coupling / determinant
    return diffusion, coupling, centre, along, across


def coarse_polynomials(total_steps):
    levels = total_steps.bit_length()
    powers = 2 * levels + 1
    unit = np.eye(4 * total_steps).reshape(-1, 2, 2, total_steps)
    fields = np.zeros((4 * total_steps, 2, total_steps, powers))
    source = np.zeros_like(fields)
    fields[..., 0] = unit[:, 0]
    source[..., 0] = unit[:, 1]

    def image(values, diffusion, coupling, centre):
        out = centre * values
        out[..., 1:] -= diffusion * values[..., :-1]
        out[:, 0, 1:] -= values[:, 0, :-1]
        out[:, 1, :-1] -= values[:, 1, 1:]
        out[:, 0] += coupling * values[:, 1]
        out[:, 1] -= coupling * values[:, 0]
        return out

    for level in range(levels):
        diffusion, coupling, centre, along, across = level_terms(level)
        for _ in range(2):
            defect = source - image(fields, diffusion, coupling, centre)
            state, adjoint = defect[:, 0], defect[:, 1]
            fields = fields + np.stack([along * state - across * adjoint, across * state + along * adjoint], 1)
        if level < levels - 1:
            defect = source - image(fields, diffusion, coupling, centre)
            source = defect[:, :, 0::2] + defect[:, :, 1::2]
            fields = np.zeros_like(source)
    return fields[:, :, 0].reshape(2, 2, total_steps, 2, powers)


def lane_index(depth):
    return lax.broadcasted_iota(jnp.int32, (depth, LANES), 1)


def sublane_index(depth):
    return lax.broadcasted_iota(jnp.int32, (depth, LANES), 0)


def column(j):
    return pl.ds(j * LANES, LANES)


def swapped_halves(value):
    return pltpu.roll(value, NY, 1)


def beside(value, lane):
    left = pltpu.roll(jnp.where((lane % NY) != NY - 1, value, 0.0), 1, 1)
    right = pltpu.roll(jnp.where((lane % NY) != 0, value, 0.0), LANES - 1, 1)
    return left + right


def tree_sum(terms):
    while len(terms) > 1:
        terms = [sum(terms[k : k + 2]) for k in range(0, len(terms), 2)]
    return terms[0]


def coarse_kernel(
    powers, steps, slabs, middle, place_ref, weights_hbm, iterate_hbm, forcing_hbm, keep_ref, send_ref, even, odd, packed, iterate_ref, forcing_ref, weights_ref, arrived, weighed
):
    copies = {
        (kind, f, n): pltpu.make_async_copy(source.at[f, n], target.at[f, n], arrived.at[kind, f, n])
        for kind, (source, target) in enumerate(((iterate_hbm, iterate_ref), (forcing_hbm, forcing_ref)))
        for n in range(steps)
        for f in range(2)
    }
    weighing = pltpu.make_async_copy(weights_hbm.at[place_ref[0]], weights_ref, weighed)
    for copy in copies.values():
        copy.start()
    weighing.start()
    even[...] = jnp.zeros_like(even)
    odd[...] = jnp.zeros_like(odd)
    depth, cells = iterate_ref.shape[2:]
    columns = cells // LANES
    rows = cells // NY
    inputs = 2 * steps
    slab, shift = place_ref[1], place_ref[2]
    lane = lane_index(depth)
    low = lane < NY
    zero = jnp.zeros((depth, LANES), jnp.float32)

    def inside(away):
        at = slab + away
        return jnp.where((at >= 0) & (at < slabs), 1.0, 0.0).astype(jnp.float32)

    for kind, ref in enumerate((iterate_ref, forcing_ref)):
        for n in range(steps):
            copies[kind, 0, n].wait()
            copies[kind, 1, n].wait()
            for j in range(columns):
                state, adjoint = ref[0, n, :, column(j)], ref[1, n, :, column(j)]
                state_turned, adjoint_turned = swapped_halves(state), swapped_halves(adjoint)
                k = 2 * (kind * steps + n)
                packed[k, 2 * j] = jnp.where(low, state, adjoint_turned)
                packed[k, 2 * j + 1] = jnp.where(low, state_turned, adjoint)
                packed[k + 1, 2 * j] = jnp.where(low, adjoint, state_turned)
                packed[k + 1, 2 * j + 1] = jnp.where(low, adjoint_turned, state)

    def weights(power):
        return [
            jnp.broadcast_to(weights_ref[pl.ds(power * 2 * inputs + k, 1), :], (depth, LANES)) for k in range(2 * inputs)
        ]

    def injected(factors, i):
        return tree_sum([factor * packed[k, i] for k, factor in enumerate(factors)])

    def advance(source, target, power, reach):
        aways = list(range(-reach, reach + 1))
        masks = [inside(away) for away in aways]
        factors = weights(power)

        def loaded(i):
            if i >= rows:
                return [zero for _ in aways]
            return [source[i, pl.ds((middle + away) * depth, depth), :] for away in aways]

        before = [zero for _ in aways]
        now = loaded(0)
        for i in range(rows):
            later = loaded(i + 1)
            for k, away in enumerate(aways):
                start = (middle + away) * depth
                above = source[i, pl.ds(shift + (start - 1), depth), :]
                below = source[i, pl.ds(shift + (start + 1), depth), :]
                value = (before[k] + later[k]) + beside(now[k], lane) + (above + below)
                if away:
                    value = value * masks[k]
                else:
                    value = value + injected(factors, i)
                target[i, pl.ds(start, depth), :] = value
            before, now = now, later

    weighing.wait()
    factors = weights(powers - 1)
    for i in range(rows):
        even[i, pl.ds(middle * depth, depth), :] = injected(factors, i)
    buffers = (even, odd)
    done = 0
    while done < powers - 1:
        reach = min(done // depth + 1, slabs - 1)
        count = powers - 1 - done if reach == slabs - 1 else min(depth, powers - 1 - done)

        def twice(index, _):
            power = powers - 2 - done - 2 * index
            advance(buffers[0], buffers[1], power, reach)
            advance(buffers[1], buffers[0], power - 1, reach)
            return 0

        lax.fori_loop(0, count // 2, twice, 0)
        done += count
        if count % 2:
            advance(buffers[0], buffers[1], powers - 1 - done, reach)
            buffers = buffers[::-1]

    final = buffers[0]
    bit = lax.rem(slab, 2)
    for half in range(slabs // 2):
        for ref, flag in ((keep_ref, bit), (send_ref, 1 - bit)):
            away = 2 * half + flag - slab
            planes = pl.ds(pl.multiple_of((middle + away) * depth, depth), depth)
            for j in range(columns):
                first, second = final[2 * j, planes, :], final[2 * j + 1, planes, :]
                for f, value in (
                    (0, jnp.where(low, first, swapped_halves(second))),
                    (1, jnp.where(low, swapped_halves(first), second)),
                ):
                    ref[half, f, j] = value


def vmem_call(kernel, out_shapes, smem_inputs, inputs, scratch=(), spaces=None, target=pltpu.VMEM, limit=6, cost=2**20):
    smem = pl.BlockSpec(memory_space=pltpu.SMEM)
    out_shape = tuple(jax.ShapeDtypeStruct(shape, jnp.float32) for shape in out_shapes)
    return pl.pallas_call(
        kernel,
        out_shape=out_shape,
        in_specs=[smem] * len(smem_inputs) + [pl.BlockSpec(memory_space=space) for space in spaces or [pltpu.VMEM] * len(inputs)],
        out_specs=(pl.BlockSpec(memory_space=target),) * len(out_shape),
        scratch_shapes=list(scratch),
        compiler_params=pltpu.CompilerParams(vmem_limit_bytes=limit * 2**20),
        cost_estimate=pl.CostEstimate(flops=10**6, bytes_accessed=cost, transcendentals=0),
    )(*smem_inputs, *inputs)


def coarse_part(place, iterate, forcing):
    steps = iterate.shape[1]
    depth, cells = iterate.shape[2:]
    ranks, slabs = lax.axis_size("tm"), 2 * lax.axis_size("pair")
    table = coarse_polynomials(steps * ranks)
    powers = table.shape[-1]
    table = table.reshape(2, 2, ranks, steps, 2, powers)
    same = np.stack([table[:, 0, :, :, 0], table[:, 1, :, :, 1]], -1)
    other = np.stack([table[:, 1, :, :, 0], table[:, 0, :, :, 1]], -1)
    weights = np.stack([same, other], -2).transpose(1, 3, 0, 2, 4, 5).astype(np.float32)
    reach = min(-(-(powers - 1) // depth), slabs - 1)
    middle = max(reach + 1, slabs - 1)
    weights = np.repeat(weights.reshape(ranks, -1, 2), NY, -1)
    half = (slabs // 2, 2, cells // LANES, depth, LANES)
    buffer = pltpu.VMEM((cells // NY, (2 * middle + 1) * depth, LANES), jnp.float32)
    packed = pltpu.VMEM((4 * steps, cells // NY, depth, LANES), jnp.float32)
    return vmem_call(
        functools.partial(coarse_kernel, powers, steps, slabs, middle),
        (half, half),
        (place,),
        [pltpu.with_memory_space_constraint(array, pltpu.HBM) for array in (jnp.asarray(weights), iterate, forcing)],
        (
            buffer,
            buffer,
            packed,
            pltpu.VMEM(iterate.shape, jnp.float32),
            pltpu.VMEM(forcing.shape, jnp.float32),
            pltpu.VMEM(weights.shape[1:], jnp.float32),
            pltpu.SemaphoreType.DMA((2, 2, steps)),
            pltpu.SemaphoreType.DMA,
        ),
        spaces=(pltpu.HBM,) * 3,
        limit=12,
        cost=24 * 2**20,
    )


def relaxed(fields, around, before, after, source):
    diffusion, coupling, centre, along, across = level_terms(0)
    state, adjoint = fields
    defect_state = source[0] - (centre * state - diffusion * around[0] - before + coupling * adjoint)
    defect_adjoint = source[1] - (centre * adjoint - diffusion * around[1] - after - coupling * state)
    return (
        state + along * defect_state - across * defect_adjoint,
        adjoint + across * defect_state + along * defect_adjoint,
    )


def first_kernel(iterate_ref, forcing_ref, first_ref, up_ref, down_ref, forth_ref, back_ref):
    steps, depth, cells = iterate_ref.shape[1:]
    columns = cells // LANES
    lane, sublane = lane_index(depth), sublane_index(depth)
    low = lane < NY
    zero = jnp.zeros((depth, LANES), jnp.float32)
    slots = [(f, n) for f in range(2) for n in range(steps)]

    def loaded(j):
        return {s: iterate_ref[s[0], s[1], :, column(j)] if j < columns else zero for s in slots}

    now = loaded(0)
    pairs_before = now
    for j in range(columns):
        later = loaded(j + 1)
        pairs = {s: now[s] + later[s] for s in slots}
        around = {}
        for s in slots:
            across_rows = swapped_halves(jnp.where(low, pairs[s], pairs_before[s]))
            above = jnp.where(sublane == 0, 0.0, pltpu.roll(now[s], 1, 0))
            below = jnp.where(sublane == depth - 1, 0.0, pltpu.roll(now[s], depth - 1, 0))
            around[s] = across_rows + beside(now[s], lane) + (above + below)
        for n in range(steps):
            values = relaxed(
                (now[0, n], now[1, n]),
                (around[0, n], around[1, n]),
                now[0, n - 1] if n else zero,
                now[1, n + 1] if n < steps - 1 else zero,
                (forcing_ref[0, n, :, column(j)], forcing_ref[1, n, :, column(j)]),
            )
            for f in range(2):
                first_ref[f, n, :, column(j)] = values[f]
                for ref, field, step in ((forth_ref, 0, steps - 1), (back_ref, 1, 0)):
                    if (f, n) == (field, step):
                        ref[j] = now[f, n]
                        ref[columns + j] = values[f]
                slot = f * steps + n
                for ref, plane in ((up_ref, depth - 1), (down_ref, 0)):
                    ref[slot : slot + 1, column(j)] = now[f, n][plane : plane + 1]
                    slot_after = 2 * steps + slot
                    ref[slot_after : slot_after + 1, column(j)] = values[f][plane : plane + 1]
        now, pairs_before = later, pairs


def second_kernel(
    steps, slabs, place_ref, first_ref, up_ref, down_ref, above_ref, below_ref, swept_ref, edge_ref, forth_ref, back_ref
):
    diffusion, _, _, along, across = level_terms(0)
    depth, cells = first_ref.shape[2:]
    columns = cells // LANES
    slab = place_ref[1]
    sublane = sublane_index(depth)
    count = 2 * steps
    has_above = jnp.where(slab > 0, 1.0, 0.0).astype(jnp.float32)
    has_below = jnp.where(slab < slabs - 1, 1.0, 0.0).astype(jnp.float32)

    def mixed(rows):
        state, adjoint = rows[:steps], rows[steps:]
        return jnp.concatenate(
            [
                (along * diffusion) * state - (across * diffusion) * adjoint,
                (across * diffusion) * state + (along * diffusion) * adjoint,
            ],
            0,
        )

    def one(j):
        return slice(j * LANES, (j + 1) * LANES)

    for j in range(columns):
        from_above, from_below = above_ref[:, one(j)], below_ref[:, one(j)]
        edge_ref[:count, one(j)] = (from_above[count:] + mixed(down_ref[:count, one(j)])) * has_above
        edge_ref[count:, one(j)] = (from_below[count:] + mixed(up_ref[:count, one(j)])) * has_below
        add_above, add_below = mixed(from_above[:count]), mixed(from_below[:count])
        for f in range(2):
            for n in range(steps):
                k = f * steps + n
                value = first_ref[f, n, :, one(j)]
                value = value + jnp.where(sublane == 0, add_above[k : k + 1], 0.0)
                value = value + jnp.where(sublane == depth - 1, add_below[k : k + 1], 0.0)
                swept_ref[f, n, :, one(j)] = value
                for ref, step in ((forth_ref, steps - 1), (back_ref, 0)):
                    if n == step:
                        for side, rows in enumerate((from_above, from_below)):
                            block, row = (2 * side + f) * (columns // depth) + j // depth, j % depth
                            ref[block, row : row + 1] = rows[k : k + 1]


def third_kernel(
    steps, ranks, place_ref, iterate_ref, forcing_ref, swept_ref, edge_ref, forth_ref, back_ref, forth_edge_ref, back_edge_ref, out_ref
):
    diffusion, _, _, along, across = level_terms(0)
    depth, cells = iterate_ref.shape[2:]
    columns = cells // LANES
    rank = place_ref[0]
    lane, sublane = lane_index(depth), sublane_index(depth)
    low = lane < NY
    zero = jnp.zeros((depth, LANES), jnp.float32)
    slots = [(f, n) for f in range(2) for n in range(steps)]
    has_before = jnp.where(rank > 0, 1.0, 0.0).astype(jnp.float32)
    has_after = jnp.where(rank < ranks - 1, 1.0, 0.0).astype(jnp.float32)
    gain = {(0, 0): ("forth", along), (1, 0): ("forth", across), (0, steps - 1): ("back", -across), (1, steps - 1): ("back", along)}

    def loaded(j):
        if j >= columns:
            return {s: zero for s in slots}
        near = {"forth": forth_ref[j], "back": back_ref[j]}
        values = {}
        for s in slots:
            values[s] = swept_ref[s[0], s[1], :, column(j)]
            if s in gain:
                values[s] = values[s] + gain[s][1] * near[gain[s][0]]
        return values

    def edge_row(ref, j, side, f):
        block, row = (2 * side + f) * (columns // depth) + j // depth, j % depth
        return ref[block, row : row + 1]

    def edges(j, side):
        near = {"forth": edge_row(forth_edge_ref, j, side, 0), "back": edge_row(back_edge_ref, j, side, 1)}
        values = {}
        for s in slots:
            k = side * 2 * steps + s[0] * steps + s[1]
            values[s] = edge_ref[k : k + 1, column(j)]
            if s in gain:
                values[s] = values[s] + gain[s][1] * near[gain[s][0]]
        return values

    now = loaded(0)
    pairs_before = now
    for j in range(columns):
        later = loaded(j + 1)
        over, under = edges(j, 0), edges(j, 1)
        pairs = {s: now[s] + later[s] for s in slots}
        around = {}
        for s in slots:
            across_rows = swapped_halves(jnp.where(low, pairs[s], pairs_before[s]))
            above = jnp.where(sublane == 0, over[s], pltpu.roll(now[s], 1, 0))
            below = jnp.where(sublane == depth - 1, under[s], pltpu.roll(now[s], depth - 1, 0))
            around[s] = across_rows + beside(now[s], lane) + (above + below)
        before = forth_ref[columns + j] - across * iterate_ref[1, 0, :, column(j)]
        after = back_ref[columns + j] + across * iterate_ref[0, steps - 1, :, column(j)]
        for side, at in ((0, sublane == 0), (1, sublane == depth - 1)):
            state, adjoint = (edge_row(forth_edge_ref, j, side, f) for f in range(2))
            before = before + jnp.where(at, (along * diffusion) * state - (across * diffusion) * adjoint, 0.0)
            state, adjoint = (edge_row(back_edge_ref, j, side, f) for f in range(2))
            after = after + jnp.where(at, (across * diffusion) * state + (along * diffusion) * adjoint, 0.0)
        before, after = before * has_before, after * has_after
        for n in range(steps):
            values = relaxed(
                (now[0, n], now[1, n]),
                (around[0, n], around[1, n]),
                now[0, n - 1] if n else before,
                now[1, n + 1] if n < steps - 1 else after,
                (forcing_ref[0, n, :, column(j)], forcing_ref[1, n, :, column(j)]),
            )
            for f in range(2):
                out_ref[f, n, :, column(j)] = values[f]
        now, pairs_before = later, pairs


def swapped(value, axis, mask):
    return lax.ppermute(value, axis, [(i, i ^ mask) for i in range(lax.axis_size(axis))])


def shifted(value, axis, by):
    size = lax.axis_size(axis)
    return lax.ppermute(value, axis, [(i, i + by) for i in range(size) if 0 <= i + by < size])


def add_kernel(place_ref, keep_ref, received_any, other_ref, own_ref, received_ref, arrived):
    pair = lax.div(place_ref[1], 2)
    parts = [(index, f) for index in (1 - pair, pair) for f in range(2)]
    copies = [
        pltpu.make_async_copy(received_any.at[index, f], received_ref.at[k], arrived.at[k])
        for k, (index, f) in enumerate(parts)
    ]
    for copy in copies:
        copy.start()
    for k, (index, f) in enumerate(parts):
        copies[k].wait()
        (other_ref, own_ref)[k // 2][f] = keep_ref[index, f] + received_ref[k]


def last_kernel(place_ref, mine_ref, given_ref, out_hbm, whole_ref, left):
    steps = out_hbm.shape[1]
    field = lax.rem(place_ref[0], 2)
    copies = []
    for k, (ref, f) in enumerate(((mine_ref, field), (given_ref, 1 - field))):
        for j in range(ref.shape[0]):
            whole_ref[k, :, column(j)] = ref[j]
        for n in range(steps):
            copies.append(pltpu.make_async_copy(whole_ref.at[k], out_hbm.at[f, n], left.at[k, n]))
            copies[-1].start()
    for copy in copies:
        copy.wait()


def local(iterate, forcing):
    steps, depth, cells = iterate.shape[1:]
    columns = cells // LANES
    ranks, slabs = lax.axis_size("tm"), 2 * lax.axis_size("pair")
    place = jnp.stack([lax.axis_index("tm"), lax.axis_index(("pair", "core")), jnp.zeros((), jnp.int32)]).astype(jnp.int32)
    keep, send = coarse_part(place, iterate, forcing)
    received = lax.ppermute(send, "core", [(0, 1), (1, 0)])

    keep, iterate_after, forcing_after = lax.optimization_barrier((keep, iterate, forcing))
    last = (2 * columns, depth, LANES)
    first, up, down, forth, back = vmem_call(
        first_kernel,
        (iterate.shape, (4 * steps, cells), (4 * steps, cells), last, last),
        (),
        (iterate_after, forcing_after),
    )
    other, own = vmem_call(
        add_kernel,
        (keep.shape[1:], keep.shape[1:]),
        (place,),
        (keep, received),
        (pltpu.VMEM((4,) + keep.shape[2:], jnp.float32), pltpu.SemaphoreType.DMA((4,))),
        spaces=(pltpu.VMEM, pl.ANY),
    )
    other, up, down, forth, back = lax.optimization_barrier((other, up, down, forth, back))
    forth = shifted(forth, "tm", 1)
    above = shifted(up, ("pair", "core"), 1)
    below = shifted(down, ("pair", "core"), -1)
    term = swapped(other, "pair", 1)
    field = lax.rem(lax.axis_index("tm"), 2)

    def chosen(array, index):
        return lax.dynamic_index_in_dim(array, index, 0, keepdims=False)

    half = chosen(own, 1 - field) + chosen(term, 1 - field)
    half, forth, above, below, back = lax.optimization_barrier((half, forth, above, below, back))
    back = shifted(back, "tm", -1)
    mine = chosen(own, field) + chosen(term, field) + swapped(half, "tm", 1)
    rows = (4 * columns // depth, depth, LANES)
    swept, edge, forth_edge, back_edge = vmem_call(
        functools.partial(second_kernel, steps, slabs),
        (iterate.shape, (4 * steps, cells), rows, rows),
        (place,),
        (first, up, down, above, below),
    )
    mine, forth_edge, back_edge = lax.optimization_barrier((mine, forth_edge, back_edge))
    forth_edge = shifted(forth_edge, "tm", 1)
    back_edge = shifted(back_edge, "tm", -1)
    mask = 2
    while mask < ranks:
        if 2 * mask == ranks:
            mine, back, forth_edge, back_edge = lax.optimization_barrier((mine, back, forth_edge, back_edge))
        mine = mine + swapped(mine, "tm", mask)
        mask *= 2
    given = swapped(mine, "tm", 1)
    (coarse,) = vmem_call(
        last_kernel,
        (iterate.shape,),
        (place,),
        (mine, given),
        (pltpu.VMEM((2, depth, cells), jnp.float32), pltpu.SemaphoreType.DMA((2, steps))),
        target=pltpu.HBM,
    )
    (smoothed,) = vmem_call(
        functools.partial(third_kernel, steps, ranks),
        (iterate.shape,),
        (place,),
        (iterate, forcing, swept, edge, forth, back, forth_edge, back_edge),
        cost=8 * 2**20,
    )
    return smoothed, coarse


def solution(mesh):
    ranks, slabs = mesh.shape["tm"], mesh.shape["space"]
    fine = jax.sharding.Mesh(mesh.devices.reshape(ranks, slabs // 2, 2), ("tm", "pair", "core"))
    specs = P(None, "tm", ("pair", "core"), None)
    return jax.shard_map(local, mesh=fine, in_specs=(specs, specs), out_specs=(specs, specs), check_vma=False)
```

```python
import functools

import numpy as np

import jax
import jax.numpy as jnp
from jax import lax
from jax.experimental import pallas as pl
from jax.experimental.pallas import tpu as pltpu
from jax.sharding import PartitionSpec as P

NY = 64
LANES = 128

KAPPA_BASE = 0.25
COUPLING_BASE = 0.5
DAMPING = 0.6


def level_terms(level):
    diffusion = KAPPA_BASE * 2.0**level
    coupling = COUPLING_BASE * 2.0**level
    centre = 1.0 + 6.0 * diffusion
    determinant = centre * centre + coupling * coupling
    along = DAMPING * centre / determinant
    across = DAMPING * coupling / determinant
    return diffusion, coupling, centre, along, across


def coarse_polynomials(total_steps):
    levels = total_steps.bit_length()
    powers = 2 * levels + 1
    unit = np.eye(4 * total_steps).reshape(-1, 2, 2, total_steps)
    fields = np.zeros((4 * total_steps, 2, total_steps, powers))
    source = np.zeros_like(fields)
    fields[..., 0] = unit[:, 0]
    source[..., 0] = unit[:, 1]

    def image(values, diffusion, coupling, centre):
        out = centre * values
        out[..., 1:] -= diffusion * values[..., :-1]
        out[:, 0, 1:] -= values[:, 0, :-1]
        out[:, 1, :-1] -= values[:, 1, 1:]
        out[:, 0] += coupling * values[:, 1]
        out[:, 1] -= coupling * values[:, 0]
        return out

    for level in range(levels):
        diffusion, coupling, centre, along, across = level_terms(level)
        for _ in range(2):
            defect = source - image(fields, diffusion, coupling, centre)
            state, adjoint = defect[:, 0], defect[:, 1]
            fields = fields + np.stack([along * state - across * adjoint, across * state + along * adjoint], 1)
        if level < levels - 1:
            defect = source - image(fields, diffusion, coupling, centre)
            source = defect[:, :, 0::2] + defect[:, :, 1::2]
            fields = np.zeros_like(source)
    return fields[:, :, 0].reshape(2, 2, total_steps, 2, powers)


def lane_index(depth):
    return lax.broadcasted_iota(jnp.int32, (depth, LANES), 1)


def sublane_index(depth):
    return lax.broadcasted_iota(jnp.int32, (depth, LANES), 0)


def column(j):
    return pl.ds(j * LANES, LANES)


def swapped_halves(value):
    return pltpu.roll(value, NY, 1)


def beside(value, lane):
    left = pltpu.roll(jnp.where((lane % NY) != NY - 1, value, 0.0), 1, 1)
    right = pltpu.roll(jnp.where((lane % NY) != 0, value, 0.0), LANES - 1, 1)
    return left + right


def tree_sum(terms):
    while len(terms) > 1:
        terms = [sum(terms[k : k + 2]) for k in range(0, len(terms), 2)]
    return terms[0]


def coarse_kernel(
    powers, steps, slabs, middle, place_ref, weights_hbm, iterate_hbm, forcing_hbm, keep_ref, send_ref, even, odd, packed, iterate_ref, forcing_ref, weights_ref, arrived, weighed
):
    copies = {
        (kind, f, n): pltpu.make_async_copy(source.at[f, n], target.at[f, n], arrived.at[kind, f, n])
        for kind, (source, target) in enumerate(((iterate_hbm, iterate_ref), (forcing_hbm, forcing_ref)))
        for n in range(steps)
        for f in range(2)
    }
    weighing = pltpu.make_async_copy(weights_hbm.at[place_ref[0]], weights_ref, weighed)
    for copy in copies.values():
        copy.start()
    weighing.start()
    even[...] = jnp.zeros_like(even)
    odd[...] = jnp.zeros_like(odd)
    depth, cells = iterate_ref.shape[2:]
    columns = cells // LANES
    rows = cells // NY
    inputs = 2 * steps
    slab, shift = place_ref[1], place_ref[2]
    lane = lane_index(depth)
    low = lane < NY
    zero = jnp.zeros((depth, LANES), jnp.float32)

    def inside(away):
        at = slab + away
        return jnp.where((at >= 0) & (at < slabs), 1.0, 0.0).astype(jnp.float32)

    for kind, ref in enumerate((iterate_ref, forcing_ref)):
        for n in range(steps):
            copies[kind, 0, n].wait()
            copies[kind, 1, n].wait()
            for j in range(columns):
                state, adjoint = ref[0, n, :, column(j)], ref[1, n, :, column(j)]
                state_turned, adjoint_turned = swapped_halves(state), swapped_halves(adjoint)
                k = 2 * (kind * steps + n)
                packed[k, 2 * j] = jnp.where(low, state, adjoint_turned)
                packed[k, 2 * j + 1] = jnp.where(low, state_turned, adjoint)
                packed[k + 1, 2 * j] = jnp.where(low, adjoint, state_turned)
                packed[k + 1, 2 * j + 1] = jnp.where(low, adjoint_turned, state)

    def weights(power):
        return [
            jnp.broadcast_to(weights_ref[pl.ds(power * 2 * inputs + k, 1), :], (depth, LANES)) for k in range(2 * inputs)
        ]

    def injected(factors, i):
        return tree_sum([factor * packed[k, i] for k, factor in enumerate(factors)])

    def advance(source, target, power, reach):
        aways = list(range(-reach, reach + 1))
        masks = [inside(away) for away in aways]
        factors = weights(power)

        def loaded(i):
            if i >= rows:
                return [zero for _ in aways]
            return [source[i, pl.ds((middle + away) * depth, depth), :] for away in aways]

        before = [zero for _ in aways]
        now = loaded(0)
        for i in range(rows):
            later = loaded(i + 1)
            for k, away in enumerate(aways):
                start = (middle + away) * depth
                above = source[i, pl.ds(shift + (start - 1), depth), :]
                below = source[i, pl.ds(shift + (start + 1), depth), :]
                value = (before[k] + later[k]) + beside(now[k], lane) + (above + below)
                if away:
                    value = value * masks[k]
                else:
                    value = value + injected(factors, i)
                target[i, pl.ds(start, depth), :] = value
            before, now = now, later

    weighing.wait()
    factors = weights(powers - 1)
    for i in range(rows):
        even[i, pl.ds(middle * depth, depth), :] = injected(factors, i)
    buffers = (even, odd)
    done = 0
    while done < powers - 1:
        reach = min(done // depth + 1, slabs - 1)
        count = powers - 1 - done if reach == slabs - 1 else min(depth, powers - 1 - done)

        def twice(index, _):
            power = powers - 2 - done - 2 * index
            advance(buffers[0], buffers[1], power, reach)
            advance(buffers[1], buffers[0], power - 1, reach)
            return 0

        lax.fori_loop(0, count // 2, twice, 0)
        done += count
        if count % 2:
            advance(buffers[0], buffers[1], powers - 1 - done, reach)
            buffers = buffers[::-1]

    final = buffers[0]
    bit = lax.rem(slab, 2)
    for half in range(slabs // 2):
        for ref, flag in ((keep_ref, bit), (send_ref, 1 - bit)):
            away = 2 * half + flag - slab
            planes = pl.ds(pl.multiple_of((middle + away) * depth, depth), depth)
            for j in range(columns):
                first, second = final[2 * j, planes, :], final[2 * j + 1, planes, :]
                for f, value in (
                    (0, jnp.where(low, first, swapped_halves(second))),
                    (1, jnp.where(low, swapped_halves(first), second)),
                ):
                    ref[half, f, j] = value


def vmem_call(kernel, out_shapes, smem_inputs, inputs, scratch=(), spaces=None, limit=6, cost=2**20):
    smem = pl.BlockSpec(memory_space=pltpu.SMEM)
    vmem = pl.BlockSpec(memory_space=pltpu.VMEM)
    out_shape = tuple(jax.ShapeDtypeStruct(shape, jnp.float32) for shape in out_shapes)
    return pl.pallas_call(
        kernel,
        out_shape=out_shape,
        in_specs=[smem] * len(smem_inputs) + [pl.BlockSpec(memory_space=space) for space in spaces or [pltpu.VMEM] * len(inputs)],
        out_specs=(vmem,) * len(out_shape),
        scratch_shapes=list(scratch),
        compiler_params=pltpu.CompilerParams(vmem_limit_bytes=limit * 2**20),
        cost_estimate=pl.CostEstimate(flops=10**6, bytes_accessed=cost, transcendentals=0),
    )(*smem_inputs, *inputs)


def coarse_part(place, iterate, forcing):
    steps = iterate.shape[1]
    depth, cells = iterate.shape[2:]
    ranks, slabs = lax.axis_size("tm"), 2 * lax.axis_size("pair")
    table = coarse_polynomials(steps * ranks)
    powers = table.shape[-1]
    table = table.reshape(2, 2, ranks, steps, 2, powers)
    same = np.stack([table[:, 0, :, :, 0], table[:, 1, :, :, 1]], -1)
    other = np.stack([table[:, 1, :, :, 0], table[:, 0, :, :, 1]], -1)
    weights = np.stack([same, other], -2).transpose(1, 3, 0, 2, 4, 5).astype(np.float32)
    reach = min(-(-(powers - 1) // depth), slabs - 1)
    middle = max(reach + 1, slabs - 1)
    weights = np.repeat(weights.reshape(ranks, -1, 2), NY, -1)
    half = (slabs // 2, 2, cells // LANES, depth, LANES)
    buffer = pltpu.VMEM((cells // NY, (2 * middle + 1) * depth, LANES), jnp.float32)
    packed = pltpu.VMEM((4 * steps, cells // NY, depth, LANES), jnp.float32)
    return vmem_call(
        functools.partial(coarse_kernel, powers, steps, slabs, middle),
        (half, half),
        (place,),
        [pltpu.with_memory_space_constraint(array, pltpu.HBM) for array in (jnp.asarray(weights), iterate, forcing)],
        (
            buffer,
            buffer,
            packed,
            pltpu.VMEM(iterate.shape, jnp.float32),
            pltpu.VMEM(forcing.shape, jnp.float32),
            pltpu.VMEM(weights.shape[1:], jnp.float32),
            pltpu.SemaphoreType.DMA((2, 2, steps)),
            pltpu.SemaphoreType.DMA,
        ),
        spaces=(pltpu.HBM,) * 3,
        limit=12,
        cost=24 * 2**20,
    )


def relaxed(fields, around, before, after, source):
    diffusion, coupling, centre, along, across = level_terms(0)
    state, adjoint = fields
    defect_state = source[0] - (centre * state - diffusion * around[0] - before + coupling * adjoint)
    defect_adjoint = source[1] - (centre * adjoint - diffusion * around[1] - after - coupling * state)
    return (
        state + along * defect_state - across * defect_adjoint,
        adjoint + across * defect_state + along * defect_adjoint,
    )


def first_kernel(iterate_ref, forcing_ref, first_ref, up_ref, down_ref):
    steps, depth, cells = iterate_ref.shape[1:]
    columns = cells // LANES
    lane, sublane = lane_index(depth), sublane_index(depth)
    low = lane < NY
    zero = jnp.zeros((depth, LANES), jnp.float32)
    slots = [(f, n) for f in range(2) for n in range(steps)]

    def loaded(j):
        return {s: iterate_ref[s[0], s[1], :, column(j)] if j < columns else zero for s in slots}

    now = loaded(0)
    pairs_before = now
    for j in range(columns):
        later = loaded(j + 1)
        pairs = {s: now[s] + later[s] for s in slots}
        around = {}
        for s in slots:
            across_rows = swapped_halves(jnp.where(low, pairs[s], pairs_before[s]))
            above = jnp.where(sublane == 0, 0.0, pltpu.roll(now[s], 1, 0))
            below = jnp.where(sublane == depth - 1, 0.0, pltpu.roll(now[s], depth - 1, 0))
            around[s] = across_rows + beside(now[s], lane) + (above + below)
        for n in range(steps):
            values = relaxed(
                (now[0, n], now[1, n]),
                (around[0, n], around[1, n]),
                now[0, n - 1] if n else zero,
                now[1, n + 1] if n < steps - 1 else zero,
                (forcing_ref[0, n, :, column(j)], forcing_ref[1, n, :, column(j)]),
            )
            for f in range(2):
                first_ref[f, n, :, column(j)] = values[f]
                slot = f * steps + n
                for ref, plane in ((up_ref, depth - 1), (down_ref, 0)):
                    ref[slot : slot + 1, column(j)] = now[f, n][plane : plane + 1]
                    slot_after = 2 * steps + slot
                    ref[slot_after : slot_after + 1, column(j)] = values[f][plane : plane + 1]
        now, pairs_before = later, pairs


def second_kernel(
    steps, slabs, place_ref, iterate_ref, first_ref, up_ref, down_ref, above_ref, below_ref, swept_ref, edge_ref, forth_ref, back_ref
):
    diffusion, _, _, along, across = level_terms(0)
    depth, cells = iterate_ref.shape[2:]
    columns = cells // LANES
    slab = place_ref[1]
    sublane = sublane_index(depth)
    count = 2 * steps
    has_above = jnp.where(slab > 0, 1.0, 0.0).astype(jnp.float32)
    has_below = jnp.where(slab < slabs - 1, 1.0, 0.0).astype(jnp.float32)

    def mixed(rows):
        state, adjoint = rows[:steps], rows[steps:]
        return jnp.concatenate(
            [
                (along * diffusion) * state - (across * diffusion) * adjoint,
                (across * diffusion) * state + (along * diffusion) * adjoint,
            ],
            0,
        )

    def one(j):
        return slice(j * LANES, (j + 1) * LANES)

    for j in range(columns):
        from_above, from_below = above_ref[:, one(j)], below_ref[:, one(j)]
        edge_ref[:count, one(j)] = (from_above[count:] + mixed(down_ref[:count, one(j)])) * has_above
        edge_ref[count:, one(j)] = (from_below[count:] + mixed(up_ref[:count, one(j)])) * has_below
        add_above, add_below = mixed(from_above[:count]), mixed(from_below[:count])
        for f in range(2):
            for n in range(steps):
                k = f * steps + n
                value = first_ref[f, n, :, one(j)]
                value = value + jnp.where(sublane == 0, add_above[k : k + 1], 0.0)
                value = value + jnp.where(sublane == depth - 1, add_below[k : k + 1], 0.0)
                swept_ref[f, n, :, one(j)] = value
                for ref, field, step in ((forth_ref, 0, steps - 1), (back_ref, 1, 0)):
                    if (f, n) == (field, step):
                        ref[j] = iterate_ref[f, n, :, one(j)]
                        ref[columns + j] = value
                        block, row = 2 * columns + j // depth, j % depth
                        ref[block, row : row + 1] = from_above[k : k + 1]
                        block += columns // depth
                        ref[block, row : row + 1] = from_below[k : k + 1]


def third_kernel(steps, ranks, place_ref, iterate_ref, forcing_ref, swept_ref, edge_ref, forth_ref, back_ref, out_ref):
    _, _, _, along, across = level_terms(0)
    depth, cells = iterate_ref.shape[2:]
    columns = cells // LANES
    rank = place_ref[0]
    lane, sublane = lane_index(depth), sublane_index(depth)
    low = lane < NY
    zero = jnp.zeros((depth, LANES), jnp.float32)
    slots = [(f, n) for f in range(2) for n in range(steps)]
    has_before = jnp.where(rank > 0, 1.0, 0.0).astype(jnp.float32)
    has_after = jnp.where(rank < ranks - 1, 1.0, 0.0).astype(jnp.float32)
    gain = {(0, 0): ("forth", along), (1, 0): ("forth", across), (0, steps - 1): ("back", -across), (1, steps - 1): ("back", along)}

    def loaded(j):
        if j >= columns:
            return {s: zero for s in slots}
        near = {"forth": forth_ref[j], "back": back_ref[j]}
        values = {}
        for s in slots:
            values[s] = swept_ref[s[0], s[1], :, column(j)]
            if s in gain:
                values[s] = values[s] + gain[s][1] * near[gain[s][0]]
        return values

    def edges(j, side):
        block, row = 2 * columns + side * (columns // depth) + j // depth, j % depth
        near = {"forth": forth_ref[block, row : row + 1], "back": back_ref[block, row : row + 1]}
        values = {}
        for s in slots:
            k = side * 2 * steps + s[0] * steps + s[1]
            values[s] = edge_ref[k : k + 1, column(j)]
            if s in gain:
                values[s] = values[s] + gain[s][1] * near[gain[s][0]]
        return values

    now = loaded(0)
    pairs_before = now
    for j in range(columns):
        later = loaded(j + 1)
        over, under = edges(j, 0), edges(j, 1)
        pairs = {s: now[s] + later[s] for s in slots}
        around = {}
        for s in slots:
            across_rows = swapped_halves(jnp.where(low, pairs[s], pairs_before[s]))
            above = jnp.where(sublane == 0, over[s], pltpu.roll(now[s], 1, 0))
            below = jnp.where(sublane == depth - 1, under[s], pltpu.roll(now[s], depth - 1, 0))
            around[s] = across_rows + beside(now[s], lane) + (above + below)
        before = (forth_ref[columns + j] - across * iterate_ref[1, 0, :, column(j)]) * has_before
        after = (back_ref[columns + j] + across * iterate_ref[0, steps - 1, :, column(j)]) * has_after
        for n in range(steps):
            values = relaxed(
                (now[0, n], now[1, n]),
                (around[0, n], around[1, n]),
                now[0, n - 1] if n else before,
                now[1, n + 1] if n < steps - 1 else after,
                (forcing_ref[0, n, :, column(j)], forcing_ref[1, n, :, column(j)]),
            )
            for f in range(2):
                out_ref[f, n, :, column(j)] = values[f]
        now, pairs_before = later, pairs


def swapped(value, axis, mask):
    return lax.ppermute(value, axis, [(i, i ^ mask) for i in range(lax.axis_size(axis))])


def shifted(value, axis, by):
    size = lax.axis_size(axis)
    return lax.ppermute(value, axis, [(i, i + by) for i in range(size) if 0 <= i + by < size])


def add_kernel(place_ref, keep_ref, received_any, other_ref, own_ref, received_ref, arrived):
    pair = lax.div(place_ref[1], 2)
    parts = [(index, f) for index in (1 - pair, pair) for f in range(2)]
    copies = [
        pltpu.make_async_copy(received_any.at[index, f], received_ref.at[k], arrived.at[k])
        for k, (index, f) in enumerate(parts)
    ]
    for copy in copies:
        copy.start()
    for k, (index, f) in enumerate(parts):
        copies[k].wait()
        (other_ref, own_ref)[k // 2][f] = keep_ref[index, f] + received_ref[k]


def last_kernel(place_ref, mine_ref, given_ref, out_ref):
    steps = out_ref.shape[1]
    field = lax.rem(place_ref[0], 2)
    for j in range(mine_ref.shape[0]):
        for n in range(steps):
            out_ref[field, n, :, column(j)] = mine_ref[j]
            out_ref[1 - field, n, :, column(j)] = given_ref[j]


def local(iterate, forcing):
    steps, depth, cells = iterate.shape[1:]
    columns = cells // LANES
    ranks, slabs = lax.axis_size("tm"), 2 * lax.axis_size("pair")
    place = jnp.stack([lax.axis_index("tm"), lax.axis_index(("pair", "core")), jnp.zeros((), jnp.int32)]).astype(jnp.int32)
    keep, send = coarse_part(place, iterate, forcing)
    received = lax.ppermute(send, "core", [(0, 1), (1, 0)])

    keep, iterate_after, forcing_after = lax.optimization_barrier((keep, iterate, forcing))
    first, up, down = vmem_call(
        first_kernel, (iterate.shape, (4 * steps, cells), (4 * steps, cells)), (), (iterate_after, forcing_after)
    )
    other, own = vmem_call(
        add_kernel,
        (keep.shape[1:], keep.shape[1:]),
        (place,),
        (keep, received),
        (pltpu.VMEM((4,) + keep.shape[2:], jnp.float32), pltpu.SemaphoreType.DMA((4,))),
        spaces=(pltpu.VMEM, pl.ANY),
    )
    other, up, down = lax.optimization_barrier((other, up, down))
    above = shifted(up, ("pair", "core"), 1)
    below = shifted(down, ("pair", "core"), -1)
    term = swapped(other, "pair", 1)
    field = lax.rem(lax.axis_index("tm"), 2)

    def chosen(array, index):
        return lax.dynamic_index_in_dim(array, index, 0, keepdims=False)

    half = chosen(own, 1 - field) + chosen(term, 1 - field)
    half, above, below = lax.optimization_barrier((half, above, below))
    mine = chosen(own, field) + chosen(term, field) + swapped(half, "tm", 1)
    payload = (2 * columns + 2 * columns // depth, depth, LANES)
    swept, edge, forth, back = vmem_call(
        functools.partial(second_kernel, steps, slabs),
        (iterate.shape, (4 * steps, cells), payload, payload),
        (place,),
        (iterate, first, up, down, above, below),
    )
    mine, _, _ = lax.optimization_barrier((mine, forth, back))
    mask = 2
    while mask < ranks:
        mine = mine + swapped(mine, "tm", mask)
        mask *= 2
    forth = shifted(forth, "tm", 1)
    back = shifted(back, "tm", -1)
    mine, forth, back = lax.optimization_barrier((mine, forth, back))
    given = swapped(mine, "tm", 1)
    (coarse,) = vmem_call(last_kernel, (iterate.shape,), (place,), (mine, given))
    (smoothed,) = vmem_call(
        functools.partial(third_kernel, steps, ranks),
        (iterate.shape,),
        (place,),
        (iterate, forcing, swept, edge, forth, back),
        cost=64 * 2**20,
    )
    return smoothed, coarse


def solution(mesh):
    ranks, slabs = mesh.shape["tm"], mesh.shape["space"]
    fine = jax.sharding.Mesh(mesh.devices.reshape(ranks, slabs // 2, 2), ("tm", "pair", "core"))
    specs = P(None, "tm", ("pair", "core"), None)
    return jax.shard_map(local, mesh=fine, in_specs=(specs, specs), out_specs=(specs, specs), check_vma=False)
```

```python
import functools

import numpy as np

import jax
import jax.numpy as jnp
from jax import lax
from jax.experimental import pallas as pl
from jax.experimental.pallas import tpu as pltpu
from jax.sharding import PartitionSpec as P

NY = 64
LANES = 128

KAPPA_BASE = 0.25
COUPLING_BASE = 0.5
DAMPING = 0.6


def level_terms(level):
    diffusion = KAPPA_BASE * 2.0**level
    coupling = COUPLING_BASE * 2.0**level
    centre = 1.0 + 6.0 * diffusion
    determinant = centre * centre + coupling * coupling
    along = DAMPING * centre / determinant
    across = DAMPING * coupling / determinant
    return diffusion, coupling, centre, along, across


def coarse_polynomials(total_steps):
    levels = total_steps.bit_length()
    powers = 2 * levels + 1
    unit = np.eye(4 * total_steps).reshape(-1, 2, 2, total_steps)
    fields = np.zeros((4 * total_steps, 2, total_steps, powers))
    source = np.zeros_like(fields)
    fields[..., 0] = unit[:, 0]
    source[..., 0] = unit[:, 1]

    def image(values, diffusion, coupling, centre):
        out = centre * values
        out[..., 1:] -= diffusion * values[..., :-1]
        out[:, 0, 1:] -= values[:, 0, :-1]
        out[:, 1, :-1] -= values[:, 1, 1:]
        out[:, 0] += coupling * values[:, 1]
        out[:, 1] -= coupling * values[:, 0]
        return out

    for level in range(levels):
        diffusion, coupling, centre, along, across = level_terms(level)
        for _ in range(2):
            defect = source - image(fields, diffusion, coupling, centre)
            state, adjoint = defect[:, 0], defect[:, 1]
            fields = fields + np.stack([along * state - across * adjoint, across * state + along * adjoint], 1)
        if level < levels - 1:
            defect = source - image(fields, diffusion, coupling, centre)
            source = defect[:, :, 0::2] + defect[:, :, 1::2]
            fields = np.zeros_like(source)
    return fields[:, :, 0].reshape(2, 2, total_steps, 2, powers)


def lane_index(depth):
    return lax.broadcasted_iota(jnp.int32, (depth, LANES), 1)


def sublane_index(depth):
    return lax.broadcasted_iota(jnp.int32, (depth, LANES), 0)


def column(j):
    return pl.ds(j * LANES, LANES)


def swapped_halves(value):
    return pltpu.roll(value, NY, 1)


def beside(value, lane):
    left = pltpu.roll(jnp.where((lane % NY) != NY - 1, value, 0.0), 1, 1)
    right = pltpu.roll(jnp.where((lane % NY) != 0, value, 0.0), LANES - 1, 1)
    return left + right


def tree_sum(terms):
    while len(terms) > 1:
        terms = [sum(terms[k : k + 2]) for k in range(0, len(terms), 2)]
    return terms[0]


def coarse_kernel(
    powers, steps, slabs, middle, place_ref, weights_hbm, iterate_hbm, forcing_hbm, keep_ref, send_ref, even, odd, packed, iterate_ref, forcing_ref, weights_ref, arrived, weighed
):
    copies = {
        (kind, f, n): pltpu.make_async_copy(source.at[f, n], target.at[f, n], arrived.at[kind, f, n])
        for kind, (source, target) in enumerate(((iterate_hbm, iterate_ref), (forcing_hbm, forcing_ref)))
        for n in range(steps)
        for f in range(2)
    }
    weighing = pltpu.make_async_copy(weights_hbm.at[place_ref[0]], weights_ref, weighed)
    for copy in copies.values():
        copy.start()
    weighing.start()
    even[...] = jnp.zeros_like(even)
    odd[...] = jnp.zeros_like(odd)
    depth, cells = iterate_ref.shape[2:]
    columns = cells // LANES
    rows = cells // NY
    inputs = 2 * steps
    slab, shift = place_ref[1], place_ref[2]
    lane = lane_index(depth)
    low = lane < NY
    zero = jnp.zeros((depth, LANES), jnp.float32)

    def inside(away):
        at = slab + away
        return jnp.where((at >= 0) & (at < slabs), 1.0, 0.0).astype(jnp.float32)

    for kind, ref in enumerate((iterate_ref, forcing_ref)):
        for n in range(steps):
            copies[kind, 0, n].wait()
            copies[kind, 1, n].wait()
            for j in range(columns):
                state, adjoint = ref[0, n, :, column(j)], ref[1, n, :, column(j)]
                state_turned, adjoint_turned = swapped_halves(state), swapped_halves(adjoint)
                k = 2 * (kind * steps + n)
                packed[k, 2 * j] = jnp.where(low, state, adjoint_turned)
                packed[k, 2 * j + 1] = jnp.where(low, state_turned, adjoint)
                packed[k + 1, 2 * j] = jnp.where(low, adjoint, state_turned)
                packed[k + 1, 2 * j + 1] = jnp.where(low, adjoint_turned, state)

    def weights(power):
        return [
            jnp.broadcast_to(weights_ref[pl.ds(power * 2 * inputs + k, 1), :], (depth, LANES)) for k in range(2 * inputs)
        ]

    def injected(factors, i):
        return tree_sum([factor * packed[k, i] for k, factor in enumerate(factors)])

    def advance(source, target, power, reach):
        aways = list(range(-reach, reach + 1))
        masks = [inside(away) for away in aways]
        factors = weights(power)

        def loaded(i):
            if i >= rows:
                return [zero for _ in aways]
            return [source[i, pl.ds((middle + away) * depth, depth), :] for away in aways]

        before = [zero for _ in aways]
        now = loaded(0)
        for i in range(rows):
            later = loaded(i + 1)
            for k, away in enumerate(aways):
                start = (middle + away) * depth
                above = source[i, pl.ds(shift + (start - 1), depth), :]
                below = source[i, pl.ds(shift + (start + 1), depth), :]
                value = (before[k] + later[k]) + beside(now[k], lane) + (above + below)
                if away:
                    value = value * masks[k]
                else:
                    value = value + injected(factors, i)
                target[i, pl.ds(start, depth), :] = value
            before, now = now, later

    weighing.wait()
    factors = weights(powers - 1)
    for i in range(rows):
        even[i, pl.ds(middle * depth, depth), :] = injected(factors, i)
    buffers = (even, odd)
    done = 0
    while done < powers - 1:
        reach = min(done // depth + 1, slabs - 1)
        count = powers - 1 - done if reach == slabs - 1 else min(depth, powers - 1 - done)

        def twice(index, _):
            power = powers - 2 - done - 2 * index
            advance(buffers[0], buffers[1], power, reach)
            advance(buffers[1], buffers[0], power - 1, reach)
            return 0

        lax.fori_loop(0, count // 2, twice, 0)
        done += count
        if count % 2:
            advance(buffers[0], buffers[1], powers - 1 - done, reach)
            buffers = buffers[::-1]

    final = buffers[0]
    bit = lax.rem(slab, 2)
    for half in range(slabs // 2):
        for ref, flag in ((keep_ref, bit), (send_ref, 1 - bit)):
            away = 2 * half + flag - slab
            planes = pl.ds(pl.multiple_of((middle + away) * depth, depth), depth)
            for j in range(columns):
                first, second = final[2 * j, planes, :], final[2 * j + 1, planes, :]
                for f, value in (
                    (0, jnp.where(low, first, swapped_halves(second))),
                    (1, jnp.where(low, swapped_halves(first), second)),
                ):
                    ref[half, f, j] = value


def vmem_call(kernel, out_shapes, smem_inputs, inputs, scratch=(), spaces=None, limit=6, cost=2**20):
    smem = pl.BlockSpec(memory_space=pltpu.SMEM)
    vmem = pl.BlockSpec(memory_space=pltpu.VMEM)
    out_shape = tuple(jax.ShapeDtypeStruct(shape, jnp.float32) for shape in out_shapes)
    return pl.pallas_call(
        kernel,
        out_shape=out_shape,
        in_specs=[smem] * len(smem_inputs) + [pl.BlockSpec(memory_space=space) for space in spaces or [pltpu.VMEM] * len(inputs)],
        out_specs=(vmem,) * len(out_shape),
        scratch_shapes=list(scratch),
        compiler_params=pltpu.CompilerParams(vmem_limit_bytes=limit * 2**20),
        cost_estimate=pl.CostEstimate(flops=10**6, bytes_accessed=cost, transcendentals=0),
    )(*smem_inputs, *inputs)


def coarse_part(place, iterate, forcing):
    steps = iterate.shape[1]
    depth, cells = iterate.shape[2:]
    ranks, slabs = lax.axis_size("tm"), 2 * lax.axis_size("pair")
    table = coarse_polynomials(steps * ranks)
    powers = table.shape[-1]
    table = table.reshape(2, 2, ranks, steps, 2, powers)
    same = np.stack([table[:, 0, :, :, 0], table[:, 1, :, :, 1]], -1)
    other = np.stack([table[:, 1, :, :, 0], table[:, 0, :, :, 1]], -1)
    weights = np.stack([same, other], -2).transpose(1, 3, 0, 2, 4, 5).astype(np.float32)
    reach = min(-(-(powers - 1) // depth), slabs - 1)
    middle = max(reach + 1, slabs - 1)
    weights = np.repeat(weights.reshape(ranks, -1, 2), NY, -1)
    half = (slabs // 2, 2, cells // LANES, depth, LANES)
    buffer = pltpu.VMEM((cells // NY, (2 * middle + 1) * depth, LANES), jnp.float32)
    packed = pltpu.VMEM((4 * steps, cells // NY, depth, LANES), jnp.float32)
    return vmem_call(
        functools.partial(coarse_kernel, powers, steps, slabs, middle),
        (half, half),
        (place,),
        [pltpu.with_memory_space_constraint(array, pltpu.HBM) for array in (jnp.asarray(weights), iterate, forcing)],
        (
            buffer,
            buffer,
            packed,
            pltpu.VMEM(iterate.shape, jnp.float32),
            pltpu.VMEM(forcing.shape, jnp.float32),
            pltpu.VMEM(weights.shape[1:], jnp.float32),
            pltpu.SemaphoreType.DMA((2, 2, steps)),
            pltpu.SemaphoreType.DMA,
        ),
        spaces=(pltpu.HBM,) * 3,
        limit=12,
        cost=24 * 2**20,
    )


def relaxed(fields, around, before, after, source):
    diffusion, coupling, centre, along, across = level_terms(0)
    state, adjoint = fields
    defect_state = source[0] - (centre * state - diffusion * around[0] - before + coupling * adjoint)
    defect_adjoint = source[1] - (centre * adjoint - diffusion * around[1] - after - coupling * state)
    return (
        state + along * defect_state - across * defect_adjoint,
        adjoint + across * defect_state + along * defect_adjoint,
    )


def first_kernel(iterate_ref, forcing_ref, first_ref, up_ref, down_ref):
    steps, depth, cells = iterate_ref.shape[1:]
    columns = cells // LANES
    lane, sublane = lane_index(depth), sublane_index(depth)
    low = lane < NY
    zero = jnp.zeros((depth, LANES), jnp.float32)
    slots = [(f, n) for f in range(2) for n in range(steps)]

    def loaded(j):
        return {s: iterate_ref[s[0], s[1], :, column(j)] if j < columns else zero for s in slots}

    now = loaded(0)
    pairs_before = now
    for j in range(columns):
        later = loaded(j + 1)
        pairs = {s: now[s] + later[s] for s in slots}
        around = {}
        for s in slots:
            across_rows = swapped_halves(jnp.where(low, pairs[s], pairs_before[s]))
            above = jnp.where(sublane == 0, 0.0, pltpu.roll(now[s], 1, 0))
            below = jnp.where(sublane == depth - 1, 0.0, pltpu.roll(now[s], depth - 1, 0))
            around[s] = across_rows + beside(now[s], lane) + (above + below)
        for n in range(steps):
            values = relaxed(
                (now[0, n], now[1, n]),
                (around[0, n], around[1, n]),
                now[0, n - 1] if n else zero,
                now[1, n + 1] if n < steps - 1 else zero,
                (forcing_ref[0, n, :, column(j)], forcing_ref[1, n, :, column(j)]),
            )
            for f in range(2):
                first_ref[f, n, :, column(j)] = values[f]
                slot = f * steps + n
                for ref, plane in ((up_ref, depth - 1), (down_ref, 0)):
                    ref[slot : slot + 1, column(j)] = now[f, n][plane : plane + 1]
                    slot_after = 2 * steps + slot
                    ref[slot_after : slot_after + 1, column(j)] = values[f][plane : plane + 1]
        now, pairs_before = later, pairs


def second_kernel(
    steps, slabs, place_ref, iterate_ref, first_ref, up_ref, down_ref, above_ref, below_ref, swept_ref, edge_ref, forth_ref, back_ref
):
    diffusion, _, _, along, across = level_terms(0)
    depth, cells = iterate_ref.shape[2:]
    columns = cells // LANES
    slab = place_ref[1]
    sublane = sublane_index(depth)
    count = 2 * steps
    has_above = jnp.where(slab > 0, 1.0, 0.0).astype(jnp.float32)
    has_below = jnp.where(slab < slabs - 1, 1.0, 0.0).astype(jnp.float32)

    def mixed(rows):
        state, adjoint = rows[:steps], rows[steps:]
        return jnp.concatenate(
            [
                (along * diffusion) * state - (across * diffusion) * adjoint,
                (across * diffusion) * state + (along * diffusion) * adjoint,
            ],
            0,
        )

    def one(j):
        return slice(j * LANES, (j + 1) * LANES)

    for j in range(columns):
        from_above, from_below = above_ref[:, one(j)], below_ref[:, one(j)]
        edge_ref[:count, one(j)] = (from_above[count:] + mixed(down_ref[:count, one(j)])) * has_above
        edge_ref[count:, one(j)] = (from_below[count:] + mixed(up_ref[:count, one(j)])) * has_below
        add_above, add_below = mixed(from_above[:count]), mixed(from_below[:count])
        for f in range(2):
            for n in range(steps):
                k = f * steps + n
                value = first_ref[f, n, :, one(j)]
                value = value + jnp.where(sublane == 0, add_above[k : k + 1], 0.0)
                value = value + jnp.where(sublane == depth - 1, add_below[k : k + 1], 0.0)
                swept_ref[f, n, :, one(j)] = value
                for ref, field, step in ((forth_ref, 0, steps - 1), (back_ref, 1, 0)):
                    if (f, n) == (field, step):
                        ref[j] = value
                        block, row = columns + j // depth, j % depth
                        ref[block, row : row + 1] = from_above[k : k + 1]
                        block += columns // depth
                        ref[block, row : row + 1] = from_below[k : k + 1]


def third_kernel(steps, ranks, place_ref, iterate_ref, forcing_ref, swept_ref, edge_ref, last_ref, next_ref, forth_ref, back_ref, out_ref):
    _, _, _, along, across = level_terms(0)
    depth, cells = iterate_ref.shape[2:]
    columns = cells // LANES
    rank = place_ref[0]
    lane, sublane = lane_index(depth), sublane_index(depth)
    low = lane < NY
    zero = jnp.zeros((depth, LANES), jnp.float32)
    slots = [(f, n) for f in range(2) for n in range(steps)]
    has_before = jnp.where(rank > 0, 1.0, 0.0).astype(jnp.float32)
    has_after = jnp.where(rank < ranks - 1, 1.0, 0.0).astype(jnp.float32)
    gain = {(0, 0): ("forth", along), (1, 0): ("forth", across), (0, steps - 1): ("back", -across), (1, steps - 1): ("back", along)}

    def loaded(j):
        if j >= columns:
            return {s: zero for s in slots}
        near = {"forth": last_ref[:, column(j)], "back": next_ref[:, column(j)]}
        values = {}
        for s in slots:
            values[s] = swept_ref[s[0], s[1], :, column(j)]
            if s in gain:
                values[s] = values[s] + gain[s][1] * near[gain[s][0]]
        return values

    def edges(j, side):
        block, row = columns + side * (columns // depth) + j // depth, j % depth
        near = {"forth": forth_ref[block, row : row + 1], "back": back_ref[block, row : row + 1]}
        values = {}
        for s in slots:
            k = side * 2 * steps + s[0] * steps + s[1]
            values[s] = edge_ref[k : k + 1, column(j)]
            if s in gain:
                values[s] = values[s] + gain[s][1] * near[gain[s][0]]
        return values

    now = loaded(0)
    pairs_before = now
    for j in range(columns):
        later = loaded(j + 1)
        over, under = edges(j, 0), edges(j, 1)
        pairs = {s: now[s] + later[s] for s in slots}
        around = {}
        for s in slots:
            across_rows = swapped_halves(jnp.where(low, pairs[s], pairs_before[s]))
            above = jnp.where(sublane == 0, over[s], pltpu.roll(now[s], 1, 0))
            below = jnp.where(sublane == depth - 1, under[s], pltpu.roll(now[s], depth - 1, 0))
            around[s] = across_rows + beside(now[s], lane) + (above + below)
        before = (forth_ref[j] - across * iterate_ref[1, 0, :, column(j)]) * has_before
        after = (back_ref[j] + across * iterate_ref[0, steps - 1, :, column(j)]) * has_after
        for n in range(steps):
            values = relaxed(
                (now[0, n], now[1, n]),
                (around[0, n], around[1, n]),
                now[0, n - 1] if n else before,
                now[1, n + 1] if n < steps - 1 else after,
                (forcing_ref[0, n, :, column(j)], forcing_ref[1, n, :, column(j)]),
            )
            for f in range(2):
                out_ref[f, n, :, column(j)] = values[f]
        now, pairs_before = later, pairs


def swapped(value, axis, mask):
    return lax.ppermute(value, axis, [(i, i ^ mask) for i in range(lax.axis_size(axis))])


def shifted(value, axis, by):
    size = lax.axis_size(axis)
    return lax.ppermute(value, axis, [(i, i + by) for i in range(size) if 0 <= i + by < size])


def add_kernel(place_ref, keep_ref, received_any, other_ref, own_ref, received_ref, arrived):
    pair = lax.div(place_ref[1], 2)
    parts = [(index, f) for index in (1 - pair, pair) for f in range(2)]
    copies = [
        pltpu.make_async_copy(received_any.at[index, f], received_ref.at[k], arrived.at[k])
        for k, (index, f) in enumerate(parts)
    ]
    for copy in copies:
        copy.start()
    for k, (index, f) in enumerate(parts):
        copies[k].wait()
        (other_ref, own_ref)[k // 2][f] = keep_ref[index, f] + received_ref[k]


def last_kernel(place_ref, mine_ref, given_ref, out_ref):
    steps = out_ref.shape[1]
    field = lax.rem(place_ref[0], 2)
    for j in range(mine_ref.shape[0]):
        for n in range(steps):
            out_ref[field, n, :, column(j)] = mine_ref[j]
            out_ref[1 - field, n, :, column(j)] = given_ref[j]


def local(iterate, forcing):
    steps, depth, cells = iterate.shape[1:]
    columns = cells // LANES
    ranks, slabs = lax.axis_size("tm"), 2 * lax.axis_size("pair")
    place = jnp.stack([lax.axis_index("tm"), lax.axis_index(("pair", "core")), jnp.zeros((), jnp.int32)]).astype(jnp.int32)
    keep, send = coarse_part(place, iterate, forcing)
    received = lax.ppermute(send, "core", [(0, 1), (1, 0)])

    keep, iterate_after, forcing_after = lax.optimization_barrier((keep, iterate, forcing))
    first, up, down = vmem_call(
        first_kernel, (iterate.shape, (4 * steps, cells), (4 * steps, cells)), (), (iterate_after, forcing_after)
    )
    other, own = vmem_call(
        add_kernel,
        (keep.shape[1:], keep.shape[1:]),
        (place,),
        (keep, received),
        (pltpu.VMEM((4,) + keep.shape[2:], jnp.float32), pltpu.SemaphoreType.DMA((4,))),
        spaces=(pltpu.VMEM, pl.ANY),
    )
    other, up, down = lax.optimization_barrier((other, up, down))
    above = shifted(up, ("pair", "core"), 1)
    below = shifted(down, ("pair", "core"), -1)
    term = swapped(other, "pair", 1)
    field = lax.rem(lax.axis_index("tm"), 2)

    def chosen(array, index):
        return lax.dynamic_index_in_dim(array, index, 0, keepdims=False)

    half = chosen(own, 1 - field) + chosen(term, 1 - field)
    last = shifted(iterate_after[0, -1], "tm", 1)
    following = shifted(iterate_after[1, 0], "tm", -1)
    half, above, below, last, following = lax.optimization_barrier((half, above, below, last, following))
    mine = chosen(own, field) + chosen(term, field) + swapped(half, "tm", 1)
    payload = (columns + 2 * columns // depth, depth, LANES)
    swept, edge, forth, back = vmem_call(
        functools.partial(second_kernel, steps, slabs),
        (iterate.shape, (4 * steps, cells), payload, payload),
        (place,),
        (iterate, first, up, down, above, below),
    )
    mine, _, _ = lax.optimization_barrier((mine, forth, back))
    mask = 2
    while mask < ranks:
        mine = mine + swapped(mine, "tm", mask)
        mask *= 2
    forth = shifted(forth, "tm", 1)
    back = shifted(back, "tm", -1)
    mine, forth, back = lax.optimization_barrier((mine, forth, back))
    given = swapped(mine, "tm", 1)
    (coarse,) = vmem_call(last_kernel, (iterate.shape,), (place,), (mine, given))
    (smoothed,) = vmem_call(
        functools.partial(third_kernel, steps, ranks),
        (iterate.shape,),
        (place,),
        (iterate, forcing, swept, edge, last, following, forth, back),
        cost=64 * 2**20,
    )
    return smoothed, coarse


def solution(mesh):
    ranks, slabs = mesh.shape["tm"], mesh.shape["space"]
    fine = jax.sharding.Mesh(mesh.devices.reshape(ranks, slabs // 2, 2), ("tm", "pair", "core"))
    specs = P(None, "tm", ("pair", "core"), None)
    return jax.shard_map(local, mesh=fine, in_specs=(specs, specs), out_specs=(specs, specs), check_vma=False)
```

```python
import functools

import numpy as np

import jax
import jax.numpy as jnp
from jax import lax
from jax.experimental import pallas as pl
from jax.experimental.pallas import tpu as pltpu
from jax.sharding import PartitionSpec as P

NY = 64
LANES = 128

KAPPA_BASE = 0.25
COUPLING_BASE = 0.5
DAMPING = 0.6


def level_terms(level):
    diffusion = KAPPA_BASE * 2.0**level
    coupling = COUPLING_BASE * 2.0**level
    centre = 1.0 + 6.0 * diffusion
    determinant = centre * centre + coupling * coupling
    along = DAMPING * centre / determinant
    across = DAMPING * coupling / determinant
    return diffusion, coupling, centre, along, across


def coarse_polynomials(total_steps):
    levels = total_steps.bit_length()
    powers = 2 * levels + 1
    unit = np.eye(4 * total_steps).reshape(-1, 2, 2, total_steps)
    fields = np.zeros((4 * total_steps, 2, total_steps, powers))
    source = np.zeros_like(fields)
    fields[..., 0] = unit[:, 0]
    source[..., 0] = unit[:, 1]

    def image(values, diffusion, coupling, centre):
        out = centre * values
        out[..., 1:] -= diffusion * values[..., :-1]
        out[:, 0, 1:] -= values[:, 0, :-1]
        out[:, 1, :-1] -= values[:, 1, 1:]
        out[:, 0] += coupling * values[:, 1]
        out[:, 1] -= coupling * values[:, 0]
        return out

    for level in range(levels):
        diffusion, coupling, centre, along, across = level_terms(level)
        for _ in range(2):
            defect = source - image(fields, diffusion, coupling, centre)
            state, adjoint = defect[:, 0], defect[:, 1]
            fields = fields + np.stack([along * state - across * adjoint, across * state + along * adjoint], 1)
        if level < levels - 1:
            defect = source - image(fields, diffusion, coupling, centre)
            source = defect[:, :, 0::2] + defect[:, :, 1::2]
            fields = np.zeros_like(source)
    return fields[:, :, 0].reshape(2, 2, total_steps, 2, powers)


def lane_index(depth):
    return lax.broadcasted_iota(jnp.int32, (depth, LANES), 1)


def sublane_index(depth):
    return lax.broadcasted_iota(jnp.int32, (depth, LANES), 0)


def column(j):
    return pl.ds(j * LANES, LANES)


def swapped_halves(value):
    return pltpu.roll(value, NY, 1)


def beside(value, lane):
    left = pltpu.roll(jnp.where((lane % NY) != NY - 1, value, 0.0), 1, 1)
    right = pltpu.roll(jnp.where((lane % NY) != 0, value, 0.0), LANES - 1, 1)
    return left + right


def tree_sum(terms):
    while len(terms) > 1:
        terms = [sum(terms[k : k + 2]) for k in range(0, len(terms), 2)]
    return terms[0]


def coarse_kernel(
    powers, steps, slabs, middle, place_ref, weights_hbm, iterate_hbm, forcing_hbm, keep_ref, send_ref, even, odd, packed, iterate_ref, forcing_ref, weights_ref, arrived, weighed
):
    copies = {
        (kind, f, n): pltpu.make_async_copy(source.at[f, n], target.at[f, n], arrived.at[kind, f, n])
        for kind, (source, target) in enumerate(((iterate_hbm, iterate_ref), (forcing_hbm, forcing_ref)))
        for n in range(steps)
        for f in range(2)
    }
    weighing = pltpu.make_async_copy(weights_hbm.at[place_ref[0]], weights_ref, weighed)
    for copy in copies.values():
        copy.start()
    weighing.start()
    even[...] = jnp.zeros_like(even)
    odd[...] = jnp.zeros_like(odd)
    depth, cells = iterate_ref.shape[2:]
    columns = cells // LANES
    rows = cells // NY
    inputs = 2 * steps
    slab, shift = place_ref[1], place_ref[2]
    lane = lane_index(depth)
    low = lane < NY
    zero = jnp.zeros((depth, LANES), jnp.float32)

    def inside(away):
        at = slab + away
        return jnp.where((at >= 0) & (at < slabs), 1.0, 0.0).astype(jnp.float32)

    for kind, ref in enumerate((iterate_ref, forcing_ref)):
        for n in range(steps):
            copies[kind, 0, n].wait()
            copies[kind, 1, n].wait()
            for j in range(columns):
                state, adjoint = ref[0, n, :, column(j)], ref[1, n, :, column(j)]
                state_turned, adjoint_turned = swapped_halves(state), swapped_halves(adjoint)
                k = 2 * (kind * steps + n)
                packed[k, 2 * j] = jnp.where(low, state, adjoint_turned)
                packed[k, 2 * j + 1] = jnp.where(low, state_turned, adjoint)
                packed[k + 1, 2 * j] = jnp.where(low, adjoint, state_turned)
                packed[k + 1, 2 * j + 1] = jnp.where(low, adjoint_turned, state)

    def weights(power):
        return [
            jnp.broadcast_to(weights_ref[pl.ds(power * 2 * inputs + k, 1), :], (depth, LANES)) for k in range(2 * inputs)
        ]

    def injected(factors, i):
        return tree_sum([factor * packed[k, i] for k, factor in enumerate(factors)])

    def advance(source, target, power, reach):
        aways = list(range(-reach, reach + 1))
        masks = [inside(away) for away in aways]
        factors = weights(power)

        def loaded(i):
            if i >= rows:
                return [zero for _ in aways]
            return [source[i, pl.ds((middle + away) * depth, depth), :] for away in aways]

        before = [zero for _ in aways]
        now = loaded(0)
        for i in range(rows):
            later = loaded(i + 1)
            for k, away in enumerate(aways):
                start = (middle + away) * depth
                above = source[i, pl.ds(shift + (start - 1), depth), :]
                below = source[i, pl.ds(shift + (start + 1), depth), :]
                value = (before[k] + later[k]) + beside(now[k], lane) + (above + below)
                if away:
                    value = value * masks[k]
                else:
                    value = value + injected(factors, i)
                target[i, pl.ds(start, depth), :] = value
            before, now = now, later

    weighing.wait()
    factors = weights(powers - 1)
    for i in range(rows):
        even[i, pl.ds(middle * depth, depth), :] = injected(factors, i)
    buffers = (even, odd)
    done = 0
    while done < powers - 1:
        reach = min(done // depth + 1, slabs - 1)
        count = powers - 1 - done if reach == slabs - 1 else min(depth, powers - 1 - done)

        def twice(index, _):
            power = powers - 2 - done - 2 * index
            advance(buffers[0], buffers[1], power, reach)
            advance(buffers[1], buffers[0], power - 1, reach)
            return 0

        lax.fori_loop(0, count // 2, twice, 0)
        done += count
        if count % 2:
            advance(buffers[0], buffers[1], powers - 1 - done, reach)
            buffers = buffers[::-1]

    final = buffers[0]
    bit = lax.rem(slab, 2)
    for half in range(slabs // 2):
        for ref, flag in ((keep_ref, bit), (send_ref, 1 - bit)):
            away = 2 * half + flag - slab
            planes = pl.ds(pl.multiple_of((middle + away) * depth, depth), depth)
            for j in range(columns):
                first, second = final[2 * j, planes, :], final[2 * j + 1, planes, :]
                for f, value in (
                    (0, jnp.where(low, first, swapped_halves(second))),
                    (1, jnp.where(low, swapped_halves(first), second)),
                ):
                    ref[half, f, j] = value


def vmem_call(kernel, out_shapes, smem_inputs, inputs, scratch=(), spaces=None, limit=6, cost=2**20):
    smem = pl.BlockSpec(memory_space=pltpu.SMEM)
    vmem = pl.BlockSpec(memory_space=pltpu.VMEM)
    out_shape = tuple(jax.ShapeDtypeStruct(shape, jnp.float32) for shape in out_shapes)
    return pl.pallas_call(
        kernel,
        out_shape=out_shape,
        in_specs=[smem] * len(smem_inputs) + [pl.BlockSpec(memory_space=space) for space in spaces or [pltpu.VMEM] * len(inputs)],
        out_specs=(vmem,) * len(out_shape),
        scratch_shapes=list(scratch),
        compiler_params=pltpu.CompilerParams(vmem_limit_bytes=limit * 2**20),
        cost_estimate=pl.CostEstimate(flops=10**6, bytes_accessed=cost, transcendentals=0),
    )(*smem_inputs, *inputs)


def coarse_part(place, iterate, forcing):
    steps = iterate.shape[1]
    depth, cells = iterate.shape[2:]
    ranks, slabs = lax.axis_size("tm"), 2 * lax.axis_size("pair")
    table = coarse_polynomials(steps * ranks)
    powers = table.shape[-1]
    table = table.reshape(2, 2, ranks, steps, 2, powers)
    same = np.stack([table[:, 0, :, :, 0], table[:, 1, :, :, 1]], -1)
    other = np.stack([table[:, 1, :, :, 0], table[:, 0, :, :, 1]], -1)
    weights = np.stack([same, other], -2).transpose(1, 3, 0, 2, 4, 5).astype(np.float32)
    reach = min(-(-(powers - 1) // depth), slabs - 1)
    middle = max(reach + 1, slabs - 1)
    weights = np.repeat(weights.reshape(ranks, -1, 2), NY, -1)
    half = (slabs // 2, 2, cells // LANES, depth, LANES)
    buffer = pltpu.VMEM((cells // NY, (2 * middle + 1) * depth, LANES), jnp.float32)
    packed = pltpu.VMEM((4 * steps, cells // NY, depth, LANES), jnp.float32)
    return vmem_call(
        functools.partial(coarse_kernel, powers, steps, slabs, middle),
        (half, half),
        (place,),
        [pltpu.with_memory_space_constraint(array, pltpu.HBM) for array in (jnp.asarray(weights), iterate, forcing)],
        (
            buffer,
            buffer,
            packed,
            pltpu.VMEM(iterate.shape, jnp.float32),
            pltpu.VMEM(forcing.shape, jnp.float32),
            pltpu.VMEM(weights.shape[1:], jnp.float32),
            pltpu.SemaphoreType.DMA((2, 2, steps)),
            pltpu.SemaphoreType.DMA,
        ),
        spaces=(pltpu.HBM,) * 3,
        limit=12,
        cost=24 * 2**20,
    )


def relaxed(fields, around, before, after, source):
    diffusion, coupling, centre, along, across = level_terms(0)
    state, adjoint = fields
    defect_state = source[0] - (centre * state - diffusion * around[0] - before + coupling * adjoint)
    defect_adjoint = source[1] - (centre * adjoint - diffusion * around[1] - after - coupling * state)
    return (
        state + along * defect_state - across * defect_adjoint,
        adjoint + across * defect_state + along * defect_adjoint,
    )


def first_kernel(iterate_ref, forcing_ref, first_ref, up_ref, down_ref):
    steps, depth, cells = iterate_ref.shape[1:]
    columns = cells // LANES
    lane, sublane = lane_index(depth), sublane_index(depth)
    low = lane < NY
    zero = jnp.zeros((depth, LANES), jnp.float32)
    slots = [(f, n) for f in range(2) for n in range(steps)]

    def loaded(j):
        return {s: iterate_ref[s[0], s[1], :, column(j)] if j < columns else zero for s in slots}

    now = loaded(0)
    pairs_before = now
    for j in range(columns):
        later = loaded(j + 1)
        pairs = {s: now[s] + later[s] for s in slots}
        around = {}
        for s in slots:
            across_rows = swapped_halves(jnp.where(low, pairs[s], pairs_before[s]))
            above = jnp.where(sublane == 0, 0.0, pltpu.roll(now[s], 1, 0))
            below = jnp.where(sublane == depth - 1, 0.0, pltpu.roll(now[s], depth - 1, 0))
            around[s] = across_rows + beside(now[s], lane) + (above + below)
        for n in range(steps):
            values = relaxed(
                (now[0, n], now[1, n]),
                (around[0, n], around[1, n]),
                now[0, n - 1] if n else zero,
                now[1, n + 1] if n < steps - 1 else zero,
                (forcing_ref[0, n, :, column(j)], forcing_ref[1, n, :, column(j)]),
            )
            for f in range(2):
                first_ref[f, n, :, column(j)] = values[f]
                slot = f * steps + n
                for ref, plane in ((up_ref, depth - 1), (down_ref, 0)):
                    ref[slot : slot + 1, column(j)] = now[f, n][plane : plane + 1]
                    slot_after = 2 * steps + slot
                    ref[slot_after : slot_after + 1, column(j)] = values[f][plane : plane + 1]
        now, pairs_before = later, pairs


def second_kernel(
    steps, slabs, place_ref, iterate_ref, first_ref, up_ref, down_ref, above_ref, below_ref, swept_ref, edge_ref, forth_ref, back_ref
):
    diffusion, _, _, along, across = level_terms(0)
    depth, cells = iterate_ref.shape[2:]
    columns = cells // LANES
    slab = place_ref[1]
    sublane = sublane_index(depth)
    count = 2 * steps
    has_above = jnp.where(slab > 0, 1.0, 0.0).astype(jnp.float32)
    has_below = jnp.where(slab < slabs - 1, 1.0, 0.0).astype(jnp.float32)

    def mixed(rows):
        state, adjoint = rows[:steps], rows[steps:]
        return jnp.concatenate(
            [
                (along * diffusion) * state - (across * diffusion) * adjoint,
                (across * diffusion) * state + (along * diffusion) * adjoint,
            ],
            0,
        )

    def one(j):
        return slice(j * LANES, (j + 1) * LANES)

    for j in range(columns):
        from_above, from_below = above_ref[:, one(j)], below_ref[:, one(j)]
        edge_ref[:count, one(j)] = (from_above[count:] + mixed(down_ref[:count, one(j)])) * has_above
        edge_ref[count:, one(j)] = (from_below[count:] + mixed(up_ref[:count, one(j)])) * has_below
        add_above, add_below = mixed(from_above[:count]), mixed(from_below[:count])
        for f in range(2):
            for n in range(steps):
                k = f * steps + n
                value = first_ref[f, n, :, one(j)]
                value = value + jnp.where(sublane == 0, add_above[k : k + 1], 0.0)
                value = value + jnp.where(sublane == depth - 1, add_below[k : k + 1], 0.0)
                swept_ref[f, n, :, one(j)] = value
                for ref, field, step in ((forth_ref, 0, steps - 1), (back_ref, 1, 0)):
                    if (f, n) == (field, step):
                        ref[j] = value
                        block, row = columns + j // depth, j % depth
                        ref[block, row : row + 1] = from_above[k : k + 1]
                        block += columns // depth
                        ref[block, row : row + 1] = from_below[k : k + 1]


def third_kernel(steps, ranks, place_ref, iterate_ref, forcing_ref, swept_ref, edge_ref, last_ref, next_ref, forth_ref, back_ref, out_ref):
    _, _, _, along, across = level_terms(0)
    depth, cells = iterate_ref.shape[2:]
    columns = cells // LANES
    rank = place_ref[0]
    lane, sublane = lane_index(depth), sublane_index(depth)
    low = lane < NY
    zero = jnp.zeros((depth, LANES), jnp.float32)
    slots = [(f, n) for f in range(2) for n in range(steps)]
    has_before = jnp.where(rank > 0, 1.0, 0.0).astype(jnp.float32)
    has_after = jnp.where(rank < ranks - 1, 1.0, 0.0).astype(jnp.float32)
    gain = {(0, 0): ("forth", along), (1, 0): ("forth", across), (0, steps - 1): ("back", -across), (1, steps - 1): ("back", along)}

    def loaded(j):
        if j >= columns:
            return {s: zero for s in slots}
        near = {"forth": last_ref[:, column(j)], "back": next_ref[:, column(j)]}
        values = {}
        for s in slots:
            values[s] = swept_ref[s[0], s[1], :, column(j)]
            if s in gain:
                values[s] = values[s] + gain[s][1] * near[gain[s][0]]
        return values

    def edges(j, side):
        block, row = columns + side * (columns // depth) + j // depth, j % depth
        near = {"forth": forth_ref[block, row : row + 1], "back": back_ref[block, row : row + 1]}
        values = {}
        for s in slots:
            k = side * 2 * steps + s[0] * steps + s[1]
            values[s] = edge_ref[k : k + 1, column(j)]
            if s in gain:
                values[s] = values[s] + gain[s][1] * near[gain[s][0]]
        return values

    now = loaded(0)
    pairs_before = now
    for j in range(columns):
        later = loaded(j + 1)
        over, under = edges(j, 0), edges(j, 1)
        pairs = {s: now[s] + later[s] for s in slots}
        around = {}
        for s in slots:
            across_rows = swapped_halves(jnp.where(low, pairs[s], pairs_before[s]))
            above = jnp.where(sublane == 0, over[s], pltpu.roll(now[s], 1, 0))
            below = jnp.where(sublane == depth - 1, under[s], pltpu.roll(now[s], depth - 1, 0))
            around[s] = across_rows + beside(now[s], lane) + (above + below)
        before = (forth_ref[j] - across * iterate_ref[1, 0, :, column(j)]) * has_before
        after = (back_ref[j] + across * iterate_ref[0, steps - 1, :, column(j)]) * has_after
        for n in range(steps):
            values = relaxed(
                (now[0, n], now[1, n]),
                (around[0, n], around[1, n]),
                now[0, n - 1] if n else before,
                now[1, n + 1] if n < steps - 1 else after,
                (forcing_ref[0, n, :, column(j)], forcing_ref[1, n, :, column(j)]),
            )
            for f in range(2):
                out_ref[f, n, :, column(j)] = values[f]
        now, pairs_before = later, pairs


def swapped(value, axis, mask):
    return lax.ppermute(value, axis, [(i, i ^ mask) for i in range(lax.axis_size(axis))])


def shifted(value, axis, by):
    size = lax.axis_size(axis)
    return lax.ppermute(value, axis, [(i, i + by) for i in range(size) if 0 <= i + by < size])


def add_kernel(place_ref, keep_ref, received_any, other_ref, own_ref, received_ref, arrived):
    pair = lax.div(place_ref[1], 2)
    parts = [(index, f) for index in (1 - pair, pair) for f in range(2)]
    copies = [
        pltpu.make_async_copy(received_any.at[index, f], received_ref.at[k], arrived.at[k])
        for k, (index, f) in enumerate(parts)
    ]
    for copy in copies:
        copy.start()
    for k, (index, f) in enumerate(parts):
        copies[k].wait()
        (other_ref, own_ref)[k // 2][f] = keep_ref[index, f] + received_ref[k]


def last_kernel(place_ref, mine_ref, given_ref, out_ref):
    steps = out_ref.shape[1]
    field = lax.rem(place_ref[0], 2)
    for j in range(mine_ref.shape[0]):
        for n in range(steps):
            out_ref[field, n, :, column(j)] = mine_ref[j]
            out_ref[1 - field, n, :, column(j)] = given_ref[j]


def local(iterate, forcing):
    steps, depth, cells = iterate.shape[1:]
    columns = cells // LANES
    ranks, slabs = lax.axis_size("tm"), 2 * lax.axis_size("pair")
    place = jnp.stack([lax.axis_index("tm"), lax.axis_index(("pair", "core")), jnp.zeros((), jnp.int32)]).astype(jnp.int32)
    keep, send = coarse_part(place, iterate, forcing)
    received = lax.ppermute(send, "core", [(0, 1), (1, 0)])

    keep, iterate_after, forcing_after = lax.optimization_barrier((keep, iterate, forcing))
    first, up, down = vmem_call(
        first_kernel, (iterate.shape, (4 * steps, cells), (4 * steps, cells)), (), (iterate_after, forcing_after)
    )
    other, own = vmem_call(
        add_kernel,
        (keep.shape[1:], keep.shape[1:]),
        (place,),
        (keep, received),
        (pltpu.VMEM((4,) + keep.shape[2:], jnp.float32), pltpu.SemaphoreType.DMA((4,))),
        spaces=(pltpu.VMEM, pl.ANY),
    )
    other, up, down = lax.optimization_barrier((other, up, down))
    above = shifted(up, ("pair", "core"), 1)
    below = shifted(down, ("pair", "core"), -1)
    term = swapped(other, "pair", 1)
    field = lax.rem(lax.axis_index("tm"), 2)

    def chosen(array, index):
        return lax.dynamic_index_in_dim(array, index, 0, keepdims=False)

    half = chosen(own, 1 - field) + chosen(term, 1 - field)
    last = shifted(iterate_after[0, -1], "tm", 1)
    following = shifted(iterate_after[1, 0], "tm", -1)
    half, above, below, last, following = lax.optimization_barrier((half, above, below, last, following))
    mine = chosen(own, field) + chosen(term, field) + swapped(half, "tm", 1)
    payload = (columns + 2 * columns // depth, depth, LANES)
    swept, edge, forth, back = vmem_call(
        functools.partial(second_kernel, steps, slabs),
        (iterate.shape, (4 * steps, cells), payload, payload),
        (place,),
        (iterate, first, up, down, above, below),
    )
    mine, _, _ = lax.optimization_barrier((mine, forth, back))
    mask = 2
    forth = shifted(forth, "tm", 1)
    back = shifted(back, "tm", -1)
    while mask < ranks:
        if 2 * mask == ranks:
            mine, forth, back = lax.optimization_barrier((mine, forth, back))
        mine = mine + swapped(mine, "tm", mask)
        mask *= 2
    given = swapped(mine, "tm", 1)
    (coarse,) = vmem_call(last_kernel, (iterate.shape,), (place,), (mine, given))
    (smoothed,) = vmem_call(
        functools.partial(third_kernel, steps, ranks),
        (iterate.shape,),
        (place,),
        (iterate, forcing, swept, edge, last, following, forth, back),
        cost=64 * 2**20,
    )
    return smoothed, coarse


def solution(mesh):
    ranks, slabs = mesh.shape["tm"], mesh.shape["space"]
    fine = jax.sharding.Mesh(mesh.devices.reshape(ranks, slabs // 2, 2), ("tm", "pair", "core"))
    specs = P(None, "tm", ("pair", "core"), None)
    return jax.shard_map(local, mesh=fine, in_specs=(specs, specs), out_specs=(specs, specs), check_vma=False)
```
